32 devices in a mesh: tower: 2 (over core), batch: 16 (over z, y, x).
Axes of the slice: x: 2, y: 2, z: 4, core: 2. Of those that a mesh axis runs over, the one named last changes fastest.
Arguments:
- tokens: bfloat16 [2, 32, 512, 768], P('tower', 'batch'), may hold values from -7 to 7
- lengths: int32 [2, 32], P('tower', 'batch'), may hold values from 128 to 512, as said below
- doc_groups: int32 [32], replicated, may hold values from 0 to 7, never falling along the last dimension, each value on 1 to 16 neighbouring positions
- positives: int32 [32], replicated, may hold values from 0 to 31, each once
- cotangent: bfloat16 [2, 32, 512, 768], P('tower', 'batch'), may hold values from -6 to 6
- w_query: bfloat16 [768, 768], replicated, may hold values from -0.0546875 to 0.0546875
- w_key: bfloat16 [768, 768], replicated, may hold values from -0.21875 to 0.21875
- w_value: bfloat16 [768, 768], replicated, may hold values from -0.21875 to 0.21875
- w_mixed: bfloat16 [768, 768], replicated, may hold values from -0.625 to 0.625
- w_inner: bfloat16 [768, 3072], replicated, may hold values from -0.21875 to 0.21875
- w_outer: bfloat16 [3072, 768], replicated, may hold values from -0.109375 to 0.109375
- gain_attn: float32 [768], replicated, may hold values from 0.25 to 1.75
- gain_ffn: float32 [768], replicated, may hold values from 0.25 to 1.75
- rel_table: float32 [32, 12], replicated, may hold values from -4 to 4
Outputs:
- activations: bfloat16 [2, 32, 512, 768], P('tower', 'batch')
- pooled: float32 [2, 32, 768], P('tower', 'batch')
- loss: float32 [], replicated
- tokens_grad: bfloat16 [2, 32, 512, 768], P('tower', 'batch')
- w_query_grad: float32 [768, 768], replicated
- w_key_grad: float32 [768, 768], replicated
- w_value_grad: float32 [768, 768], replicated
- w_mixed_grad: float32 [768, 768], replicated
- w_inner_grad: float32 [768, 3072], replicated
- w_outer_grad: float32 [3072, 768], replicated
- gain_attn_grad: float32 [768], replicated
- gain_ffn_grad: float32 [768], replicated
- rel_table_grad: float32 [32, 12], replicated
The draws below stay inside these ranges and needn't reach their ends.
Inputs may be any that keep to these rules, and one draw needn't show every extreme that they name: `doc_groups`: group numbers never fall along the rows; each group holds 1 to 16 documents. `positives`: each document row is named once. `lengths`: each tower has at least one row whose length is exactly 512.
All inputs are finite; a program needn't handle non-finite values.
Results may differ from the reference program's by a relative error of at most 0.014.
The reference program's roundings to bfloat16 on the way count: a program that leaves them out, or rounds other values in their place, can miss the bound.
Values sent between devices are 32-bit elements; how exact they have to be, the bound alone decides.
A program may use at most 320 MiB of HBM per device.

```python
import math
import jax
import jax.numpy as jnp
import numpy as np
from jax import lax

D = 768
HEADS = 12
HEAD_SIZE = 64
FF = 3072
BUCKETS = 32
SEQ = 512
GMOST = 16
ROWS = 32
GROUPS = 8


def draw_tokens(key, part):
    key = jax.random.fold_in(key, 11)
    noise_key, offset_key = jax.random.split(key)
    noise = jnp.clip(jax.random.normal(noise_key, (2, ROWS, SEQ, D), jnp.float32), -4.0, 4.0)
    offsets = 0.7 * jnp.clip(jax.random.normal(offset_key, (2, ROWS, 1, D), jnp.float32), -4.0, 4.0)
    return (noise + offsets).astype(jnp.bfloat16)


def draw_lengths(key, part):
    key = jax.random.fold_in(key, 23)
    value_key, place_key = jax.random.split(key)
    values = jax.random.randint(value_key, (2, ROWS), SEQ // 4, SEQ + 1, dtype=jnp.int32)
    places = jax.random.randint(place_key, (2, 1), 0, ROWS, dtype=jnp.int32)
    rows_index = jnp.arange(ROWS, dtype=jnp.int32)[None, :]
    return jnp.where(rows_index == places, SEQ, values).astype(jnp.int32)


def shard_levels(key, dims, cuts, least, top_value):
    loudness = 1.0
    for dim, blocks in cuts:
        steps = jax.random.uniform(jax.random.fold_in(jax.random.fold_in(key, 6), dim), (blocks,), jnp.float32, least / len(cuts), top_value / len(cuts))
        loudness = loudness * jnp.repeat(jnp.exp(steps), dims[dim] // blocks).reshape((-1,) + (1,) * (len(dims) - 1 - dim))
    return loudness


def split_up(count, total, bound, slope):
    weights = [(1 << 20) // math.isqrt(rank ** slope) + 1 for rank in range(2, count + 1)]
    surplus, holding = total - bound - (count - 1), [1] * (count - 1)
    while surplus > 0:
        free = [i for i in range(count - 1) if holding[i] < bound]
        pool, budget = sum([weights[i] for i in free]), surplus
        for i in free:
            extra = min(bound - holding[i], max(1, budget * weights[i] // pool), surplus)
            holding[i] = holding[i] + extra
            surplus = surplus - extra
    return np.array([bound] + holding)


def uneven_parts(rng, amount, total, reach, skew):
    if amount == 2:
        one = jax.random.randint(rng, (), max(1, total - reach), min(reach, total - 1) + 1)
        return jnp.stack([one, total - one])
    sizes = jnp.asarray(split_up(amount, total, reach, skew), jnp.int32)
    pairs = (amount - 1) // 2
    donor, receiver = sizes[1:1 + 2 * pairs:2], sizes[2:2 + 2 * pairs:2]
    room = jnp.minimum(donor - 1, reach - receiver)
    shifted = jax.random.randint(jax.random.fold_in(rng, 1), (pairs,), 0, 1 << 20) % (room + 1)
    sizes = sizes.at[1:1 + 2 * pairs:2].set(donor - shifted).at[2:2 + 2 * pairs:2].set(receiver + shifted)
    return sizes[jax.random.permutation(jax.random.fold_in(rng, 2), amount)]


def scatter_about(rng, dims, scale, most, cuts=(), kind=jnp.bfloat16):
    drawn = jax.random.normal(rng, dims, jnp.float32) * scale
    if len(cuts) > 0:
        drawn = shard_levels(rng, dims, cuts, -0.22, 0.18) * drawn
    return jnp.clip(drawn, min=-most, max=most).astype(kind)


def setup_inputs(seed: int = 0) -> dict:
    splits = jax.random.split(jax.random.key(seed), 15)
    tokens = draw_tokens(jax.random.fold_in(splits[14], 71), 0)
    lengths = draw_lengths(jax.random.fold_in(splits[14], 71), 0)
    doc_groups = jnp.searchsorted(jnp.cumsum(uneven_parts(splits[2], GROUPS, ROWS, GMOST, 2)), jnp.arange(ROWS), side="right").astype(jnp.int32)
    positives = jax.random.permutation(splits[3], ROWS).astype(jnp.int32)
    cotangent = scatter_about(splits[4], (2, ROWS, SEQ, D), 1.0, 6.0, ((0, 2), (1, 16)))
    w_query = scatter_about(splits[5], (D, D), (16 * D) ** -0.5, 0.0546875)
    w_key = scatter_about(splits[6], (D, D), D ** -0.5, 0.21875)
    w_value = scatter_about(splits[7], (D, D), D ** -0.5, 0.21875)
    w_mixed = scatter_about(splits[8], (D, D), (D // 8) ** -0.5, 0.625)
    w_inner = scatter_about(splits[9], (D, FF), D ** -0.5, 0.21875)
    w_outer = scatter_about(splits[10], (FF, D), FF ** -0.5, 0.109375)
    gain_attn = jnp.clip(1.0 + 0.15 * jax.random.normal(splits[11], (D,), jnp.float32), 0.25, 1.75)
    gain_ffn = jnp.clip(1.0 + 0.15 * jax.random.normal(splits[12], (D,), jnp.float32), 0.25, 1.75)
    rel_table = scatter_about(splits[13], (BUCKETS, HEADS), 1.0, 4.0, (), jnp.float32)
    return {"tokens": tokens, "lengths": lengths, "doc_groups": doc_groups, "positives": positives, "cotangent": cotangent, "w_query": w_query, "w_key": w_key, "w_value": w_value, "w_mixed": w_mixed, "w_inner": w_inner, "w_outer": w_outer, "gain_attn": gain_attn, "gain_ffn": gain_ffn, "rel_table": rel_table}


EPSILON = 1e-06
SCALE = 50.0
NEGATIVE = -1000000000.0
THRESHOLDS = (12, 16, 23, 32, 46, 64, 91)
HIGHEST = lax.Precision.HIGHEST

@jax.custom_vjp
def low(v):
    return lax.optimization_barrier(v.astype(jnp.bfloat16)).astype(jnp.float32)

@jax.custom_vjp
def low_back(v):
    return v

def low_keep(v):
    return (low(v), None)

def low_pass(kept, grad):
    return (grad,)

def back_keep(v):
    return (v, None)

def back_low(kept, grad):
    return (low(grad),)
low.defvjp(low_keep, low_pass)
low_back.defvjp(back_keep, back_low)

def bucket_ids(length):
    places = jnp.arange(length, dtype=jnp.int32)
    offsets = places[None, :] - places[:, None]
    distance = jnp.abs(offsets)
    distant = 8 + sum(((distance >= limit).astype(jnp.int32) for limit in THRESHOLDS))
    buckets = jnp.where(distance < 8, distance, distant)
    return buckets + 16 * (offsets > 0).astype(jnp.int32)

def bucket_onehot(length, count_buckets):
    ids = bucket_ids(length)
    return (ids[:, :, None] == jnp.arange(count_buckets, dtype=jnp.int32)[None, None, :]).astype(jnp.float32)

def normalize(values, gain_vec):
    return values * lax.rsqrt(lax.optimization_barrier(jnp.mean(values * values, -1, keepdims=True)) + EPSILON) * gain_vec

def contrast(stacked, doc_groups, positives):
    unit_vecs = stacked * lax.rsqrt(lax.optimization_barrier(jnp.sum(stacked * stacked, -1, keepdims=True)) + EPSILON)
    scores = SCALE * jnp.dot(unit_vecs[0], unit_vecs[1].T, precision=HIGHEST, preferred_element_type=jnp.float32)
    indices = jnp.arange(doc_groups.shape[0], dtype=jnp.int32)
    chosen = positives[:, None] == indices[None, :]
    query_groups = lax.optimization_barrier(jnp.sum(jnp.where(chosen, doc_groups[None, :], 0), 1))
    same_group = query_groups[:, None] == doc_groups[None, :]
    masked = jnp.where(same_group, scores, NEGATIVE)
    highest = lax.optimization_barrier(jnp.max(masked, 1, keepdims=True))
    log_total = highest[:, 0] + jnp.log(lax.optimization_barrier(jnp.sum(jnp.exp(masked - highest), 1)))
    matched = lax.optimization_barrier(jnp.sum(jnp.where(chosen, scores, 0.0), 1))
    return jnp.sum(log_total - matched)

def matmul(left, right):
    return jnp.dot(left, right, precision=HIGHEST, preferred_element_type=jnp.float32)

def layer_block(inputs, present, weights, bias):
    w_query, w_key, w_value, w_mixed, w_inner, w_outer, gain_attn, gain_ffn = weights
    count_rows = inputs.shape[0]
    flat = inputs.reshape(-1, D)
    normed1 = low(normalize(flat, gain_attn))

    def heads_of(matrix):
        return low(low_back(matmul(normed1, matrix))).reshape(count_rows, SEQ, HEADS, HEAD_SIZE)
    queries = heads_of(w_query)
    keys_all = heads_of(w_key)
    values_all = heads_of(w_value)
    scores = jnp.einsum('gqhd,gkhd->ghqk', queries, keys_all, precision=HIGHEST) + bias[None]
    scores = low_back(scores)
    scores = jnp.where(present[:, None, None, :], scores, NEGATIVE)
    weights_soft = low(jax.nn.softmax(scores, axis=-1))
    heads_out = jnp.einsum('ghqk,gkhd->gqhd', weights_soft, values_all, precision=HIGHEST).reshape(-1, D)
    heads_out = low(low_back(heads_out))
    hidden1 = flat + low_back(matmul(heads_out, w_mixed))
    normed2 = low(normalize(hidden1, gain_ffn))
    inner_pre = low_back(matmul(normed2, w_inner))
    activated = low(jax.nn.gelu(inner_pre, approximate=False))
    output = hidden1 + low_back(matmul(activated, w_outer))
    return output.reshape(count_rows, SEQ, D)

def encode(inputs, weights, bias_table, present):
    onehot = bucket_onehot(SEQ, BUCKETS)
    bias = jnp.einsum('qkb,bh->hqk', onehot, bias_table, precision=HIGHEST)
    group_rows = math.gcd(2 * ROWS, max(1, 4096 // SEQ))
    blocks = inputs.reshape(-1, group_rows, SEQ, D)
    masks = present.reshape(-1, group_rows, SEQ)

    def one_block(pair):
        return layer_block(pair[0], pair[1], weights, bias)
    outputs = lax.map(jax.checkpoint(one_block), (blocks, masks))
    return outputs.reshape(inputs.shape)

def reference(tokens, lengths, doc_groups, positives, cotangent, w_query, w_key, w_value, w_mixed, w_inner, w_outer, gain_attn, gain_ffn, rel_table):
    inputs = tokens.astype(jnp.float32)
    upstream = cotangent.astype(jnp.float32)
    present = jnp.arange(SEQ, dtype=jnp.int32)[None, None, :] < lengths[:, :, None]
    length_f = lengths.astype(jnp.float32)
    matrices = tuple((matrix.astype(jnp.float32) for matrix in (w_query, w_key, w_value, w_mixed, w_inner, w_outer)))

    def objective(inputs, wq_f, wk_f, wv_f, wm_f, wi_f, wo_f, gain_one, gain_two, bias_table):
        output = encode(inputs, (wq_f, wk_f, wv_f, wm_f, wi_f, wo_f, gain_one, gain_two), bias_table, present)
        pooled = lax.optimization_barrier(jnp.sum(jnp.where(present[:, :, :, None], output, 0.0), 2)) / length_f[:, :, None]
        summed_ce = contrast(pooled, doc_groups, positives)
        return (jnp.sum(output * upstream) + summed_ce, (output, pooled, summed_ce))
    primals = (inputs,) + matrices + (gain_attn, gain_ffn, rel_table)
    unused, backward, extras = jax.vjp(objective, *primals, has_aux=True)
    output, pooled, summed_ce = extras
    grads = backward(jnp.ones((), jnp.float32))
    loss = summed_ce / doc_groups.shape[0]
    return (output.astype(jnp.bfloat16), pooled, loss, grads[0].astype(jnp.bfloat16), grads[1], grads[2], grads[3], grads[4], grads[5], grads[6], grads[7], grads[8], grads[9])
```

```python
import functools

import jax
import jax.numpy as jnp
from jax import lax
from jax.experimental import pallas as pl
from jax.experimental.pallas import tpu as pltpu
from jax.sharding import PartitionSpec as P

EPSILON = 1e-06
SCALE = 50.0
NEGATIVE = -1000000000.0
THRESHOLDS = (12, 16, 23, 32, 46, 64, 91)
HIGHEST = lax.Precision.HIGHEST


def bucket_ids(length):
    places = jnp.arange(length, dtype=jnp.int32)
    offsets = places[None, :] - places[:, None]
    distance = jnp.abs(offsets)
    distant = 8 + sum(((distance >= limit).astype(jnp.int32) for limit in THRESHOLDS))
    buckets = jnp.where(distance < 8, distance, distant)
    return buckets + 16 * (offsets > 0).astype(jnp.int32)


def bucket_onehot(length, count_buckets):
    ids = bucket_ids(length)
    return (ids[:, :, None] == jnp.arange(count_buckets, dtype=jnp.int32)[None, None, :]).astype(
        jnp.float32
    )


def normalize(values, gain_vec):
    return values * lax.rsqrt(jnp.mean(values * values, -1, keepdims=True) + EPSILON) * gain_vec


def contrast(stacked, doc_groups, positives):
    unit_vecs = stacked * lax.rsqrt(jnp.sum(stacked * stacked, -1, keepdims=True) + EPSILON)
    scores = SCALE * jnp.dot(
        unit_vecs[0], unit_vecs[1].T, precision=HIGHEST, preferred_element_type=jnp.float32
    )
    indices = jnp.arange(doc_groups.shape[0], dtype=jnp.int32)
    chosen = positives[:, None] == indices[None, :]
    query_groups = jnp.sum(jnp.where(chosen, doc_groups[None, :], 0), 1)
    same_group = query_groups[:, None] == doc_groups[None, :]
    masked = jnp.where(same_group, scores, NEGATIVE)
    highest = jnp.max(masked, 1, keepdims=True)
    log_total = highest[:, 0] + jnp.log(jnp.sum(jnp.exp(masked - highest), 1))
    matched = jnp.sum(jnp.where(chosen, scores, 0.0), 1)
    return jnp.sum(log_total - matched)


def smooth(values):
    return jax.nn.gelu(values, approximate=False)


def matmul(left, right):
    return jnp.dot(left, right, preferred_element_type=jnp.float32)


def left_product(left, right):
    return lax.dot_general(
        left, right, (((0,), (0,)), ((), ())), preferred_element_type=jnp.float32
    )


def right_product(left, right):
    return lax.dot_general(
        left, right, (((1,), (1,)), ((), ())), preferred_element_type=jnp.float32
    )


LINK = 45.0e3
CORE = 480.0e3
MESH = pl.DeviceIdType.MESH


class Bit:
    def __init__(self, axis, mask, place):
        self.axis, self.mask = axis, mask
        self.value = lax.rem(lax.div(place[axis], jnp.int32(mask)), jnp.int32(2))
        other = dict(place)
        other[axis] = place[axis] + mask * (1 - 2 * self.value)
        self.partner = (other["tower"], other["batch"])


def bit_names(sizes):
    names = []
    for axis in ("tower", "batch"):
        mask = 1
        while mask < sizes[axis]:
            names.append((axis, mask))
            mask *= 2
    return names


def bit_orders(sizes):
    tower = [k for k, name in enumerate(bit_names(sizes)) if name[0] == "tower"]
    rest = [k for k, name in enumerate(bit_names(sizes)) if name[0] == "batch"]
    firsts = [(0, 1, 2), (1, 0, 2), (2, 0, 1), (2, 1, 0)]
    return [tower + [rest[i] for i in first] + rest[3:] for first in firsts]


class Unit:
    def __init__(self, name, matrix, row, rows, col, cols, order):
        self.name, self.matrix = name, matrix
        self.row, self.rows, self.col, self.cols, self.order = row, rows, col, cols, order
        self.steps = []
        size = rows
        back = []
        recv = 0
        for k in order:
            halves = size % 16 == 0
            sent = size // 2 if halves else size
            self.steps.append(("halve" if halves else "whole", k, sent, recv))
            recv += sent
            if halves:
                back.append(("double", k, sent, 0))
                size = sent
        self.recv_rows = recv
        self.returns = len(self.steps)
        self.steps += back[::-1]

    def place_at(self, bits):
        start = jnp.int32(self.row)
        self.starts = []
        stack = []
        for kind, k, sent, _ in self.steps:
            self.starts.append(start)
            if kind == "halve":
                stack.append(start)
                start = start + bits[k].value * sent
            elif kind == "double":
                start = stack.pop()


def service_order(units, names, ready, work=()):
    free = {k: 0.0 for k in range(len(names))}
    clock = 0.0
    waiting = []
    order = []

    def issue(u, s, now):
        kind, k, sent, _ = units[u].steps[s]
        size = sent * units[u].cols * 4
        rate = CORE if names[k][0] == "tower" else LINK / (2 if names[k][1] == 8 else 1)
        start = max(now, free[k])
        free[k] = start + size / rate
        waiting.append((free[k] + 1.5, u, s))

    for u in range(len(units)):
        clock = max(clock, ready[u])
        issue(u, 0, clock)
    while waiting:
        waiting.sort()
        done, u, s = waiting.pop(0)
        clock = max(clock, done) + 0.3
        kind, k, sent, _ = units[u].steps[s]
        if kind != "double":
            clock += sent * units[u].cols * 4 / 2.0e6
        order.append((u, s))
        if s + 1 < len(units[u].steps):
            issue(u, s + 1, clock)
    return order, clock


class Exchange:
    def __init__(self, units, bits, grads, kept, land, outs, sems):
        self.units, self.bits, self.grads, self.kept, self.land, self.outs = units, bits, grads, kept, land, outs
        self.send_sem, self.recv_sem, self.load_sem, self.store_sem = sems
        for unit in units:
            unit.place_at(bits)

    def part(self, refs, unit, start, rows):
        return refs[unit.matrix].at[pl.ds(pl.multiple_of(start, 8), rows), pl.ds(unit.col, unit.cols)]

    def own(self, u, start, rows):
        unit = self.units[u]
        return self.kept[u].at[pl.ds(pl.multiple_of(start - unit.starts[1], 8), rows), :]

    def load(self, u):
        unit = self.units[u]
        half = unit.steps[0][2]
        return pltpu.make_async_copy(
            self.part(self.grads, unit, unit.starts[1], half), self.kept[u], self.load_sem.at[u]
        )

    def store(self, u):
        unit = self.units[u]
        s = unit.returns
        start, rows = unit.starts[s], unit.steps[s][2]
        return pltpu.make_async_copy(
            self.own(u, start, rows), self.part(self.outs, unit, start, rows), self.store_sem.at[u]
        )

    def copy(self, u, s):
        unit = self.units[u]
        kind, k, sent, recv = unit.steps[s]
        bit = self.bits[k]
        start = unit.starts[s]
        if kind == "halve":
            start = start + (1 - bit.value) * sent
        if s == 0:
            source = self.part(self.grads, unit, start, sent)
        elif s <= unit.returns:
            source = self.own(u, start, sent)
        else:
            source = self.part(self.outs, unit, start, sent)
        if kind == "double":
            target = self.part(self.outs, unit, start, sent)
        else:
            target = self.land[u].at[pl.ds(recv, sent), :]
        return pltpu.make_async_remote_copy(
            src_ref=source,
            dst_ref=target,
            send_sem=self.send_sem.at[u, s],
            recv_sem=self.recv_sem.at[u, s],
            device_id=bit.partner,
            device_id_type=MESH,
        )

    def begin(self, u):
        self.load(u).start()
        self.copy(u, 0).start()

    def serve(self, u, s):
        unit = self.units[u]
        if s == 0:
            self.load(u).wait()
        self.copy(u, s).wait()
        kind, k, sent, recv = unit.steps[s]
        if kind != "double":
            start = unit.starts[s]
            if kind == "halve":
                start = start + self.bits[k].value * sent
            kept = self.own(u, start, sent)
            kept[...] = kept[...] + self.land[u][pl.ds(recv, sent), :]
        if s + 1 == unit.returns:
            self.store(u).start()
        if s == unit.returns:
            self.store(u).wait()
        if s + 1 < len(unit.steps):
            self.copy(u, s + 1).start()


def gradient_units(sizes):
    orders = bit_orders(sizes)
    pattern = (0, 1, 2, 0, 1, 3)
    units = [Unit("outer%d" % i, 0, 512 * i, 512, 0, 768, orders[pattern[i]]) for i in range(6)]
    units += [Unit("inner%d" % i, 1, 0, 768, 512 * i, 512, orders[pattern[i]]) for i in range(6)]
    for i in range(8):
        units.append(Unit("proj%d" % i, 2 + i // 2, 0, 768, 384 * (i % 2), 384, orders[pattern[i % 6]]))
    return units


def sum_kernel(sizes, units, names, *refs):
    count = len(units)
    grads, small_in = refs[:6], refs[6]
    outs, small_out = refs[7:13], refs[13]
    kept, land = refs[14 : 14 + count], refs[14 + count : 14 + 2 * count]
    small_land, send_sem, recv_sem, small_send, small_recv, load_sem, store_sem = refs[14 + 2 * count :]
    place = {axis: lax.axis_index(axis) for axis in ("tower", "batch")}
    bits = [Bit(axis, mask, place) for axis, mask in names]
    exchange = Exchange(units, bits, grads, kept, land, outs, (send_sem, recv_sem, load_sem, store_sem))
    barrier = pltpu.get_barrier_semaphore()
    for bit in bits:
        pl.semaphore_signal(barrier, inc=1, device_id=bit.partner, device_id_type=MESH)
    pl.semaphore_wait(barrier, len(bits))
    for u in range(count):
        exchange.begin(u)

    def small_copy(k):
        return pltpu.make_async_remote_copy(
            src_ref=small_out,
            dst_ref=small_land.at[k],
            send_sem=small_send.at[k],
            recv_sem=small_recv.at[k],
            device_id=bits[k].partner,
            device_id_type=MESH,
        )

    small_out[...] = small_in[...]
    small_copy(0).start()
    order, _ = service_order(units, names, [0.0] * count)
    small_at = {len(order) * (k + 1) // (len(bits) + 1): k for k in range(len(bits))}
    for place_in_order, (u, s) in enumerate(order):
        if place_in_order in small_at:
            k = small_at[place_in_order]
            small_copy(k).wait()
            small_out[...] = small_out[...] + small_land[k]
            if k + 1 < len(bits):
                small_copy(k + 1).start()
        exchange.serve(u, s)


def sum_gradients(sizes, grads, small):
    units = gradient_units(sizes)
    names = bit_names(sizes)
    steps = max(len(unit.steps) for unit in units)
    any_spec = pl.BlockSpec(memory_space=pl.ANY)
    vmem_spec = pl.BlockSpec(memory_space=pltpu.VMEM)
    return pl.pallas_call(
        functools.partial(sum_kernel, sizes, units, names),
        out_shape=[jax.ShapeDtypeStruct(g.shape, g.dtype) for g in grads]
        + [jax.ShapeDtypeStruct(small.shape, small.dtype)],
        in_specs=[any_spec] * 6 + [vmem_spec],
        out_specs=[any_spec] * 6 + [vmem_spec],
        scratch_shapes=[pltpu.VMEM((unit.steps[0][2], unit.cols), jnp.float32) for unit in units]
        + [pltpu.VMEM((unit.recv_rows, unit.cols), jnp.float32) for unit in units]
        + [
            pltpu.VMEM((len(names),) + small.shape, jnp.float32),
            pltpu.SemaphoreType.DMA((len(units), steps)),
            pltpu.SemaphoreType.DMA((len(units), steps)),
            pltpu.SemaphoreType.DMA((len(names),)),
            pltpu.SemaphoreType.DMA((len(names),)),
            pltpu.SemaphoreType.DMA((len(units),)),
            pltpu.SemaphoreType.DMA((len(units),)),
        ],
        compiler_params=pltpu.CompilerParams(
            collective_id=0, has_side_effects=True, vmem_limit_bytes=62 * 2**20
        ),
    )(*grads, small)


def shards(
    tokens,
    lengths,
    doc_groups,
    positives,
    cotangent,
    w_query,
    w_key,
    w_value,
    w_mixed,
    w_inner,
    w_outer,
    gain_attn,
    gain_ffn,
    rel_table,
):
    rows_dev = tokens.shape[1]
    seq_len = tokens.shape[2]
    width = tokens.shape[3]
    heads = rel_table.shape[1]
    head_size = width // heads
    count = rows_dev * seq_len
    inputs = tokens.reshape(count, width).astype(jnp.float32)
    row_lengths = lengths.reshape(rows_dev)
    length_f = row_lengths.astype(jnp.float32)
    present = jnp.arange(seq_len, dtype=jnp.int32)[None, :] < row_lengths[:, None]
    onehot = bucket_onehot(seq_len, rel_table.shape[0])
    bias = jnp.einsum("qkb,bh->hqk", onehot, rel_table, precision=HIGHEST)

    def split_heads(matrix):
        return matrix.reshape(rows_dev, seq_len, heads, head_size)

    normed1, norm_back1 = jax.vjp(normalize, inputs, gain_attn)
    normed1 = normed1.astype(jnp.bfloat16)
    queries = matmul(normed1, w_query).astype(jnp.bfloat16)
    keys_all = matmul(normed1, w_key).astype(jnp.bfloat16)
    values_all = matmul(normed1, w_value).astype(jnp.bfloat16)

    def score_of():
        raw = (
            jnp.einsum(
                "rqhd,rkhd->rhqk",
                split_heads(queries),
                split_heads(keys_all),
                preferred_element_type=jnp.float32,
            )
            + bias[None]
        )
        return jnp.where(present[:, None, None, :], raw, NEGATIVE)

    scores = score_of()
    highest = jnp.max(scores, -1, keepdims=True)
    log_sums = highest + jnp.log(jnp.sum(jnp.exp(scores - highest), -1, keepdims=True))
    weights_soft = jnp.exp(scores - log_sums)
    heads_out = jnp.einsum(
        "rhqk,rkhd->rqhd",
        weights_soft.astype(jnp.bfloat16),
        split_heads(values_all),
        preferred_element_type=jnp.float32,
    )
    heads_out = heads_out.reshape(count, width).astype(jnp.bfloat16)
    hidden1 = inputs + matmul(heads_out, w_mixed)
    normed2, norm_back2 = jax.vjp(normalize, hidden1, gain_ffn)
    normed2 = normed2.astype(jnp.bfloat16)
    inner_pre = matmul(normed2, w_inner)
    activated, smooth_back = jax.vjp(smooth, inner_pre)
    activated = activated.astype(jnp.bfloat16)
    output = hidden1 + matmul(activated, w_outer)
    activations = output.astype(jnp.bfloat16).reshape(tokens.shape)
    row_outputs = output.reshape(rows_dev, seq_len, width)
    pooled = jnp.sum(jnp.where(present[:, :, None], row_outputs, 0.0), 1) / length_f[:, None]
    gathered = lax.all_gather(pooled[None], ("tower", "batch"), axis=1, tiled=True)[0]
    position = lax.axis_index(("tower", "batch"))

    def summed_loss(every):
        return contrast(every.reshape(2, -1, width), doc_groups, positives)

    summed_ce, loss_back = jax.vjp(summed_loss, gathered)
    grad_every = loss_back(jnp.ones((), jnp.float32))[0]
    loss = summed_ce / doc_groups.shape[0]
    grad_pooled = lax.dynamic_slice_in_dim(grad_every, position * rows_dev, rows_dev, 0)
    spread_grad = jnp.where(
        present[:, :, None], grad_pooled[:, None, :] / length_f[:, None, None], 0.0
    )
    grad_output = cotangent.reshape(count, width).astype(jnp.float32) + spread_grad.reshape(
        count, width
    )
    grad_out_b = grad_output.astype(jnp.bfloat16)
    w_outer_grad = left_product(activated, grad_out_b)
    grad_act = right_product(grad_out_b, w_outer)
    grad_inner = smooth_back(grad_act)[0].astype(jnp.bfloat16)
    w_inner_grad = left_product(normed2, grad_inner)
    grad_normed2 = right_product(grad_inner, w_inner)
    grad_hid_norm, gain_ffn_grad = norm_back2(grad_normed2)
    grad_hidden1 = grad_output + grad_hid_norm
    grad_attn_b = grad_hidden1.astype(jnp.bfloat16)
    w_mixed_grad = left_product(heads_out, grad_attn_b)
    grad_heads = right_product(grad_attn_b, w_mixed).astype(jnp.bfloat16)
    again = jnp.exp(score_of() - log_sums)
    grad_soft = jnp.einsum(
        "rqhd,rkhd->rhqk",
        split_heads(grad_heads),
        split_heads(values_all),
        preferred_element_type=jnp.float32,
    )
    row_delta = jnp.sum(again * grad_soft, -1, keepdims=True)
    grad_scores = (again * (grad_soft - row_delta)).astype(jnp.bfloat16)
    grad_query = (
        jnp.einsum(
            "rhqk,rkhd->rqhd",
            grad_scores,
            split_heads(keys_all),
            preferred_element_type=jnp.float32,
        )
        .reshape(count, width)
        .astype(jnp.bfloat16)
    )
    grad_key = (
        jnp.einsum(
            "rhqk,rqhd->rkhd", grad_scores, split_heads(queries), preferred_element_type=jnp.float32
        )
        .reshape(count, width)
        .astype(jnp.bfloat16)
    )
    grad_value = (
        jnp.einsum(
            "rhqk,rqhd->rkhd",
            again.astype(jnp.bfloat16),
            split_heads(grad_heads),
            preferred_element_type=jnp.float32,
        )
        .reshape(count, width)
        .astype(jnp.bfloat16)
    )
    bias_grad = jnp.sum(grad_scores.astype(jnp.float32), 0)
    table_grad = jnp.einsum("qkb,hqk->bh", onehot, bias_grad, precision=HIGHEST)
    w_query_grad = left_product(normed1, grad_query)
    w_key_grad = left_product(normed1, grad_key)
    w_value_grad = left_product(normed1, grad_value)
    grad_normed1 = (
        right_product(grad_query, w_query)
        + right_product(grad_key, w_key)
        + right_product(grad_value, w_value)
    )
    grad_in_norm, gain_attn_grad = norm_back1(grad_normed1)
    tokens_grad = (grad_hidden1 + grad_in_norm).astype(jnp.bfloat16).reshape(tokens.shape)
    sizes = {axis: lax.axis_size(axis) for axis in ("tower", "batch")}
    small = jnp.concatenate(
        [
            gain_attn_grad[None],
            gain_ffn_grad[None],
            jnp.pad(table_grad.reshape(1, -1), ((0, 0), (0, width - table_grad.size))),
            jnp.zeros((5, width), jnp.float32),
        ]
    )
    total = sum_gradients(
        sizes,
        [w_outer_grad, w_inner_grad, w_query_grad, w_key_grad, w_value_grad, w_mixed_grad],
        small,
    )
    results = [
        total[2],
        total[3],
        total[4],
        total[5],
        total[1],
        total[0],
        total[6][0],
        total[6][1],
        total[6][2, : table_grad.size].reshape(table_grad.shape),
    ]
    return (
        activations,
        pooled[None],
        loss,
        tokens_grad,
        results[0],
        results[1],
        results[2],
        results[3],
        results[4],
        results[5],
        results[6],
        results[7],
        results[8],
    )


def solution(mesh):
    return jax.shard_map(
        shards,
        mesh=mesh,
        in_specs=(
            P("tower", "batch", None, None),
            P("tower", "batch"),
            P(),
            P(),
            P("tower", "batch", None, None),
            P(),
            P(),
            P(),
            P(),
            P(),
            P(),
            P(),
            P(),
            P(),
        ),
        out_specs=(
            P("tower", "batch", None, None),
            P("tower", "batch", None),
            P(),
            P("tower", "batch", None, None),
            P(),
            P(),
            P(),
            P(),
            P(),
            P(),
            P(),
            P(),
            P(),
        ),
        check_vma=False,
    )
```

```python
import functools

import jax
import jax.numpy as jnp
from jax import lax
from jax.experimental import pallas as pl
from jax.experimental.pallas import tpu as pltpu
from jax.sharding import PartitionSpec as P

EPSILON = 1e-06
SCALE = 50.0
NEGATIVE = -1000000000.0
THRESHOLDS = (12, 16, 23, 32, 46, 64, 91)
HIGHEST = lax.Precision.HIGHEST


LINK = 45.0e3
CORE = 480.0e3
MESH = pl.DeviceIdType.MESH


class Bit:
    def __init__(self, axis, mask, place):
        self.axis, self.mask = axis, mask
        self.value = lax.rem(lax.div(place[axis], jnp.int32(mask)), jnp.int32(2))
        other = dict(place)
        other[axis] = place[axis] + mask * (1 - 2 * self.value)
        self.partner = (other["tower"], other["batch"])


def bit_names(sizes):
    names = []
    for axis in ("tower", "batch"):
        mask = 1
        while mask < sizes[axis]:
            names.append((axis, mask))
            mask *= 2
    return names


def bit_orders(sizes):
    tower = [k for k, name in enumerate(bit_names(sizes)) if name[0] == "tower"]
    rest = [k for k, name in enumerate(bit_names(sizes)) if name[0] == "batch"]
    firsts = [(0, 1, 2), (1, 0, 2), (2, 0, 1), (2, 1, 0)]
    return [tower + [rest[i] for i in first] + rest[3:] for first in firsts]


class Unit:
    def __init__(self, name, matrix, row, rows, col, cols, order):
        self.name, self.matrix = name, matrix
        self.row, self.rows, self.col, self.cols, self.order = row, rows, col, cols, order
        self.steps = []
        size = rows
        back = []
        recv = 0
        for k in order:
            halves = size % 16 == 0
            sent = size // 2 if halves else size
            self.steps.append(("halve" if halves else "whole", k, sent, recv))
            recv += sent
            if halves:
                back.append(("double", k, sent, 0))
                size = sent
        self.recv_rows = recv
        self.returns = len(self.steps)
        self.steps += back[::-1]

    def place_at(self, bits):
        start = jnp.int32(self.row)
        self.starts = []
        stack = []
        for kind, k, sent, _ in self.steps:
            self.starts.append(start)
            if kind == "halve":
                stack.append(start)
                start = start + bits[k].value * sent
            elif kind == "double":
                start = stack.pop()


def service_order(units, names, ready, work=()):
    free = {k: 0.0 for k in range(len(names))}
    clock = 0.0
    waiting = []
    order = []

    def issue(u, s, now):
        kind, k, sent, _ = units[u].steps[s]
        size = sent * units[u].cols * 4
        rate = CORE if names[k][0] == "tower" else LINK / (2 if names[k][1] == 8 else 1)
        start = max(now, free[k])
        free[k] = start + size / rate
        waiting.append((free[k] + 1.5, u, s))

    for u in range(len(units)):
        clock = max(clock, ready[u])
        issue(u, 0, clock)
    while waiting:
        waiting.sort()
        done, u, s = waiting.pop(0)
        clock = max(clock, done) + 0.3
        kind, k, sent, _ = units[u].steps[s]
        if kind != "double":
            clock += sent * units[u].cols * 4 / 2.0e6
        order.append((u, s))
        if s + 1 < len(units[u].steps):
            issue(u, s + 1, clock)
    return order, clock


class Exchange:
    def __init__(self, units, bits, grads, kept, land, outs, sems):
        self.units, self.bits, self.grads, self.kept, self.land, self.outs = units, bits, grads, kept, land, outs
        self.send_sem, self.recv_sem, self.load_sem, self.store_sem = sems
        for unit in units:
            unit.place_at(bits)

    def part(self, refs, unit, start, rows):
        return refs[unit.matrix].at[pl.ds(pl.multiple_of(start, 8), rows), pl.ds(unit.col, unit.cols)]

    def own(self, u, start, rows):
        unit = self.units[u]
        return self.kept[u].at[pl.ds(pl.multiple_of(start - unit.starts[1], 8), rows), :]

    def load(self, u):
        unit = self.units[u]
        half = unit.steps[0][2]
        return pltpu.make_async_copy(
            self.part(self.grads, unit, unit.starts[1], half), self.kept[u], self.load_sem.at[u]
        )

    def store(self, u):
        unit = self.units[u]
        s = unit.returns
        start, rows = unit.starts[s], unit.steps[s][2]
        return pltpu.make_async_copy(
            self.own(u, start, rows), self.part(self.outs, unit, start, rows), self.store_sem.at[u]
        )

    def copy(self, u, s):
        unit = self.units[u]
        kind, k, sent, recv = unit.steps[s]
        bit = self.bits[k]
        start = unit.starts[s]
        if kind == "halve":
            start = start + (1 - bit.value) * sent
        if s == 0:
            source = self.part(self.grads, unit, start, sent)
        elif s <= unit.returns:
            source = self.own(u, start, sent)
        else:
            source = self.part(self.outs, unit, start, sent)
        if kind == "double":
            target = self.part(self.outs, unit, start, sent)
        else:
            target = self.land[u].at[pl.ds(recv, sent), :]
        return pltpu.make_async_remote_copy(
            src_ref=source,
            dst_ref=target,
            send_sem=self.send_sem.at[u, s],
            recv_sem=self.recv_sem.at[u, s],
            device_id=bit.partner,
            device_id_type=MESH,
        )

    def begin(self, u):
        self.load(u).start()
        self.copy(u, 0).start()

    def serve(self, u, s):
        unit = self.units[u]
        if s == 0:
            self.load(u).wait()
        self.copy(u, s).wait()
        kind, k, sent, recv = unit.steps[s]
        if kind != "double":
            start = unit.starts[s]
            if kind == "halve":
                start = start + self.bits[k].value * sent
            kept = self.own(u, start, sent)
            kept[...] = kept[...] + self.land[u][pl.ds(recv, sent), :]
        if s + 1 == unit.returns:
            self.store(u).start()
        if s == unit.returns:
            self.store(u).wait()
        if s + 1 < len(unit.steps):
            self.copy(u, s + 1).start()


LOW = jnp.bfloat16
FULL = jnp.float32


def dot_nn(left, right):
    return lax.dot_general(left, right, (((1,), (0,)), ((), ())), preferred_element_type=FULL)


def dot_nt(left, right):
    return lax.dot_general(left, right, (((1,), (1,)), ((), ())), preferred_element_type=FULL)


def dot_tn(left, right):
    return lax.dot_general(left, right, (((0,), (0,)), ((), ())), preferred_element_type=FULL)


def loop(count, body):
    def step(i, carry):
        body(i)
        return carry

    lax.fori_loop(0, count, step, 0)


def rows_of(i, size):
    return pl.ds(pl.multiple_of(i * size, size), size)


def offset_buckets(shift):
    keys = lax.broadcasted_iota(jnp.int32, (128, 128), 0)
    queries = lax.broadcasted_iota(jnp.int32, (128, 128), 1)
    offsets = keys - queries + 128 * shift
    distance = jnp.abs(offsets)
    distant = jnp.full((128, 128), 8, jnp.int32)
    for limit in THRESHOLDS:
        distant = distant + jnp.where(distance >= limit, 1, 0)
    buckets = jnp.where(distance < 8, distance, distant)
    return buckets + jnp.where(offsets > 0, 16, 0)


NEAR = ((-1, range(1, 16)), (0, range(32)), (1, range(17, 32)))


def bias_strip(bias, table, head, jb, blocks):
    parts = []
    for ib in range(blocks):
        shift = jb - ib
        if abs(shift) <= 1:
            parts.append(bias[head, shift + 1])
        else:
            parts.append(jnp.full((128, 128), table[31 if shift > 0 else 15, head], FULL))
    return jnp.concatenate(parts, axis=1)


def forward_kernel(
    tokens, lengths, wq, wk, wv, wm, wi, wo, gain1, gain2, table,
    q_out, k_out, v_out, ho_out, n1_out, n2_out, h1_out, act_out, slope_out, result_out, lse_out, bias_out, pooled_out,
    x_s, wq_s, wk_s, wv_s, wm_s, wi_s, wo_s, q_s, k_s, v_s, ho_s, n1_s, n2_s, h1_s, act_s, slope_s, result_s, total_s,
    score_s, prob_s, in_sem, out_sem,
):
    count, width = tokens.shape
    rows, seq = lengths.shape[0], tokens.shape[0] // lengths.shape[0]
    heads = table.shape[1]
    size = width // heads
    hidden = wi.shape[1]
    parts = hidden // width
    loads = [
        pltpu.make_async_copy(source, target, in_sem.at[i])
        for i, (source, target) in enumerate(
            [(tokens, x_s), (wq, wq_s), (wk, wk_s), (wv, wv_s), (wm, wm_s), (wi, wi_s), (wo, wo_s)]
        )
    ]
    for load in loads:
        load.start()
    stores = []

    def store(source, target):
        copy = pltpu.make_async_copy(source, target, out_sem.at[len(stores)])
        copy.start()
        stores.append(copy)

    ids = [offset_buckets(shift) for shift, _ in NEAR]

    def bias_of(head):
        for place, (shift, members) in enumerate(NEAR):
            block = jnp.zeros((128, 128), FULL)
            for b in members:
                block = jnp.where(ids[place] == b, table[b, head], block)
            bias_out[head, place] = block

    loop(heads, bias_of)
    block = 256
    loads[0].wait()

    def norm1(i):
        at = rows_of(i, block)
        x = x_s[at, :].astype(FULL)
        scale = lax.rsqrt(jnp.mean(x * x, -1, keepdims=True) + EPSILON)
        n1_s[at, :] = (x * scale * gain1[...]).astype(LOW)

    loop(count // block, norm1)
    store(n1_s, n1_out)
    for i, (w_s, p_s, p_out) in enumerate(((wq_s, q_s, q_out), (wk_s, k_s, k_out), (wv_s, v_s, v_out))):
        loads[1 + i].wait()

        def project(m, w_s=w_s, p_s=p_s):
            at = rows_of(m, 512)
            p_s[at, :] = dot_nn(n1_s[at, :], w_s[...]).astype(LOW)

        loop(count // 512, project)
        store(p_s, p_out)
    blocks = seq // 128
    lanes = lax.broadcasted_iota(jnp.int32, (seq, 2 * size), 1)
    keys = lax.broadcasted_iota(jnp.int32, (128, seq), 0)

    def attend(step):
        row = lax.div(step, jnp.int32(heads // 2))
        pair = lax.rem(step, jnp.int32(heads // 2))
        at = rows_of(row, seq)
        here = rows_of(pair, 2 * size)
        limit = lengths[row]
        q, k = q_s[at, here], k_s[at, here]
        vt = v_s[at, here].T
        found = []
        for side in range(2):
            head = pair * 2 + side
            chosen = jnp.where((lanes >= size) == (side == 1), q, jnp.zeros_like(q))
            score_s[side] = dot_nt(k, chosen)
        for side in range(2):
            head = pair * 2 + side
            top = jnp.full((1, seq), NEGATIVE, FULL)
            for jb in range(blocks):
                strip = score_s[side, jb * 128 : (jb + 1) * 128, :] + bias_strip(bias_out, table, head, jb, blocks)
                strip = jnp.where(keys + jb * 128 < limit, strip, NEGATIVE)
                score_s[side, jb * 128 : (jb + 1) * 128, :] = strip
                top = jnp.maximum(top, jnp.max(strip, 0, keepdims=True))
            mass = jnp.zeros((1, seq), FULL)
            for jb in range(blocks):
                strip = jnp.exp(score_s[side, jb * 128 : (jb + 1) * 128, :] - top)
                mass = mass + jnp.sum(strip, 0, keepdims=True)
                prob_s[side, jb * 128 : (jb + 1) * 128, :] = strip.astype(LOW)
            lse_out[row * heads + head] = top + jnp.log(mass)
            found.append(dot_nn(vt[side * size : (side + 1) * size, :], prob_s[side]) / mass)
        ho_s[at, here] = jnp.concatenate(found, 0).T.astype(LOW)

    loop(rows * (heads // 2), attend)
    store(ho_s, ho_out)
    loads[4].wait()

    def mix(i):
        at = rows_of(i, block)
        h1 = x_s[at, :].astype(FULL) + dot_nn(ho_s[at, :], wm_s[...])
        h1_s[at, :] = h1
        scale = lax.rsqrt(jnp.mean(h1 * h1, -1, keepdims=True) + EPSILON)
        n2_s[at, :] = (h1 * scale * gain2[...]).astype(LOW)

    loop(count // block, mix)
    store(h1_s, h1_out)
    store(n2_s, n2_out)
    loads[5].wait()
    loads[6].wait()

    for part in range(parts):
        columns = pl.ds(part * width, width)

        def feed(i, part=part, columns=columns):
            at = rows_of(i, block)
            inner = dot_nn(n2_s[at, :], wi_s[:, columns])
            share = 0.5 + 0.5 * lax.erf(inner * 0.7071067811865476)
            act = (inner * share).astype(LOW)
            act_s[at, columns] = act
            slope = share + inner * (jnp.exp(inner * inner * -0.5) * 0.3989422804014327)
            slope_s[at, columns] = slope.astype(LOW)
            more = dot_nn(act, wo_s[columns, :])
            if part == 0:
                total_s[at, :] = h1_s[at, :] + more
            elif part < parts - 1:
                total_s[at, :] = total_s[at, :] + more
            else:
                output = total_s[at, :] + more
                total_s[at, :] = output
                result_s[at, :] = output.astype(LOW)

        loop(count // block, feed)
        store(act_s.at[:, columns], act_out.at[:, columns])
        store(slope_s.at[:, columns], slope_out.at[:, columns])
    store(result_s, result_out)
    slots = lax.broadcasted_iota(jnp.int32, (seq, 1), 0)
    for row in range(rows):
        kept = jnp.where(slots < lengths[row], total_s[row * seq : (row + 1) * seq, :], 0.0)
        pooled_out[row : row + 1, :] = jnp.sum(kept, 0, keepdims=True) / lengths[row].astype(FULL)
    for copy in stores:
        copy.wait()


def forward(tokens, lengths, wq, wk, wv, wm, wi, wo, gain1, gain2, table):
    count, width = tokens.shape
    hidden = wi.shape[1]
    rows = lengths.shape[0]
    heads = table.shape[1]
    seq = count // rows
    shape = jax.ShapeDtypeStruct
    any_spec = pl.BlockSpec(memory_space=pl.ANY)
    vmem_spec = pl.BlockSpec(memory_space=pltpu.VMEM)
    smem_spec = pl.BlockSpec(memory_space=pltpu.SMEM)
    low = shape((count, width), LOW)
    wide = shape((count, hidden), LOW)
    weights = [pltpu.VMEM(w.shape, LOW) for w in (wq, wk, wv, wm, wi, wo)]
    narrow_s = pltpu.VMEM((count, width), LOW)
    full_s = pltpu.VMEM((count, width), FULL)
    wide_s = pltpu.VMEM((count, hidden), LOW)
    return pl.pallas_call(
        forward_kernel,
        out_shape=[low, low, low, low, low, low, shape((count, width), FULL), wide, wide, low]
        + [shape((rows * heads, 1, seq), FULL), shape((heads, 3, 128, 128), FULL), shape((rows, width), FULL)],
        in_specs=[any_spec, smem_spec] + [any_spec] * 6 + [vmem_spec] * 2 + [smem_spec],
        out_specs=[any_spec] * 10 + [vmem_spec] * 3,
        scratch_shapes=[narrow_s]
        + weights
        + [narrow_s] * 6
        + [full_s, wide_s, wide_s, narrow_s, full_s]
        + [
            pltpu.VMEM((2, seq, seq), FULL),
            pltpu.VMEM((2, seq, seq), LOW),
            pltpu.SemaphoreType.DMA((7,)),
            pltpu.SemaphoreType.DMA((24,)),
        ],
        compiler_params=pltpu.CompilerParams(vmem_limit_bytes=62 * 2**20),
    )(tokens, lengths, wq, wk, wv, wm, wi, wo, gain1.reshape(1, width), gain2.reshape(1, width), table)


def contrast_kernel(units, doc_groups_row, positives_col):
    count = doc_groups_row.shape[1]
    queries, documents = units
    precise = functools.partial(
        lax.dot_general, precision=HIGHEST, preferred_element_type=FULL
    )
    rates = [lax.rsqrt(jnp.sum(p * p, -1, keepdims=True) + EPSILON) for p in units]
    unit = [p * rate for p, rate in zip(units, rates)]
    scores = SCALE * precise(unit[0], unit[1], (((1,), (1,)), ((), ())))
    indices = lax.broadcasted_iota(jnp.int32, (count, count), 1)
    chosen = positives_col == indices
    query_groups = jnp.sum(jnp.where(chosen, doc_groups_row, 0), 1, keepdims=True)
    masked = jnp.where(query_groups == doc_groups_row, scores, NEGATIVE)
    highest = jnp.max(masked, 1, keepdims=True)
    weights = jnp.exp(masked - highest)
    mass = jnp.sum(weights, 1, keepdims=True)
    matched = jnp.sum(jnp.where(chosen, scores, 0.0), 1, keepdims=True)
    loss = jnp.sum(highest + jnp.log(mass) - matched, 0, keepdims=True) / count
    dscore = weights / mass - jnp.where(chosen, 1.0, 0.0)
    dunit = (
        SCALE * precise(dscore, unit[1], (((1,), (0,)), ((), ()))),
        SCALE * precise(dscore, unit[0], (((0,), (0,)), ((), ()))),
    )
    dpooled = [
        rate * (d - u * jnp.sum(u * d, -1, keepdims=True)) for rate, d, u in zip(rates, dunit, unit)
    ]
    return loss, dpooled


def middle_kernel(
    sizes, names,
    cot, pooled, lengths, doc_groups, positives, act, slope, wo, n2,
    wo_grad, wi_grad, dinner, spread_out, loss_out,
    cot_s, act_s, slope_s, wo_s, n2_s, dact_s, wo_grad_s, wi_grad_s, mass_s, every_s, pool_s,
    in_sem, out_sem, send_sem, recv_sem,
):
    count, width = cot_s.shape
    rows = pooled.shape[0]
    seq = count // rows
    parts = act_s.shape[1] // width
    places = sizes["batch"]
    place = {axis: lax.axis_index(axis) for axis in ("tower", "batch")}
    tower, batch = place["tower"], place["batch"]
    bits = [Bit(axis, mask, place) for axis, mask in names]
    hops = [k for k, name in enumerate(names) if name[0] == "batch"]
    hops += [k for k, name in enumerate(names) if name[0] == "tower"]
    loads = []

    def load(source, target):
        copy = pltpu.make_async_copy(source, target, in_sem.at[len(loads)])
        copy.start()
        loads.append(copy)

    def cut(part):
        return pl.ds(part * width, width)

    load(cot, cot_s)
    for part in range(parts):
        load(wo.at[cut(part), :], wo_s.at[cut(part), :])
    for part in range(parts):
        load(act.at[:, cut(part)], act_s.at[:, cut(part)])
    load(n2, n2_s)
    for part in range(parts):
        load(slope.at[:, cut(part)], slope_s.at[:, cut(part)])
    every_s[tower, batch] = pooled[...]
    barrier = pltpu.get_barrier_semaphore()
    for bit in bits:
        pl.semaphore_signal(barrier, inc=1, device_id=bit.partner, device_id_type=MESH)
    pl.semaphore_wait(barrier, len(bits))

    def hop(h):
        axis, mask = names[hops[h]]
        bit = bits[hops[h]]
        if axis == "batch":
            first = lax.div(batch, jnp.int32(mask)) * mask
            block = every_s.at[tower, pl.ds(first, mask)]
        else:
            block = every_s.at[tower]
        return pltpu.make_async_remote_copy(
            src_ref=block,
            dst_ref=block,
            send_sem=send_sem.at[h],
            recv_sem=recv_sem.at[h],
            device_id=bit.partner,
            device_id_type=MESH,
        )

    hop(0).start()
    slots = lax.broadcasted_iota(jnp.int32, (seq, 1), 0)
    columns = lax.broadcasted_iota(jnp.int32, (seq, 128), 1)
    marks = jnp.concatenate(
        [
            jnp.where((slots < lengths[row]) & (columns == row), 1.0, 0.0).astype(LOW)
            for row in range(rows)
        ],
        0,
    )

    def first_dact(part):
        loads[1 + part].wait()

        def body(i):
            at = rows_of(i, 512)
            dact_s[at, cut(part)] = dot_nt(cot_s[at, :], wo_s[cut(part), :])

        loop(count // 512, body)

    def first_grad(part):
        loads[1 + parts + part].wait()
        wo_grad_s[cut(part), :] = dot_tn(act_s[:, cut(part)], cot_s[...])
        mass_s[cut(part), :] = dot_tn(act_s[:, cut(part)], marks)

    loads[0].wait()
    work = [functools.partial(first_dact, part) for part in range(parts)]
    work += [functools.partial(first_grad, part) for part in range(parts)]
    served = 0
    for done, item in enumerate(work):
        item()
        while served < len(hops) and (served + 1) * len(work) <= (done + 1) * len(hops):
            hop(served).wait()
            served += 1
            if served < len(hops):
                hop(served).start()
    for t in range(2):
        for b in range(places):
            pool_s[t, b * rows : (b + 1) * rows, :] = every_s[t, b]
    loss, dpooled = contrast_kernel((pool_s[0], pool_s[1]), doc_groups[...], positives[...])
    loss_out[...] = loss
    chosen = jnp.where(tower == 0, dpooled[0], dpooled[1])
    ids = lax.broadcasted_iota(jnp.int32, (chosen.shape[0], 1), 0)
    spread = [
        jnp.sum(jnp.where(ids == batch * rows + row, chosen, 0.0), 0, keepdims=True) / lengths[row].astype(FULL)
        for row in range(rows)
    ]
    for row in range(rows):
        spread_out[row : row + 1, :] = spread[row]
    stacked = jnp.concatenate(spread, 0)
    upper = stacked.astype(LOW)
    lower = (stacked - upper.astype(FULL)).astype(LOW)
    stacked = jnp.concatenate([upper, lower, jnp.zeros((16 - 2 * rows, width), LOW)], 0)
    stores = []

    def store(source, target):
        copy = pltpu.make_async_copy(source, target, out_sem.at[len(stores)])
        copy.start()
        stores.append(copy)

    loads[1 + 2 * parts].wait()
    for part in range(parts):
        shift = dot_nt(stacked, wo_s[cut(part), :])
        loads[2 + 2 * parts + part].wait()
        for row in range(rows):
            extra = shift[row : row + 1] + shift[rows + row : rows + row + 1]

            def body(i, row=row, extra=extra, part=part):
                at = rows_of(i + row * (seq // 128), 128)
                inside = rows_of(i, 128)
                present = lax.broadcasted_iota(jnp.int32, (128, 1), 0) + i * 128 < lengths[row]
                dact = dact_s[at, cut(part)] + jnp.where(present, extra, 0.0)
                slope_s[at, cut(part)] = (slope_s[at, cut(part)].astype(FULL) * dact).astype(LOW)

            loop(seq // 128, body)
        wi_grad_s[:, cut(part)] = dot_tn(n2_s[...], slope_s[:, cut(part)])
        store(wi_grad_s.at[:, cut(part)], wi_grad.at[:, cut(part)])
        store(slope_s.at[:, cut(part)], dinner.at[:, cut(part)])

        def correct(i, part=part):
            at = pl.ds(pl.multiple_of(part * width + i * 128, 128), 128)
            more = wo_grad_s[at, :]
            sums = mass_s[at, :]
            for row in range(rows):
                more = more + sums[:, row : row + 1] * spread[row]
            wo_grad_s[at, :] = more

        loop(width // 128, correct)
        store(wo_grad_s.at[cut(part), :], wo_grad.at[cut(part), :])
    for copy in stores:
        copy.wait()


def middle(sizes, cot, pooled, lengths, doc_groups, positives, act, slope, wo, n2):
    count, width = cot.shape
    hidden = wo.shape[0]
    rows = lengths.shape[0]
    names = bit_names(sizes)
    parts = hidden // width
    total = doc_groups.shape[0]
    shape = jax.ShapeDtypeStruct
    any_spec = pl.BlockSpec(memory_space=pl.ANY)
    vmem_spec = pl.BlockSpec(memory_space=pltpu.VMEM)
    smem_spec = pl.BlockSpec(memory_space=pltpu.SMEM)
    narrow_s = pltpu.VMEM((count, width), LOW)
    wide_s = pltpu.VMEM((count, hidden), LOW)
    return pl.pallas_call(
        functools.partial(middle_kernel, sizes, names),
        out_shape=[
            shape((hidden, width), FULL),
            shape((width, hidden), FULL),
            shape((count, hidden), LOW),
            shape((rows, width), FULL),
            shape((1, 1), FULL),
        ],
        in_specs=[any_spec, vmem_spec, smem_spec, vmem_spec, vmem_spec] + [any_spec] * 4,
        out_specs=[any_spec] * 3 + [vmem_spec] * 2,
        scratch_shapes=[
            narrow_s,
            wide_s,
            wide_s,
            pltpu.VMEM((hidden, width), LOW),
            narrow_s,
            pltpu.VMEM((count, hidden), FULL),
            pltpu.VMEM((hidden, width), FULL),
            pltpu.VMEM((width, hidden), FULL),
            pltpu.VMEM((hidden, 128), FULL),
            pltpu.VMEM((2, sizes["batch"], rows, width), FULL),
            pltpu.VMEM((2, total, width), FULL),
            pltpu.SemaphoreType.DMA((2 + 3 * parts,)),
            pltpu.SemaphoreType.DMA((3 * parts,)),
            pltpu.SemaphoreType.DMA((len(names),)),
            pltpu.SemaphoreType.DMA((len(names),)),
        ],
        compiler_params=pltpu.CompilerParams(
            collective_id=1, has_side_effects=True, vmem_limit_bytes=63 * 2**20
        ),
    )(cot, pooled, lengths, doc_groups.reshape(1, total), positives.reshape(total, 1), act, slope, wo, n2)


def norm_back(values, gain, dy):
    scale = lax.rsqrt(jnp.mean(values * values, -1, keepdims=True) + EPSILON)
    along = values * scale
    dscaled = gain * dy
    mean = jnp.mean(along * dscaled, -1, keepdims=True)
    return scale * (dscaled - along * mean), jnp.sum(along * dy, 0, keepdims=True)


def backward_kernel(
    cot, spread, lengths, dinner, wi, h1, ho, q, k, v, n1, tokens, lse, bias, wq, wk, wv, wm, gain1, gain2, table,
    wq_grad, wk_grad, wv_grad, wm_grad, tokens_grad, small_out,
    cot_s, h1_s, sum_s, ho_s, q_s, k_s, v_s, n1_s, x_s, dh_s, dq_s, dk_s, dv_s, wq_s, wk_s, wv_s, wm_s,
    score_s, dprob_s, prob_s, dscore_s, near_s, stage_s, in_sem, out_sem, chunk_sem,
):
    count, width = cot_s.shape
    rows = lengths.shape[0]
    seq = count // rows
    heads = table.shape[1]
    size = width // heads
    parts = wi.shape[1] // width
    block = 256
    loads = {}

    def load(name, source, target):
        copy = pltpu.make_async_copy(source, target, in_sem.at[len(loads)])
        copy.start()
        loads[name] = copy

    def chunk(part):
        turn = part % 2
        return (
            pltpu.make_async_copy(
                dinner.at[:, pl.ds(part * width, width)], (dq_s, dk_s)[turn], chunk_sem.at[0, part]
            ),
            pltpu.make_async_copy(
                wi.at[:, pl.ds(part * width, width)], (dv_s, dh_s)[turn].at[pl.ds(0, width), :], chunk_sem.at[1, part]
            ),
        )

    for part in range(2):
        for copy in chunk(part):
            copy.start()
    load("h1", h1, h1_s)
    load("cot", cot, cot_s)
    load("wm", wm, wm_s)
    load("ho", ho, ho_s)
    for name, source, target in (
        ("q", q, q_s), ("k", k, k_s), ("v", v, v_s), ("n1", n1, n1_s),
        ("wq", wq, wq_s), ("wk", wk, wk_s), ("wv", wv, wv_s), ("x", tokens, x_s),
    ):
        load(name, source, target)
    stores = []

    def store(source, target):
        copy = pltpu.make_async_copy(source, target, out_sem.at[len(stores)])
        copy.start()
        stores.append(copy)

    small_out[...] = jnp.zeros_like(small_out)
    near_s[...] = jnp.zeros_like(near_s)

    for part in range(parts):
        for copy in chunk(part):
            copy.wait()
        left, right = (dq_s, dk_s)[part % 2], (dv_s, dh_s)[part % 2]

        def add_dn2(i, part=part, left=left, right=right):
            at = rows_of(i, block)
            more = dot_nt(left[at, :], right[0:width, :])
            sum_s[at, :] = more if part == 0 else sum_s[at, :] + more

        loop(count // block, add_dn2)
        if part + 2 < parts:
            for copy in chunk(part + 2):
                copy.start()
    loads["h1"].wait()
    loads["cot"].wait()
    loads["wm"].wait()

    def mix_back(i):
        at = rows_of(i, block)
        row = lax.div(i, jnp.int32(seq // block))
        slot = lax.broadcasted_iota(jnp.int32, (block, 1), 0) + lax.rem(i, jnp.int32(seq // block)) * block
        extra = spread[0:1, :]
        for other in range(1, rows):
            extra = jnp.where(row == other, spread[other : other + 1, :], extra)
        dout = cot_s[at, :].astype(FULL) + jnp.where(slot < lengths[row], extra, 0.0)
        dv, dgain = norm_back(h1_s[at, :], gain2[...], sum_s[at, :])
        dh1 = dout + dv
        h1_s[at, :] = dh1
        small_out[1:2, :] = small_out[1:2, :] + dgain
        da = dh1.astype(LOW)
        cot_s[at, :] = da
        dh_s[at, :] = dot_nt(da, wm_s[...]).astype(LOW)

    loop(count // block, mix_back)
    loads["ho"].wait()
    stage_s[0] = dot_tn(ho_s[...], cot_s[...])
    store(stage_s.at[0], wm_grad)

    for name in ("q", "k", "v"):
        loads[name].wait()
    blocks = seq // 128
    lanes = lax.broadcasted_iota(jnp.int32, (seq, 2 * size), 1)
    keys = lax.broadcasted_iota(jnp.int32, (128, seq), 0)

    def attend_back(step):
        row = lax.div(step, jnp.int32(heads // 2))
        pair = lax.rem(step, jnp.int32(heads // 2))
        at = rows_of(row, seq)
        here = rows_of(pair, 2 * size)
        limit = lengths[row]
        qp, kp, vp, dp = q_s[at, here], k_s[at, here], v_s[at, here], dh_s[at, here]
        nothing = jnp.zeros_like(qp)
        kt = kp.T
        dq, dk, dv = [], [], []
        for side in range(2):
            chosen = (lanes >= size) == (side == 1)
            score_s[side] = dot_nt(kp, jnp.where(chosen, qp, nothing))
            dprob_s[side] = dot_nt(vp, jnp.where(chosen, dp, nothing))
        for side in range(2):
            head = pair * 2 + side
            level = lse[row * heads + head]
            delta = jnp.zeros((1, seq), FULL)
            for jb in range(blocks):
                here_rows = slice(jb * 128, (jb + 1) * 128)
                strip = score_s[side, here_rows, :] + bias_strip(bias, table, head, jb, blocks)
                strip = jnp.where(keys + jb * 128 < limit, strip, NEGATIVE)
                prob = jnp.exp(strip - level)
                prob_s[side, here_rows, :] = prob.astype(LOW)
                score_s[side, here_rows, :] = prob
                delta = delta + jnp.sum(prob * dprob_s[side, here_rows, :], 0, keepdims=True)
            for jb in range(blocks):
                here_rows = slice(jb * 128, (jb + 1) * 128)
                prob = score_s[side, here_rows, :]
                dscore = prob * (dprob_s[side, here_rows, :] - delta)
                dscore_s[side, here_rows, :] = dscore.astype(LOW)
                for ib in range(blocks):
                    place = min(max(jb - ib, -2), 2) + 2
                    near_s[head, place] = near_s[head, place] + dscore[:, ib * 128 : (ib + 1) * 128]
            dk.append(dot_nn(dscore_s[side], qp))
            dv.append(dot_nn(prob_s[side], dp))
            dq.append(dot_nn(kt[side * size : (side + 1) * size, :], dscore_s[side]))
        first = lanes < size
        dk_s[at, here] = jnp.where(first, dk[0], dk[1]).astype(LOW)
        dv_s[at, here] = jnp.where(first, dv[0], dv[1]).astype(LOW)
        dq_s[at, here] = jnp.concatenate(dq, 0).T.astype(LOW)

    loop(rows * (heads // 2), attend_back)

    ids = [offset_buckets(shift) for shift, _ in NEAR]

    def bucket_sums(head):
        row_id = lax.broadcasted_iota(jnp.int32, (1, 128), 1)
        found = jnp.zeros((1, 128), FULL)
        for place, (shift, members) in enumerate(NEAR):
            block_sum = near_s[head, place + 1]
            for b in members:
                part = jnp.sum(jnp.where(ids[place] == b, block_sum, 0.0), 0, keepdims=True)
                found = found + jnp.where(row_id == b, jnp.sum(part, 1, keepdims=True), 0.0)
        for place, b in ((0, 15), (4, 31)):
            part = jnp.sum(near_s[head, place], 0, keepdims=True)
            found = found + jnp.where(row_id == b, jnp.sum(part, 1, keepdims=True), 0.0)
        near_s[head, 0, 0:1, :] = found

    loop(heads, bucket_sums)
    for head in range(heads):
        small_out[8 + head : 9 + head, 0:128] = near_s[head, 0, 0:1, :]

    loads["n1"].wait()
    for turn, (d_s, target) in enumerate(((dq_s, wq_grad), (dk_s, wk_grad), (dv_s, wv_grad))):
        spot = (turn + 1) % 2
        if turn >= 1:
            stores[turn - 1].wait()
        stage_s[spot] = dot_tn(n1_s[...], d_s[...])
        store(stage_s.at[spot], target)
    for name in ("wq", "wk", "wv", "x"):
        loads[name].wait()

    def input_back(i):
        at = rows_of(i, block)
        dn1 = dot_nt(dq_s[at, :], wq_s[...]) + dot_nt(dk_s[at, :], wk_s[...]) + dot_nt(dv_s[at, :], wv_s[...])
        dv, dgain = norm_back(x_s[at, :].astype(FULL), gain1[...], dn1)
        small_out[0:1, :] = small_out[0:1, :] + dgain
        cot_s[at, :] = (h1_s[at, :] + dv).astype(LOW)

    loop(count // block, input_back)
    store(cot_s, tokens_grad)
    for copy in stores[2:]:
        copy.wait()


def backward(cot, spread, lengths, dinner, wi, h1, ho, q, k, v, n1, tokens, lse, bias, wq, wk, wv, wm, gain1, gain2, table):
    count, width = cot.shape
    rows = lengths.shape[0]
    heads = table.shape[1]
    seq = count // rows
    shape = jax.ShapeDtypeStruct
    any_spec = pl.BlockSpec(memory_space=pl.ANY)
    vmem_spec = pl.BlockSpec(memory_space=pltpu.VMEM)
    smem_spec = pl.BlockSpec(memory_space=pltpu.SMEM)
    narrow_s = pltpu.VMEM((count, width), LOW)
    full_s = pltpu.VMEM((count, width), FULL)
    square = shape((width, width), FULL)
    return pl.pallas_call(
        backward_kernel,
        out_shape=[square] * 4 + [shape((count, width), LOW), shape((24, width), FULL)],
        in_specs=[any_spec, vmem_spec, smem_spec] + [any_spec] * 9 + [vmem_spec] * 2 + [any_spec] * 4 + [vmem_spec] * 2 + [smem_spec],
        out_specs=[any_spec] * 5 + [vmem_spec],
        scratch_shapes=[narrow_s, full_s, full_s]
        + [narrow_s] * 10
        + [pltpu.VMEM((width, width), LOW)] * 4
        + [
            pltpu.VMEM((2, seq, seq), FULL),
            pltpu.VMEM((2, seq, seq), FULL),
            pltpu.VMEM((2, seq, seq), LOW),
            pltpu.VMEM((2, seq, seq), LOW),
            pltpu.VMEM((heads, 5, 128, 128), FULL),
            pltpu.VMEM((2, width, width), FULL),
            pltpu.SemaphoreType.DMA((16,)),
            pltpu.SemaphoreType.DMA((8,)),
            pltpu.SemaphoreType.DMA((2, 8)),
        ],
        compiler_params=pltpu.CompilerParams(vmem_limit_bytes=62 * 2**20),
    )(cot, spread, lengths, dinner, wi, h1, ho, q, k, v, n1, tokens, lse, bias, wq, wk, wv, wm,
      gain1.reshape(1, width), gain2.reshape(1, width), table)


def gradient_units(sizes):
    orders = bit_orders(sizes)
    pattern = (0, 1, 2, 0, 1, 3)
    units = [Unit("outer%d" % i, 0, 512 * i, 512, 0, 768, orders[pattern[i]]) for i in range(6)]
    units += [Unit("inner%d" % i, 1, 0, 768, 512 * i, 512, orders[pattern[i]]) for i in range(6)]
    for i in range(8):
        units.append(Unit("proj%d" % i, 2 + i // 2, 0, 768, 384 * (i % 2), 384, orders[pattern[i % 6]]))
    return units


def sum_kernel(sizes, units, names, *refs):
    count = len(units)
    grads, small_in = refs[:6], refs[6]
    outs, small_out = refs[7:13], refs[13]
    kept, land = refs[14 : 14 + count], refs[14 + count : 14 + 2 * count]
    small_land, send_sem, recv_sem, small_send, small_recv, load_sem, store_sem = refs[14 + 2 * count :]
    place = {axis: lax.axis_index(axis) for axis in ("tower", "batch")}
    bits = [Bit(axis, mask, place) for axis, mask in names]
    exchange = Exchange(units, bits, grads, kept, land, outs, (send_sem, recv_sem, load_sem, store_sem))
    barrier = pltpu.get_barrier_semaphore()
    for bit in bits:
        pl.semaphore_signal(barrier, inc=1, device_id=bit.partner, device_id_type=MESH)
    pl.semaphore_wait(barrier, len(bits))
    for u in range(count):
        exchange.begin(u)

    def small_copy(k):
        return pltpu.make_async_remote_copy(
            src_ref=small_out,
            dst_ref=small_land.at[k],
            send_sem=small_send.at[k],
            recv_sem=small_recv.at[k],
            device_id=bits[k].partner,
            device_id_type=MESH,
        )

    small_out[...] = small_in[...]
    small_copy(0).start()
    order, _ = service_order(units, names, [0.0] * count)
    small_at = {len(order) * (k + 1) // (len(bits) + 1): k for k in range(len(bits))}
    for place_in_order, (u, s) in enumerate(order):
        if place_in_order in small_at:
            k = small_at[place_in_order]
            small_copy(k).wait()
            small_out[...] = small_out[...] + small_land[k]
            if k + 1 < len(bits):
                small_copy(k + 1).start()
        exchange.serve(u, s)


def sum_gradients(sizes, grads, small):
    units = gradient_units(sizes)
    names = bit_names(sizes)
    steps = max(len(unit.steps) for unit in units)
    any_spec = pl.BlockSpec(memory_space=pl.ANY)
    vmem_spec = pl.BlockSpec(memory_space=pltpu.VMEM)
    return pl.pallas_call(
        functools.partial(sum_kernel, sizes, units, names),
        out_shape=[jax.ShapeDtypeStruct(g.shape, g.dtype) for g in grads]
        + [jax.ShapeDtypeStruct(small.shape, small.dtype)],
        in_specs=[any_spec] * 6 + [vmem_spec],
        out_specs=[any_spec] * 6 + [vmem_spec],
        scratch_shapes=[pltpu.VMEM((unit.steps[0][2], unit.cols), jnp.float32) for unit in units]
        + [pltpu.VMEM((unit.recv_rows, unit.cols), jnp.float32) for unit in units]
        + [
            pltpu.VMEM((len(names),) + small.shape, jnp.float32),
            pltpu.SemaphoreType.DMA((len(units), steps)),
            pltpu.SemaphoreType.DMA((len(units), steps)),
            pltpu.SemaphoreType.DMA((len(names),)),
            pltpu.SemaphoreType.DMA((len(names),)),
            pltpu.SemaphoreType.DMA((len(units),)),
            pltpu.SemaphoreType.DMA((len(units),)),
        ],
        compiler_params=pltpu.CompilerParams(
            collective_id=0, has_side_effects=True, vmem_limit_bytes=62 * 2**20
        ),
    )(*grads, small)


def shards(
    tokens,
    lengths,
    doc_groups,
    positives,
    cotangent,
    w_query,
    w_key,
    w_value,
    w_mixed,
    w_inner,
    w_outer,
    gain_attn,
    gain_ffn,
    rel_table,
):
    rows = tokens.shape[1]
    count, width = rows * tokens.shape[2], tokens.shape[3]
    buckets, heads = rel_table.shape
    sizes = {axis: lax.axis_size(axis) for axis in ("tower", "batch")}
    flat = tokens.reshape(count, width)
    cot = cotangent.reshape(count, width)
    own_lengths = lengths.reshape(rows)
    q, k, v, ho, n1, n2, h1, act, slope, result, lse, bias, pooled = forward(
        flat, own_lengths, w_query, w_key, w_value, w_mixed, w_inner, w_outer, gain_attn, gain_ffn, rel_table
    )
    wo_grad, wi_grad, dinner, spread, loss = middle(
        sizes, cot, pooled, own_lengths, doc_groups, positives, act, slope, w_outer, n2
    )
    wq_grad, wk_grad, wv_grad, wm_grad, tokens_grad, small = backward(
        cot, spread, own_lengths, dinner, w_inner, h1, ho, q, k, v, n1, flat, lse, bias,
        w_query, w_key, w_value, w_mixed, gain_attn, gain_ffn, rel_table,
    )
    total = sum_gradients(sizes, [wo_grad, wi_grad, wq_grad, wk_grad, wv_grad, wm_grad], small)
    return (
        result.reshape(tokens.shape),
        pooled[None],
        loss[0, 0],
        tokens_grad.reshape(tokens.shape),
        total[2],
        total[3],
        total[4],
        total[5],
        total[1],
        total[0],
        total[6][0],
        total[6][1],
        total[6][8 : 8 + heads, :buckets].T,
    )


def solution(mesh):
    return jax.shard_map(
        shards,
        mesh=mesh,
        in_specs=(
            P("tower", "batch", None, None),
            P("tower", "batch"),
            P(),
            P(),
            P("tower", "batch", None, None),
            P(),
            P(),
            P(),
            P(),
            P(),
            P(),
            P(),
            P(),
            P(),
        ),
        out_specs=(
            P("tower", "batch", None, None),
            P("tower", "batch", None),
            P(),
            P("tower", "batch", None, None),
            P(),
            P(),
            P(),
            P(),
            P(),
            P(),
            P(),
            P(),
            P(),
        ),
        check_vma=False,
    )
```

```python
import functools

import jax
import jax.numpy as jnp
from jax import lax
from jax.experimental import pallas as pl
from jax.experimental.pallas import tpu as pltpu
from jax.sharding import PartitionSpec as P

EPSILON = 1e-06
SCALE = 50.0
NEGATIVE = -1000000000.0
THRESHOLDS = (12, 16, 23, 32, 46, 64, 91)
HIGHEST = lax.Precision.HIGHEST


MESH = pl.DeviceIdType.MESH
LINK = 45.7e3
CORE = 500e3
FLIGHT = 1.8
CLASSES = "ABCD"
PATTERN = "ABCABD"
UNIT_ROWS = 256


def bit_names(sizes):
    names = []
    for axis in ("tower", "batch"):
        mask = 1
        while mask < sizes[axis]:
            names.append((axis, mask))
            mask *= 2
    return names


def set_counts(sizes):
    return {"A": 5, "B": 5, "C": 3, "D": 3} if sizes["batch"] <= 16 else {"A": 3, "B": 3, "C": 2, "D": 2}


def bit_groups(sizes):
    names = bit_names(sizes)
    core = [(k,) for k, name in enumerate(names) if name[0] == "tower"]
    rest = [k for k, name in enumerate(names) if name[0] == "batch"]
    x, y, low, high = rest[:4]
    more = [(k,) for k in rest[4:]]
    firsts = {
        "A": [(x,), (y,), (low, high)],
        "B": [(y,), (x,), (low, high)],
        "C": [(low,), (x,), (y,), (high,)],
        "D": [(low,), (y,), (x,), (high,)],
    }
    return {name: core + groups + more for name, groups in firsts.items()}


def flips_of(group):
    return [tuple(k for i, k in enumerate(group) if choice >> i & 1) for choice in range(1, 2 ** len(group))]


def gather_groups(sizes):
    rest = [k for k, name in enumerate(bit_names(sizes)) if name[0] == "batch"]
    groups = [tuple(rest[i : i + 2]) for i in range(0, len(rest), 2)]
    return groups + [(k,) for k, name in enumerate(bit_names(sizes)) if name[0] == "tower"]


class Place:
    def __init__(self, sizes):
        self.names = bit_names(sizes)
        self.at = {axis: lax.axis_index(axis) for axis in ("tower", "batch")}
        self.bits = [
            lax.rem(lax.div(self.at[axis], jnp.int32(mask)), jnp.int32(2)) for axis, mask in self.names
        ]

    def partner(self, flips):
        other = dict(self.at)
        for k in flips:
            axis, mask = self.names[k]
            other[axis] = other[axis] + mask * (1 - 2 * self.bits[k])
        return (other["tower"], other["batch"])

    def code(self, group, flips=()):
        total = jnp.int32(0)
        for k in group:
            total = total * 2 + (1 - self.bits[k] if k in flips else self.bits[k])
        return total


class Unit:
    def __init__(self, matrix, row, col, cols, kind, groups, item):
        self.matrix, self.row, self.col, self.cols, self.kind, self.item = matrix, row, col, cols, kind, item
        self.steps = []
        size, back, land = UNIT_ROWS, [], 0
        for group in groups:
            ways = 2 ** len(group)
            if size % (8 * ways) == 0:
                size //= ways
                self.steps.append(("cut", group, size, land))
                back.append(("join", group, size, 0))
                land += size * (ways - 1)
            else:
                for k in group:
                    self.steps.append(("whole", (k,), size, land))
                    land += size
        self.land = land
        self.returns = len(self.steps)
        self.steps += back[::-1]

    def place_at(self, place):
        start, stack = jnp.int32(self.row), []
        self.starts = []
        for kind, group, size, _ in self.steps:
            self.starts.append(start)
            if kind == "cut":
                stack.append(start)
                start = start + place.code(group) * size
            elif kind == "join":
                start = stack.pop()


def link_use(names, group, size):
    link = size / LINK
    masks = [names[k] for k in group]
    if masks[0][0] == "tower":
        return {"core": size / CORE}
    if masks == [("batch", 4)]:
        return {"end": link}
    if masks == [("batch", 8)]:
        return {"end": link, "middle": 2 * link}
    if masks == [("batch", 4), ("batch", 8)]:
        return {"end": 3 * link, "middle": 4 * link}
    return {mask: link * (2 ** len(group) - 1) for mask in masks}


def plan(units, names, counts, items, depth=4.0):
    free, clock, flight, pending = {}, 0.0, [], []
    idle = {kind: [(kind, i) for i in range(counts[kind])] for kind in CLASSES}
    done, order = 0, [[] for _ in items]
    left = list(range(len(units)))

    def use(u, s):
        _, group, size, _ = units[u].steps[s]
        return link_use(names, group, size * units[u].cols * 4)

    def pump():
        nonlocal clock
        for u in left:
            if units[u].item < done and (u, 0) not in pending:
                pending.append((u, 0))
        pending.sort()
        for u, s in list(pending):
            unit = units[u]
            if s == 0 and not idle[unit.kind]:
                continue
            if any(free.get(link, 0.0) - clock > depth for link in use(u, 1 if s == 0 else s)):
                continue
            pending.remove((u, s))
            if s == 0:
                left.remove(u)
                unit.set = idle[unit.kind].pop(0)
            clock += 0.08
            end = clock
            for link, time in use(u, s).items():
                free[link] = max(clock, free.get(link, 0.0)) + time
                end = max(end, free[link])
            flight.append((end + FLIGHT, u, s))
            order[done - 1].append(("go", u, s))

    while left or flight or pending or done < len(items):
        flight.sort()
        if flight and (flight[0][0] <= clock or done == len(items)):
            if flight[0][0] > clock and pending:
                clock = min(flight[0][0], clock + 0.5)
                pump()
                continue
            arrived, u, s = flight.pop(0)
            clock = max(clock, arrived) + 0.15
            kind, group, size, _ = units[u].steps[s]
            if kind != "join":
                clock += size * units[u].cols * 4 * (2 ** len(group) - 1) / 4e6
            order[done - 1].append(("serve", u, s))
            if s + 1 < len(units[u].steps):
                pending.append((u, s + 1))
            else:
                idle[units[u].kind].append(units[u].set)
            pump()
        elif done < len(items):
            clock += items[done]
            done += 1
            pump()
        else:
            clock += 0.5
            pump()
    return order, clock


class Exchange:
    def __init__(self, units, place, counts, grads, kept, land, outs, sems):
        self.units, self.place, self.grads, self.kept, self.land, self.outs = units, place, grads, kept, land, outs
        self.send_sem, self.recv_sem, self.load_sem, self.store_sem = sems
        self.sets = {name: i for i, name in enumerate((kind, i) for kind in CLASSES for i in range(counts[kind]))}
        for unit in units:
            unit.place_at(place)

    def part(self, refs, unit, start, rows):
        return refs[unit.matrix].at[pl.ds(pl.multiple_of(start, 8), rows), pl.ds(unit.col, unit.cols)]

    def own(self, unit, start, rows):
        ref = self.kept.at[self.sets[unit.set]]
        return ref.at[pl.ds(pl.multiple_of(start - unit.starts[1], 8), rows), :]

    def load(self, unit):
        spot = self.sets[unit.set]
        return pltpu.make_async_copy(
            self.part(self.grads, unit, unit.starts[1], unit.steps[0][2]), self.kept.at[spot], self.load_sem.at[spot]
        )

    def store(self, unit):
        spot, s = self.sets[unit.set], unit.returns
        start, rows = unit.starts[s], unit.steps[s][2]
        return pltpu.make_async_copy(
            self.own(unit, start, rows), self.part(self.outs, unit, start, rows), self.store_sem.at[spot]
        )

    def copies(self, unit, s):
        kind, group, size, land = unit.steps[s]
        spot, found = self.sets[unit.set], []
        for turn, flips in enumerate(flips_of(group)):
            start = unit.starts[s]
            if kind == "cut":
                start = start + self.place.code(group, flips) * size
            if s == 0:
                source = self.part(self.grads, unit, start, size)
            elif s <= unit.returns:
                source = self.own(unit, start, size)
            else:
                source = self.part(self.outs, unit, start, size)
            if kind == "join":
                target = self.part(self.outs, unit, start, size)
            else:
                target = self.land.at[spot, pl.ds(land + turn * size, size), :]
            found.append(
                pltpu.make_async_remote_copy(
                    src_ref=source,
                    dst_ref=target,
                    send_sem=self.send_sem.at[spot, s, turn],
                    recv_sem=self.recv_sem.at[spot, s, turn],
                    device_id=self.place.partner(flips),
                    device_id_type=MESH,
                )
            )
        return found

    def go(self, u, s):
        unit = self.units[u]
        if s == 0:
            self.load(unit).start()
        for copy in self.copies(unit, s):
            copy.start()

    def serve(self, u, s):
        unit = self.units[u]
        if s == 0:
            self.load(unit).wait()
        for copy in self.copies(unit, s):
            copy.wait()
        kind, group, size, land = unit.steps[s]
        if kind != "join":
            spot = self.sets[unit.set]
            start = unit.starts[s]
            if kind == "cut":
                start = start + self.place.code(group) * size
            kept = self.own(unit, start, size)
            total = kept[...]
            for turn in range(2 ** len(group) - 1):
                total = total + self.land[spot, land + turn * size : land + (turn + 1) * size, :]
            kept[...] = total
        if s + 1 == unit.returns:
            self.store(unit).start()
        if s == unit.returns:
            self.store(unit).wait()


LOW = jnp.bfloat16
FULL = jnp.float32


def dot_nn(left, right):
    return lax.dot_general(left, right, (((1,), (0,)), ((), ())), preferred_element_type=FULL)


def dot_nt(left, right):
    return lax.dot_general(left, right, (((1,), (1,)), ((), ())), preferred_element_type=FULL)


def dot_tn(left, right):
    return lax.dot_general(left, right, (((0,), (0,)), ((), ())), preferred_element_type=FULL)


def loop(count, body):
    def step(i, carry):
        body(i)
        return carry

    lax.fori_loop(0, count, step, 0)


def rows_of(i, size):
    return pl.ds(pl.multiple_of(i * size, size), size)


def offset_buckets(shift):
    keys = lax.broadcasted_iota(jnp.int32, (128, 128), 0)
    queries = lax.broadcasted_iota(jnp.int32, (128, 128), 1)
    offsets = keys - queries + 128 * shift
    distance = jnp.abs(offsets)
    distant = jnp.full((128, 128), 8, jnp.int32)
    for limit in THRESHOLDS:
        distant = distant + jnp.where(distance >= limit, 1, 0)
    buckets = jnp.where(distance < 8, distance, distant)
    return buckets + jnp.where(offsets > 0, 16, 0)


NEAR = ((-1, range(1, 16)), (0, range(32)), (1, range(17, 32)))


def fill_bias(bias, table, head, count):
    ids = [offset_buckets(shift) for shift, _ in NEAR]
    for side in range(count):
        for spot, (shift, members) in enumerate(NEAR):
            block = jnp.zeros((128, 128), FULL)
            for b in members:
                block = jnp.where(ids[spot] == b, table[head + side, b], block)
            bias[side, spot] = block


def bias_strip(bias, side, table, head, jb, blocks):
    parts = []
    for ib in range(blocks):
        shift = jb - ib
        if abs(shift) <= 1:
            parts.append(bias[side, shift + 1])
        else:
            parts.append(jnp.full((128, 128), table[head, 31 if shift > 0 else 15], FULL))
    return jnp.concatenate(parts, axis=1)


def forward_kernel(
    tokens, lengths, wq, wk, wv, wm, wi, wo, gain1, gain2, table,
    q_out, k_out, v_out, ho_out, n1_out, n2_out, h1_out, act_out, slope_out, result_out, lse_out, pooled_out,
    x_s, wq_s, wk_s, wv_s, wm_s, wi_s, wo_s, q_s, k_s, v_s, ho_s, n1_s, n2_s, h1_s, act_s, slope_s, result_s, total_s,
    score_s, prob_s, bias_s, in_sem, out_sem,
):
    count, width = tokens.shape
    rows, seq = lengths.shape[0], tokens.shape[0] // lengths.shape[0]
    heads = table.shape[0]
    size = width // heads
    hidden = wi.shape[1]
    parts = hidden // width
    loads = [
        pltpu.make_async_copy(source, target, in_sem.at[i])
        for i, (source, target) in enumerate(
            [(tokens, x_s), (wq, wq_s), (wk, wk_s), (wv, wv_s), (wm, wm_s), (wi, wi_s), (wo, wo_s)]
        )
    ]
    for load in loads:
        load.start()
    stores = []

    def store(source, target):
        copy = pltpu.make_async_copy(source, target, out_sem.at[len(stores)])
        copy.start()
        stores.append(copy)

    block = 256
    loads[0].wait()

    def norm1(i):
        at = rows_of(i, block)
        x = x_s[at, :].astype(FULL)
        scale = lax.rsqrt(jnp.mean(x * x, -1, keepdims=True) + EPSILON)
        n1_s[at, :] = (x * scale * gain1[...]).astype(LOW)

    loop(count // block, norm1)
    store(n1_s, n1_out)
    for i, (w_s, p_s, p_out) in enumerate(((wq_s, q_s, q_out), (wk_s, k_s, k_out), (wv_s, v_s, v_out))):
        loads[1 + i].wait()

        def project(m, w_s=w_s, p_s=p_s):
            at = rows_of(m, 512)
            p_s[at, :] = dot_nn(n1_s[at, :], w_s[...]).astype(LOW)

        loop(count // 512, project)
        store(p_s, p_out)
    blocks = seq // 128
    lanes = lax.broadcasted_iota(jnp.int32, (seq, 2 * size), 1)
    keys = lax.broadcasted_iota(jnp.int32, (128, seq), 0)

    def attend(step):
        pair = lax.div(step, jnp.int32(rows))
        row = lax.rem(step, jnp.int32(rows))
        at = rows_of(row, seq)
        here = rows_of(pair, 2 * size)
        limit = lengths[row]

        @pl.when(row == 0)
        def _():
            fill_bias(bias_s, table, pair * 2, 2)

        q, k = q_s[at, here], k_s[at, here]
        vt = v_s[at, here].T
        found = []
        for side in range(2):
            head = pair * 2 + side
            chosen = jnp.where((lanes >= size) == (side == 1), q, jnp.zeros_like(q))
            score_s[side] = dot_nt(k, chosen)
        for side in range(2):
            head = pair * 2 + side
            top = jnp.full((1, seq), NEGATIVE, FULL)
            for jb in range(blocks):
                strip = score_s[side, jb * 128 : (jb + 1) * 128, :] + bias_strip(bias_s, side, table, head, jb, blocks)
                strip = jnp.where(keys + jb * 128 < limit, strip, NEGATIVE)
                score_s[side, jb * 128 : (jb + 1) * 128, :] = strip
                top = jnp.maximum(top, jnp.max(strip, 0, keepdims=True))
            mass = jnp.zeros((1, seq), FULL)
            for jb in range(blocks):
                strip = jnp.exp(score_s[side, jb * 128 : (jb + 1) * 128, :] - top)
                mass = mass + jnp.sum(strip, 0, keepdims=True)
                prob_s[side, jb * 128 : (jb + 1) * 128, :] = strip.astype(LOW)
            lse_out[row * heads + head] = top + jnp.log(mass)
            found.append(dot_nn(vt[side * size : (side + 1) * size, :], prob_s[side]) / mass)
        ho_s[at, here] = jnp.concatenate(found, 0).T.astype(LOW)

    loop(rows * (heads // 2), attend)
    store(ho_s, ho_out)
    loads[4].wait()

    def mix(i):
        at = rows_of(i, block)
        h1 = x_s[at, :].astype(FULL) + dot_nn(ho_s[at, :], wm_s[...])
        h1_s[at, :] = h1
        scale = lax.rsqrt(jnp.mean(h1 * h1, -1, keepdims=True) + EPSILON)
        n2_s[at, :] = (h1 * scale * gain2[...]).astype(LOW)

    loop(count // block, mix)
    store(h1_s, h1_out)
    store(n2_s, n2_out)
    loads[5].wait()
    loads[6].wait()

    for part in range(parts):
        columns = pl.ds(part * width, width)

        def feed(i, part=part, columns=columns):
            at = rows_of(i, block)
            inner = dot_nn(n2_s[at, :], wi_s[:, columns])
            share = 0.5 + 0.5 * lax.erf(inner * 0.7071067811865476)
            act = (inner * share).astype(LOW)
            act_s[at, columns] = act
            slope = share + inner * (jnp.exp(inner * inner * -0.5) * 0.3989422804014327)
            slope_s[at, columns] = slope.astype(LOW)
            more = dot_nn(act, wo_s[columns, :])
            if part == 0:
                total_s[at, :] = h1_s[at, :] + more
            elif part < parts - 1:
                total_s[at, :] = total_s[at, :] + more
            else:
                output = total_s[at, :] + more
                total_s[at, :] = output
                result_s[at, :] = output.astype(LOW)

        loop(count // block, feed)
        store(act_s.at[:, columns], act_out.at[:, columns])
        store(slope_s.at[:, columns], slope_out.at[:, columns])
    store(result_s, result_out)
    slots = lax.broadcasted_iota(jnp.int32, (seq, 1), 0)
    for row in range(rows):
        kept = jnp.where(slots < lengths[row], total_s[row * seq : (row + 1) * seq, :], 0.0)
        pooled_out[row : row + 1, :] = jnp.sum(kept, 0, keepdims=True) / lengths[row].astype(FULL)
    for copy in stores:
        copy.wait()


def forward(tokens, lengths, wq, wk, wv, wm, wi, wo, gain1, gain2, table):
    count, width = tokens.shape
    hidden = wi.shape[1]
    rows = lengths.shape[0]
    heads = table.shape[0]
    seq = count // rows
    shape = jax.ShapeDtypeStruct
    any_spec = pl.BlockSpec(memory_space=pl.ANY)
    vmem_spec = pl.BlockSpec(memory_space=pltpu.VMEM)
    smem_spec = pl.BlockSpec(memory_space=pltpu.SMEM)
    low = shape((count, width), LOW)
    wide = shape((count, hidden), LOW)
    weights = [pltpu.VMEM(w.shape, LOW) for w in (wq, wk, wv, wm, wi, wo)]
    narrow_s = pltpu.VMEM((count, width), LOW)
    full_s = pltpu.VMEM((count, width), FULL)
    wide_s = pltpu.VMEM((count, hidden), LOW)
    return pl.pallas_call(
        forward_kernel,
        out_shape=[low, low, low, low, low, low, shape((count, width), FULL), wide, wide, low]
        + [shape((rows * heads, 1, seq), FULL), shape((rows, width), FULL)],
        in_specs=[any_spec, smem_spec] + [any_spec] * 6 + [vmem_spec] * 2 + [smem_spec],
        out_specs=[any_spec] * 10 + [vmem_spec] * 2,
        scratch_shapes=[narrow_s]
        + weights
        + [narrow_s] * 6
        + [full_s, wide_s, wide_s, narrow_s, full_s]
        + [
            pltpu.VMEM((2, seq, seq), FULL),
            pltpu.VMEM((2, seq, seq), LOW),
            pltpu.VMEM((2, 3, 128, 128), FULL),
            pltpu.SemaphoreType.DMA((7,)),
            pltpu.SemaphoreType.DMA((24,)),
        ],
        compiler_params=pltpu.CompilerParams(vmem_limit_bytes=62 * 2**20),
    )(tokens, lengths, wq, wk, wv, wm, wi, wo, gain1.reshape(1, width), gain2.reshape(1, width), table)


def norm_back(values, gain, dy):
    scale = lax.rsqrt(jnp.mean(values * values, -1, keepdims=True) + EPSILON)
    along = values * scale
    dscaled = gain * dy
    mean = jnp.mean(along * dscaled, -1, keepdims=True)
    return scale * (dscaled - along * mean), jnp.sum(along * dy, 0, keepdims=True)


def contrast(queries, documents, doc_groups, positives):
    count = doc_groups.shape[1]
    precise = functools.partial(lax.dot_general, precision=HIGHEST, preferred_element_type=FULL)
    rates = [lax.rsqrt(jnp.sum(p * p, -1, keepdims=True) + EPSILON) for p in (queries, documents)]
    unit = [p * rate for p, rate in zip((queries, documents), rates)]
    scores = SCALE * precise(unit[0], unit[1], (((1,), (1,)), ((), ())))
    indices = lax.broadcasted_iota(jnp.int32, (count, count), 0)
    chosen = jnp.where(positives == indices, 1.0, 0.0).T
    query_groups = jnp.sum(chosen * doc_groups.astype(FULL), 1, keepdims=True)
    masked = jnp.where(query_groups == doc_groups.astype(FULL), scores, NEGATIVE)
    highest = jnp.max(masked, 1, keepdims=True)
    weights = jnp.exp(masked - highest)
    mass = jnp.sum(weights, 1, keepdims=True)
    matched = jnp.sum(jnp.where(chosen > 0.5, scores, 0.0), 1, keepdims=True)
    loss = jnp.sum(highest + jnp.log(mass) - matched, 0, keepdims=True) / count
    dscore = weights / mass - chosen
    dunit = (
        SCALE * precise(dscore, unit[1], (((1,), (0,)), ((), ()))),
        SCALE * precise(dscore, unit[0], (((0,), (0,)), ((), ()))),
    )
    dpooled = [rate * (d - u * jnp.sum(u * d, -1, keepdims=True)) for rate, d, u in zip(rates, dunit, unit)]
    return loss, dpooled


def make_units(sizes, hidden, width):
    groups = bit_groups(sizes)
    parts, thirds = hidden // width, width // UNIT_ROWS
    items = [("gather", 12.0), ("loss", 3.0)]
    blocks = []
    for part in range(parts):
        items.append(("outer", 1.9))
        blocks += [(0, part * width + i * UNIT_ROWS, 0, len(items)) for i in range(thirds)]
    for part in range(parts):
        items.append(("inner", 6.2))
        blocks += [(1, i * UNIT_ROWS, part * width, len(items)) for i in range(thirds)]
    items += [("mix", 3.5), ("mixed", 1.8)]
    blocks += [(5, i * UNIT_ROWS, 0, len(items)) for i in range(thirds)]
    items += [("attend", 2.4)] * 24
    for matrix in range(2, 5):
        items.append(("projection", 1.8))
        blocks += [(matrix, i * UNIT_ROWS, 0, len(items)) for i in range(thirds)]
    items.append(("input", 6.0))
    units = []
    for i, (matrix, row, col, item) in enumerate(blocks):
        kind = PATTERN[i % len(PATTERN)]
        units.append(Unit(matrix, row, col, width, kind, groups[kind], item))
    return units, items


def backward_kernel(
    sizes, units, order, counts,
    cot, pooled, lengths, doc_groups, positives, act, slope, wo, wi, n2, h1, ho, q, k, v, n1, tokens, lse,
    wq, wk, wv, wm, gain1, gain2, table,
    *refs,
):
    grads, outs = refs[:6], refs[6:12]
    tokens_grad, small_out, loss_out = refs[12:15]
    (
        narrow, square, staged, full, bias_s, near_s, sums_s, every_s, small_land, kept, land,
        in_sem, chunk_sem, stage_sem, last_sem, hop_send, hop_recv, small_send, small_recv,
        send_sem, recv_sem, load_sem, store_sem,
    ) = refs[15:]
    count, width = narrow.shape[1:]
    rows = lengths.shape[0]
    seq = count // rows
    heads = table.shape[0]
    size = width // heads
    parts = wo.shape[0] // width
    block = 256
    place = Place(sizes)
    names = place.names
    tower, batch = place.at["tower"], place.at["batch"]
    exchange = Exchange(units, place, counts, grads, kept, land, outs, (send_sem, recv_sem, load_sem, store_sem))
    cot_s, n2_s, dout_s = narrow.at[8], narrow.at[9], narrow.at[10]
    act_s = [narrow.at[part] for part in range(parts)]
    slope_s = [narrow.at[parts + part] for part in range(parts)]
    h1_s, sum_s = full.at[0], full.at[1]
    loads = {}

    def load(name, source, target):
        copy = pltpu.make_async_copy(source, target, in_sem.at[len(loads)])
        copy.start()
        loads[name] = copy

    def cut(part):
        return pl.ds(part * width, width)

    load("cot", cot, cot_s)
    for part in range(parts):
        load("act%d" % part, act.at[:, cut(part)], act_s[part])
    for part in range(parts):
        load("wo%d" % part, wo.at[cut(part), :], square.at[part])
    load("n2", n2, n2_s)
    for part in range(parts):
        load("slope%d" % part, slope.at[:, cut(part)], slope_s[part])

    def wi_chunk(part):
        return pltpu.make_async_copy(wi.at[:, cut(part)], square.at[parts + part % 2], chunk_sem.at[part])

    for part in range(2):
        wi_chunk(part).start()
    load("h1", h1, h1_s)

    item = 0
    stage_of = {}

    def act_on(actions):
        for action, u, s in actions:
            if action == "go":
                if s == 0:
                    exchange_ready(u)
                exchange.go(u, s)
            else:
                exchange.serve(u, s)

    def exchange_ready(u):
        unit = units[u]
        key = (unit.matrix, unit.row // width if unit.matrix == 0 else unit.col // width)
        if key in stage_of:
            stage_of.pop(key).wait()

    def between():
        nonlocal item
        act_on(order[item])
        item += 1

    staged_count = 0
    staged_last = {}

    def stage(value, matrix, part, target):
        nonlocal staged_count
        spot = staged_count % 3
        if spot in staged_last and staged_last[spot] in stage_of:
            stage_of.pop(staged_last[spot]).wait()
        staged[spot] = value
        copy = pltpu.make_async_copy(staged.at[spot], target, stage_sem.at[staged_count])
        copy.start()
        stage_of[(matrix, part)] = copy
        staged_last[spot] = (matrix, part)
        staged_count += 1

    hops = gather_groups(sizes)
    every_s[tower, batch] = pooled[...]
    deltas = set()
    for group in list(bit_groups(sizes).values()) + [hops]:
        for bits in group:
            deltas.update(flips_of(bits))
    barrier = pltpu.get_barrier_semaphore()
    for flips in sorted(deltas):
        pl.semaphore_signal(barrier, inc=1, device_id=place.partner(flips), device_id_type=MESH)
    pl.semaphore_wait(barrier, len(deltas))
    for h, group in enumerate(hops):
        masks = [names[bit] for bit in group]
        if masks[0][0] == "tower":
            held = every_s.at[tower]
        else:
            mask = masks[0][1]
            held = every_s.at[tower, pl.ds(lax.div(batch, jnp.int32(mask)) * mask, mask)]
        copies = [
            pltpu.make_async_remote_copy(
                src_ref=held,
                dst_ref=held,
                send_sem=hop_send.at[h, turn],
                recv_sem=hop_recv.at[h, turn],
                device_id=place.partner(flips),
                device_id_type=MESH,
            )
            for turn, flips in enumerate(flips_of(group))
        ]
        for copy in copies:
            copy.start()
        for copy in copies:
            copy.wait()
    between()

    for t in range(2):
        for b in range(sizes["batch"]):
            staged[t, b * rows : (b + 1) * rows, :] = every_s[t, b]
    total = rows * sizes["batch"]
    loss, dpooled = contrast(staged[0, 0:total, :], staged[1, 0:total, :], doc_groups[...], positives[...])
    loss_out[...] = loss
    mine = jnp.where(tower == 0, dpooled[0], dpooled[1])
    ids = lax.broadcasted_iota(jnp.int32, (mine.shape[0], 1), 0)
    spread = [
        jnp.sum(jnp.where(ids == batch * rows + row, mine, 0.0), 0, keepdims=True) / lengths[row].astype(FULL)
        for row in range(rows)
    ]
    loads["cot"].wait()

    def full_dout(row, i):
        at = pl.ds(pl.multiple_of(row * seq + i * block, block), block)
        slot = lax.broadcasted_iota(jnp.int32, (block, 1), 0) + i * block
        return at, cot_s[at, :].astype(FULL) + jnp.where(slot < lengths[row], spread[row], 0.0)

    for row in range(rows):

        def round_dout(i, row=row):
            at, dout = full_dout(row, i)
            dout_s[at, :] = dout.astype(LOW)

        loop(seq // block, round_dout)
    between()

    for part in range(parts):
        loads["act%d" % part].wait()
        stage(dot_tn(act_s[part][...], dout_s[...]), 0, part, grads[0].at[cut(part), :])
        between()
    for name, source, target in (("q", q, 0), ("k", k, 1), ("v", v, 2), ("n1", n1, 3)):
        load(name, source, narrow.at[target])
    loads["n2"].wait()
    for part in range(parts):
        loads["slope%d" % part].wait()
        loads["wo%d" % part].wait()
        wi_chunk(part).wait()

        def inner_back(i, part=part):
            at = rows_of(i, block)
            dact = dot_nt(dout_s[at, :], square[part])
            dinner = (slope_s[part][at, :].astype(FULL) * dact).astype(LOW)
            slope_s[part][at, :] = dinner
            more = dot_nt(dinner, square[parts + part % 2])
            sum_s[at, :] = more if part == 0 else sum_s[at, :] + more

        loop(count // block, inner_back)
        if part + 2 < parts:
            wi_chunk(part + 2).start()
        stage(dot_tn(n2_s[...], slope_s[part][...]), 1, part, grads[1].at[:, cut(part)])
        between()
    load("ho", ho, narrow.at[9])
    for name, source, target in (("wm", wm, 0), ("wq", wq, 1), ("wk", wk, 2), ("wv", wv, 3)):
        load(name, source, square.at[target])
    small_out[...] = jnp.zeros_like(small_out)
    loads["h1"].wait()
    loads["wm"].wait()
    q_s, k_s, v_s, n1_s = (narrow.at[i] for i in range(4))
    dh_s, dq_s, dk_s, dv_s = (narrow.at[i] for i in range(4, 8))

    for row in range(rows):

        def mix_back(i, row=row):
            at, dout = full_dout(row, i)
            dv, dgain = norm_back(h1_s[at, :], gain2[...], sum_s[at, :])
            dh1 = dout + dv
            h1_s[at, :] = dh1
            small_out[1:2, :] = small_out[1:2, :] + dgain
            da = dh1.astype(LOW)
            cot_s[at, :] = da
            dh_s[at, :] = dot_nt(da, square[0]).astype(LOW)

        loop(seq // block, mix_back)
    between()
    loads["ho"].wait()
    stage(dot_tn(narrow[9], cot_s[...]), 5, 0, grads[5])
    between()
    for copy in list(stage_of.values()):
        copy.wait()
    stage_of.clear()
    load("x", tokens, narrow.at[9])
    for name in ("q", "k", "v"):
        loads[name].wait()

    blocks = seq // 128
    lanes = lax.broadcasted_iota(jnp.int32, (seq, 2 * size), 1)
    keys = lax.broadcasted_iota(jnp.int32, (128, seq), 0)
    first_item = item
    steps = rows * (heads // 2)

    def between_at(step, side):
        for index in range(steps):
            actions = order[first_item + 2 * index + side] if 2 * index + side < 24 else []
            if actions:
                pl.when(step == index)(functools.partial(act_on, actions))

    def attend_back(step):
        pair = lax.div(step, jnp.int32(rows))
        row = lax.rem(step, jnp.int32(rows))
        at = rows_of(row, seq)
        here = rows_of(pair, 2 * size)
        limit = lengths[row]

        @pl.when(row == 0)
        def _():
            near_s[...] = jnp.zeros_like(near_s)
            fill_bias(bias_s, table, pair * 2, 2)

        qp, kp, vp, dp = q_s[at, here], k_s[at, here], v_s[at, here], dh_s[at, here]
        nothing = jnp.zeros_like(qp)
        kt = kp.T
        dq, dk, dv = [], [], []
        score_s = [staged.at[side, 0:seq, 0:seq] for side in range(2)]
        dprob_s = [staged.at[2 + side, 0:seq, 0:seq] for side in range(2)]
        prob_s = [narrow.at[8, side * seq : (side + 1) * seq, 0:seq] for side in range(2)]
        dscore_s = [narrow.at[10, side * seq : (side + 1) * seq, 0:seq] for side in range(2)]
        for side in range(2):
            chosen = (lanes >= size) == (side == 1)
            score_s[side][...] = dot_nt(kp, jnp.where(chosen, qp, nothing))
            dprob_s[side][...] = dot_nt(vp, jnp.where(chosen, dp, nothing))
        for side in range(2):
            head = pair * 2 + side
            level = lse[row * heads + head]
            delta = jnp.zeros((1, seq), FULL)
            for jb in range(blocks):
                some = slice(jb * 128, (jb + 1) * 128)
                strip = score_s[side][some, :] + bias_strip(bias_s, side, table, head, jb, blocks)
                strip = jnp.where(keys + jb * 128 < limit, strip, NEGATIVE)
                prob = jnp.exp(strip - level)
                prob_s[side][some, :] = prob.astype(LOW)
                score_s[side][some, :] = prob
                delta = delta + jnp.sum(prob * dprob_s[side][some, :], 0, keepdims=True)
            for jb in range(blocks):
                some = slice(jb * 128, (jb + 1) * 128)
                dscore = score_s[side][some, :] * (dprob_s[side][some, :] - delta)
                dscore_s[side][some, :] = dscore.astype(LOW)
                for ib in range(blocks):
                    spot = min(max(jb - ib, -2), 2) + 2
                    near_s[side, spot] = near_s[side, spot] + dscore[:, ib * 128 : (ib + 1) * 128]
            dk.append(dot_nn(dscore_s[side][...], qp))
            dv.append(dot_nn(prob_s[side][...], dp))
            dq.append(dot_nn(kt[side * size : (side + 1) * size, :], dscore_s[side][...]))
            if side == 0:
                between_at(step, 0)
        first = lanes < size
        dk_s[at, here] = jnp.where(first, dk[0], dk[1]).astype(LOW)
        dv_s[at, here] = jnp.where(first, dv[0], dv[1]).astype(LOW)
        dq_s[at, here] = jnp.concatenate(dq, 0).T.astype(LOW)

        @pl.when(row == rows - 1)
        def _():
            ids = [offset_buckets(shift) for shift, _ in NEAR]
            for side in range(2):
                bucket = lax.broadcasted_iota(jnp.int32, (1, 128), 1)
                found = jnp.zeros((1, 128), FULL)
                for spot, (shift, members) in enumerate(NEAR):
                    total = near_s[side, spot + 1]
                    for b in members:
                        share = jnp.sum(jnp.where(ids[spot] == b, total, 0.0), 0, keepdims=True)
                        found = found + jnp.where(bucket == b, jnp.sum(share, 1, keepdims=True), 0.0)
                for spot, b in ((0, 15), (4, 31)):
                    share = jnp.sum(near_s[side, spot], 0, keepdims=True)
                    found = found + jnp.where(bucket == b, jnp.sum(share, 1, keepdims=True), 0.0)
                sums_s[pair * 2 + side] = found

        between_at(step, 1)

    loop(steps, attend_back)
    item = first_item + 24
    for head in range(heads):
        small_out[8 + head : 9 + head, 0:128] = sums_s[head]

    loads["n1"].wait()
    for matrix, d_s in ((2, dq_s), (3, dk_s), (4, dv_s)):
        stage(dot_tn(n1_s[...], d_s[...]), matrix, 0, grads[matrix])
        between()
    for name in ("wq", "wk", "wv", "x"):
        loads[name].wait()

    def input_back(i):
        at = rows_of(i, block)
        dn1 = dot_nt(dq_s[at, :], square[1]) + dot_nt(dk_s[at, :], square[2]) + dot_nt(dv_s[at, :], square[3])
        dv, dgain = norm_back(narrow[9, at, :].astype(FULL), gain1[...], dn1)
        small_out[0:1, :] = small_out[0:1, :] + dgain
        cot_s[at, :] = (h1_s[at, :] + dv).astype(LOW)

    loop(count // block, input_back)
    last = pltpu.make_async_copy(cot_s, tokens_grad, last_sem)
    last.start()

    def small_copy(bit):
        return pltpu.make_async_remote_copy(
            src_ref=small_out,
            dst_ref=small_land.at[bit],
            send_sem=small_send.at[bit],
            recv_sem=small_recv.at[bit],
            device_id=place.partner((bit,)),
            device_id_type=MESH,
        )

    small_copy(0).start()
    actions = order[item]
    for bit in range(len(names)):
        act_on(actions[len(actions) * bit // (len(names) + 1) : len(actions) * (bit + 1) // (len(names) + 1)])
        small_copy(bit).wait()
        small_out[...] = small_out[...] + small_land[bit]
        if bit + 1 < len(names):
            small_copy(bit + 1).start()
    act_on(actions[len(actions) * len(names) // (len(names) + 1) :])
    last.wait()
    for copy in stage_of.values():
        copy.wait()


def backward(
    sizes, cot, pooled, lengths, doc_groups, positives, act, slope, wo, wi, n2, h1, ho, q, k, v, n1, tokens, lse,
    wq, wk, wv, wm, gain1, gain2, table,
):
    count, width = cot.shape
    hidden = wo.shape[0]
    rows = lengths.shape[0]
    heads = table.shape[0]
    total = doc_groups.shape[0]
    names = bit_names(sizes)
    units, items = make_units(sizes, hidden, width)
    counts = set_counts(sizes)
    order, _ = plan(units, names, counts, [time for _, time in items])
    steps = max(len(unit.steps) for unit in units)
    sets = sum(counts.values())
    shape = jax.ShapeDtypeStruct
    any_spec = pl.BlockSpec(memory_space=pl.ANY)
    vmem_spec = pl.BlockSpec(memory_space=pltpu.VMEM)
    smem_spec = pl.BlockSpec(memory_space=pltpu.SMEM)
    squares = [shape((hidden, width), FULL), shape((width, hidden), FULL)] + [shape((width, width), FULL)] * 4
    hops = len(gather_groups(sizes))
    dma = pltpu.SemaphoreType.DMA
    return pl.pallas_call(
        functools.partial(backward_kernel, sizes, units, order, counts),
        out_shape=squares + squares + [shape((count, width), LOW), shape((24, width), FULL), shape((1, 1), FULL)],
        in_specs=[any_spec, vmem_spec, smem_spec, vmem_spec, vmem_spec]
        + [any_spec] * 12
        + [vmem_spec]
        + [any_spec] * 4
        + [vmem_spec] * 2
        + [smem_spec],
        out_specs=[any_spec] * 13 + [vmem_spec] * 2,
        scratch_shapes=[
            pltpu.VMEM((11, count, width), LOW),
            pltpu.VMEM((6, width, width), LOW),
            pltpu.VMEM((4, width, width), FULL),
            pltpu.VMEM((2, count, width), FULL),
            pltpu.VMEM((2, 3, 128, 128), FULL),
            pltpu.VMEM((2, 5, 128, 128), FULL),
            pltpu.VMEM((heads, 1, 128), FULL),
            pltpu.VMEM((2, sizes["batch"], rows, width), FULL),
            pltpu.VMEM((len(names), 24, width), FULL),
            pltpu.VMEM((sets, units[0].steps[0][2], width), FULL),
            pltpu.VMEM((sets, max(unit.land for unit in units), width), FULL),
            dma((32,)),
            dma((8,)),
            dma((16,)),
            dma,
            dma((hops, 3)),
            dma((hops, 3)),
            dma((len(names),)),
            dma((len(names),)),
            dma((sets, steps, 3)),
            dma((sets, steps, 3)),
            dma((sets,)),
            dma((sets,)),
        ],
        compiler_params=pltpu.CompilerParams(
            collective_id=0, has_side_effects=True, vmem_limit_bytes=int(63.5 * 2**20)
        ),
    )(
        cot, pooled, lengths, doc_groups.reshape(1, total), positives.reshape(1, total), act, slope, wo, wi, n2, h1,
        ho, q, k, v, n1, tokens, lse, wq, wk, wv, wm, gain1.reshape(1, width), gain2.reshape(1, width), table,
    )


def hand_out_kernel(count, *refs):
    sources, targets, sem = refs[:count], refs[count : 2 * count], refs[-1]
    copies = [pltpu.make_async_copy(source, target, sem.at[i]) for i, (source, target) in enumerate(zip(sources, targets))]
    for copy in copies:
        copy.start()
    for copy in copies:
        copy.wait()


def hand_out(arrays):
    any_spec = pl.BlockSpec(memory_space=pl.ANY)
    return pl.pallas_call(
        functools.partial(hand_out_kernel, len(arrays)),
        out_shape=[jax.ShapeDtypeStruct(a.shape, a.dtype) for a in arrays],
        in_specs=[any_spec] * len(arrays),
        out_specs=[any_spec] * len(arrays),
        scratch_shapes=[pltpu.SemaphoreType.DMA((len(arrays),))],
    )(*arrays)


def shards(
    tokens,
    lengths,
    doc_groups,
    positives,
    cotangent,
    w_query,
    w_key,
    w_value,
    w_mixed,
    w_inner,
    w_outer,
    gain_attn,
    gain_ffn,
    rel_table,
):
    rows = tokens.shape[1]
    count, width = rows * tokens.shape[2], tokens.shape[3]
    buckets, heads = rel_table.shape
    sizes = {axis: lax.axis_size(axis) for axis in ("tower", "batch")}
    flat = tokens.reshape(count, width)
    cot = cotangent.reshape(count, width)
    own_lengths = lengths.reshape(rows)
    table = rel_table.T
    q, k, v, ho, n1, n2, h1, act, slope, result, lse, pooled = forward(
        flat, own_lengths, w_query, w_key, w_value, w_mixed, w_inner, w_outer, gain_attn, gain_ffn, table
    )
    found = backward(
        sizes, cot, pooled, own_lengths, doc_groups, positives, act, slope, w_outer, w_inner, n2, h1, ho, q, k, v, n1,
        flat, lse, w_query, w_key, w_value, w_mixed, gain_attn, gain_ffn, table,
    )
    small, loss = found[13:]
    wo_grad, wi_grad, wq_grad, wk_grad, wv_grad, wm_grad, tokens_grad = hand_out(found[6:13])
    return (
        result.reshape(tokens.shape),
        pooled[None],
        loss[0, 0],
        tokens_grad.reshape(tokens.shape),
        wq_grad,
        wk_grad,
        wv_grad,
        wm_grad,
        wi_grad,
        wo_grad,
        small[0],
        small[1],
        small[8 : 8 + heads, :buckets].T,
    )


def solution(mesh):
    return jax.shard_map(
        shards,
        mesh=mesh,
        in_specs=(
            P("tower", "batch", None, None),
            P("tower", "batch"),
            P(),
            P(),
            P("tower", "batch", None, None),
            P(),
            P(),
            P(),
            P(),
            P(),
            P(),
            P(),
            P(),
            P(),
        ),
        out_specs=(
            P("tower", "batch", None, None),
            P("tower", "batch", None),
            P(),
            P("tower", "batch", None, None),
            P(),
            P(),
            P(),
            P(),
            P(),
            P(),
            P(),
            P(),
            P(),
        ),
        check_vma=False,
    )
```

```python
import functools

import jax
import jax.numpy as jnp
from jax import lax
from jax.experimental import pallas as pl
from jax.experimental.pallas import tpu as pltpu
from jax.sharding import PartitionSpec as P

EPSILON = 1e-06
SCALE = 50.0
NEGATIVE = -1000000000.0
THRESHOLDS = (12, 16, 23, 32, 46, 64, 91)
HIGHEST = lax.Precision.HIGHEST


MESH = pl.DeviceIdType.MESH
LINK = 45.7e3
CORE = 500e3
FLIGHT = 1.8
CLASSES = "ABCD"
PATTERN = "ABCABD"
UNIT_ROWS = 256


def bit_names(sizes):
    names = []
    for axis in ("tower", "batch"):
        mask = 1
        while mask < sizes[axis]:
            names.append((axis, mask))
            mask *= 2
    return names


def set_counts(sizes):
    return {"A": 5, "B": 5, "C": 3, "D": 3} if sizes["batch"] <= 16 else {"A": 3, "B": 3, "C": 2, "D": 2}


def bit_groups(sizes):
    names = bit_names(sizes)
    core = [(k,) for k, name in enumerate(names) if name[0] == "tower"]
    rest = [k for k, name in enumerate(names) if name[0] == "batch"]
    x, y, low, high = rest[:4]
    more = [(k,) for k in rest[4:]]
    firsts = {
        "A": [(x,), (y,), (low, high)],
        "B": [(y,), (x,), (low, high)],
        "C": [(low,), (x,), (y,), (high,)],
        "D": [(low,), (y,), (x,), (high,)],
    }
    return {name: core + groups + more for name, groups in firsts.items()}


def flips_of(group):
    return [tuple(k for i, k in enumerate(group) if choice >> i & 1) for choice in range(1, 2 ** len(group))]


def gather_groups(sizes):
    rest = [k for k, name in enumerate(bit_names(sizes)) if name[0] == "batch"]
    groups = [tuple(rest[i : i + 2]) for i in range(0, len(rest), 2)]
    return groups + [(k,) for k, name in enumerate(bit_names(sizes)) if name[0] == "tower"]


class Place:
    def __init__(self, sizes):
        self.names = bit_names(sizes)
        self.at = {axis: lax.axis_index(axis) for axis in ("tower", "batch")}
        self.bits = [
            lax.rem(lax.div(self.at[axis], jnp.int32(mask)), jnp.int32(2)) for axis, mask in self.names
        ]

    def partner(self, flips):
        other = dict(self.at)
        for k in flips:
            axis, mask = self.names[k]
            other[axis] = other[axis] + mask * (1 - 2 * self.bits[k])
        return (other["tower"], other["batch"])

    def code(self, group, flips=()):
        total = jnp.int32(0)
        for k in group:
            total = total * 2 + (1 - self.bits[k] if k in flips else self.bits[k])
        return total


class Unit:
    def __init__(self, matrix, row, col, cols, kind, groups, item):
        self.matrix, self.row, self.col, self.cols, self.kind, self.item = matrix, row, col, cols, kind, item
        self.steps = []
        size, back, land = UNIT_ROWS, [], 0
        for group in groups:
            ways = 2 ** len(group)
            if size % (8 * ways) == 0:
                size //= ways
                self.steps.append(("cut", group, size, land))
                back.append(("join", group, size, 0))
                land += size * (ways - 1)
            else:
                for k in group:
                    self.steps.append(("whole", (k,), size, land))
                    land += size
        self.land = land
        self.returns = len(self.steps)
        self.steps += back[::-1]

    def place_at(self, place):
        start, stack = jnp.int32(self.row), []
        self.starts = []
        for kind, group, size, _ in self.steps:
            self.starts.append(start)
            if kind == "cut":
                stack.append(start)
                start = start + place.code(group) * size
            elif kind == "join":
                start = stack.pop()


def link_use(names, group, size):
    link = size / LINK
    masks = [names[k] for k in group]
    if masks[0][0] == "tower":
        return {"core": size / CORE}
    if masks == [("batch", 4)]:
        return {"end": link}
    if masks == [("batch", 8)]:
        return {"end": link, "middle": 2 * link}
    if masks == [("batch", 4), ("batch", 8)]:
        return {"end": 3 * link, "middle": 4 * link}
    return {mask: link * (2 ** len(group) - 1) for mask in masks}


def plan(units, names, counts, items, depth=4.0):
    free, clock, flight, pending = {}, 0.0, [], []
    idle = {kind: [(kind, i) for i in range(counts[kind])] for kind in CLASSES}
    done, order = 0, [[] for _ in items]
    left = list(range(len(units)))

    def use(u, s):
        _, group, size, _ = units[u].steps[s]
        return link_use(names, group, size * units[u].cols * 4)

    def pump():
        nonlocal clock
        for u in left:
            if units[u].item < done and (u, 0) not in pending:
                pending.append((u, 0))
        pending.sort()
        for u, s in list(pending):
            unit = units[u]
            if s == 0 and not idle[unit.kind]:
                continue
            if any(free.get(link, 0.0) - clock > depth for link in use(u, 1 if s == 0 else s)):
                continue
            pending.remove((u, s))
            if s == 0:
                left.remove(u)
                unit.set = idle[unit.kind].pop(0)
            clock += 0.08
            end = clock
            for link, time in use(u, s).items():
                free[link] = max(clock, free.get(link, 0.0)) + time
                end = max(end, free[link])
            flight.append((end + FLIGHT, u, s))
            order[done - 1].append(("go", u, s))

    while left or flight or pending or done < len(items):
        flight.sort()
        if flight and (flight[0][0] <= clock or done == len(items)):
            if flight[0][0] > clock and pending:
                clock = min(flight[0][0], clock + 0.5)
                pump()
                continue
            arrived, u, s = flight.pop(0)
            clock = max(clock, arrived) + 0.15
            kind, group, size, _ = units[u].steps[s]
            if kind != "join":
                clock += size * units[u].cols * 4 * (2 ** len(group) - 1) / 4e6
            order[done - 1].append(("serve", u, s))
            if s + 1 < len(units[u].steps):
                pending.append((u, s + 1))
            else:
                idle[units[u].kind].append(units[u].set)
            pump()
        elif done < len(items):
            clock += items[done]
            done += 1
            pump()
        else:
            clock += 0.5
            pump()
    return order, clock


class Exchange:
    def __init__(self, units, place, counts, grads, kept, land, outs, sems):
        self.units, self.place, self.grads, self.kept, self.land, self.outs = units, place, grads, kept, land, outs
        self.send_sem, self.recv_sem, self.load_sem, self.store_sem = sems
        self.sets = {name: i for i, name in enumerate((kind, i) for kind in CLASSES for i in range(counts[kind]))}
        for unit in units:
            unit.place_at(place)

    def part(self, refs, unit, start, rows):
        return refs[unit.matrix].at[pl.ds(pl.multiple_of(start, 8), rows), pl.ds(unit.col, unit.cols)]

    def own(self, unit, start, rows):
        ref = self.kept.at[self.sets[unit.set]]
        return ref.at[pl.ds(pl.multiple_of(start - unit.starts[1], 8), rows), :]

    def load(self, unit):
        spot = self.sets[unit.set]
        return pltpu.make_async_copy(
            self.part(self.grads, unit, unit.starts[1], unit.steps[0][2]), self.kept.at[spot], self.load_sem.at[spot]
        )

    def store(self, unit):
        spot, s = self.sets[unit.set], unit.returns
        start, rows = unit.starts[s], unit.steps[s][2]
        return pltpu.make_async_copy(
            self.own(unit, start, rows), self.part(self.outs, unit, start, rows), self.store_sem.at[spot]
        )

    def copies(self, unit, s):
        kind, group, size, land = unit.steps[s]
        spot, found = self.sets[unit.set], []
        for turn, flips in enumerate(flips_of(group)):
            start = unit.starts[s]
            if kind == "cut":
                start = start + self.place.code(group, flips) * size
            if s == 0:
                source = self.part(self.grads, unit, start, size)
            elif s <= unit.returns:
                source = self.own(unit, start, size)
            else:
                source = self.part(self.outs, unit, start, size)
            if kind == "join":
                target = self.part(self.outs, unit, start, size)
            else:
                target = self.land.at[spot, pl.ds(land + turn * size, size), :]
            found.append(
                pltpu.make_async_remote_copy(
                    src_ref=source,
                    dst_ref=target,
                    send_sem=self.send_sem.at[spot, s, turn],
                    recv_sem=self.recv_sem.at[spot, s, turn],
                    device_id=self.place.partner(flips),
                    device_id_type=MESH,
                )
            )
        return found

    def go(self, u, s):
        unit = self.units[u]
        if s == 0:
            self.load(unit).start()
        for copy in self.copies(unit, s):
            copy.start()

    def serve(self, u, s):
        unit = self.units[u]
        if s == 0:
            self.load(unit).wait()
        for copy in self.copies(unit, s):
            copy.wait()
        kind, group, size, land = unit.steps[s]
        if kind != "join":
            spot = self.sets[unit.set]
            start = unit.starts[s]
            if kind == "cut":
                start = start + self.place.code(group) * size
            kept = self.own(unit, start, size)
            total = kept[...]
            for turn in range(2 ** len(group) - 1):
                total = total + self.land[spot, land + turn * size : land + (turn + 1) * size, :]
            kept[...] = total
        if s + 1 == unit.returns:
            self.store(unit).start()
        if s == unit.returns:
            self.store(unit).wait()


LOW = jnp.bfloat16
FULL = jnp.float32


def dot_nn(left, right):
    return lax.dot_general(left, right, (((1,), (0,)), ((), ())), preferred_element_type=FULL)


def dot_nt(left, right):
    return lax.dot_general(left, right, (((1,), (1,)), ((), ())), preferred_element_type=FULL)


def dot_tn(left, right):
    return lax.dot_general(left, right, (((0,), (0,)), ((), ())), preferred_element_type=FULL)


def loop(count, body):
    def step(i, carry):
        body(i)
        return carry

    lax.fori_loop(0, count, step, 0)


def rows_of(i, size):
    return pl.ds(pl.multiple_of(i * size, size), size)


def offset_buckets(shift):
    keys = lax.broadcasted_iota(jnp.int32, (128, 128), 0)
    queries = lax.broadcasted_iota(jnp.int32, (128, 128), 1)
    offsets = keys - queries + 128 * shift
    distance = jnp.abs(offsets)
    distant = jnp.full((128, 128), 8, jnp.int32)
    for limit in THRESHOLDS:
        distant = distant + jnp.where(distance >= limit, 1, 0)
    buckets = jnp.where(distance < 8, distance, distant)
    return buckets + jnp.where(offsets > 0, 16, 0)


NEAR = ((-1, range(1, 16)), (0, range(32)), (1, range(17, 32)))


def fill_bias(bias, table, head, count):
    ids = [offset_buckets(shift) for shift, _ in NEAR]
    for side in range(count):
        for spot, (shift, members) in enumerate(NEAR):
            block = jnp.zeros((128, 128), FULL)
            for b in members:
                block = jnp.where(ids[spot] == b, table[head + side, b], block)
            bias[side, spot] = block


def bias_strip(bias, side, table, head, jb, blocks):
    parts = []
    for ib in range(blocks):
        shift = jb - ib
        if abs(shift) <= 1:
            parts.append(bias[side, shift + 1])
        else:
            parts.append(jnp.full((128, 128), table[head, 31 if shift > 0 else 15], FULL))
    return jnp.concatenate(parts, axis=1)


def forward_kernel(
    tokens, lengths, wq, wk, wv, wm, wi, wo, gain1, gain2, table,
    q_out, k_out, v_out, ho_out, n1_out, n2_out, h1_out, act_out, slope_out, result_out, lse_out, pooled_out,
    x_s, wq_s, wk_s, wv_s, wm_s, wi_s, wo_s, q_s, k_s, v_s, ho_s, n1_s, n2_s, h1_s, act_s, slope_s, result_s, total_s,
    score_s, prob_s, bias_s, in_sem, out_sem,
):
    count, width = tokens.shape
    rows, seq = lengths.shape[0], tokens.shape[0] // lengths.shape[0]
    heads = table.shape[0]
    size = width // heads
    hidden = wi.shape[1]
    parts = hidden // width
    loads = [
        pltpu.make_async_copy(source, target, in_sem.at[i])
        for i, (source, target) in enumerate(
            [(tokens, x_s), (wq, wq_s), (wk, wk_s), (wv, wv_s), (wm, wm_s), (wi, wi_s), (wo, wo_s)]
        )
    ]
    for load in loads:
        load.start()
    stores = []

    def store(source, target):
        copy = pltpu.make_async_copy(source, target, out_sem.at[len(stores)])
        copy.start()
        stores.append(copy)

    block = 256
    loads[0].wait()

    def norm1(i):
        at = rows_of(i, block)
        x = x_s[at, :].astype(FULL)
        scale = lax.rsqrt(jnp.mean(x * x, -1, keepdims=True) + EPSILON)
        n1_s[at, :] = (x * scale * gain1[...].reshape(1, width)).astype(LOW)

    loop(count // block, norm1)
    store(n1_s, n1_out)
    for i, (w_s, p_s, p_out) in enumerate(((wq_s, q_s, q_out), (wk_s, k_s, k_out), (wv_s, v_s, v_out))):
        loads[1 + i].wait()

        def project(m, w_s=w_s, p_s=p_s):
            at = rows_of(m, 512)
            p_s[at, :] = dot_nn(n1_s[at, :], w_s[...]).astype(LOW)

        loop(count // 512, project)
        store(p_s, p_out)
    blocks = seq // 128
    lanes = lax.broadcasted_iota(jnp.int32, (seq, 2 * size), 1)
    keys = lax.broadcasted_iota(jnp.int32, (128, seq), 0)

    def attend(step):
        pair = lax.div(step, jnp.int32(rows))
        row = lax.rem(step, jnp.int32(rows))
        at = rows_of(row, seq)
        here = rows_of(pair, 2 * size)
        limit = lengths[row]

        @pl.when(row == 0)
        def _():
            fill_bias(bias_s, table, pair * 2, 2)

        q, k = q_s[at, here], k_s[at, here]
        vt = v_s[at, here].T
        found = []
        for side in range(2):
            head = pair * 2 + side
            chosen = jnp.where((lanes >= size) == (side == 1), q, jnp.zeros_like(q))
            score_s[side] = dot_nt(k, chosen)
        for side in range(2):
            head = pair * 2 + side
            top = jnp.full((1, seq), NEGATIVE, FULL)
            for jb in range(blocks):
                strip = score_s[side, jb * 128 : (jb + 1) * 128, :] + bias_strip(bias_s, side, table, head, jb, blocks)
                strip = jnp.where(keys + jb * 128 < limit, strip, NEGATIVE)
                score_s[side, jb * 128 : (jb + 1) * 128, :] = strip
                top = jnp.maximum(top, jnp.max(strip, 0, keepdims=True))
            mass = jnp.zeros((1, seq), FULL)
            for jb in range(blocks):
                strip = jnp.exp(score_s[side, jb * 128 : (jb + 1) * 128, :] - top)
                mass = mass + jnp.sum(strip, 0, keepdims=True)
                prob_s[side, jb * 128 : (jb + 1) * 128, :] = strip.astype(LOW)
            lse_out[row * heads + head] = top + jnp.log(mass)
            found.append(dot_nn(vt[side * size : (side + 1) * size, :], prob_s[side]) / mass)
        ho_s[at, here] = jnp.concatenate(found, 0).T.astype(LOW)

    loop(rows * (heads // 2), attend)
    store(ho_s, ho_out)
    loads[4].wait()

    def mix(i):
        at = rows_of(i, block)
        h1 = x_s[at, :].astype(FULL) + dot_nn(ho_s[at, :], wm_s[...])
        h1_s[at, :] = h1
        scale = lax.rsqrt(jnp.mean(h1 * h1, -1, keepdims=True) + EPSILON)
        n2_s[at, :] = (h1 * scale * gain2[...].reshape(1, width)).astype(LOW)

    loop(count // block, mix)
    store(h1_s, h1_out)
    store(n2_s, n2_out)
    loads[5].wait()
    loads[6].wait()

    for part in range(parts):
        columns = pl.ds(part * width, width)

        def feed(i, part=part, columns=columns):
            at = rows_of(i, block)
            inner = dot_nn(n2_s[at, :], wi_s[:, columns])
            share = 0.5 + 0.5 * lax.erf(inner * 0.7071067811865476)
            act = (inner * share).astype(LOW)
            act_s[at, columns] = act
            slope = share + inner * (jnp.exp(inner * inner * -0.5) * 0.3989422804014327)
            slope_s[at, columns] = slope.astype(LOW)
            more = dot_nn(act, wo_s[columns, :])
            if part == 0:
                total_s[at, :] = h1_s[at, :] + more
            elif part < parts - 1:
                total_s[at, :] = total_s[at, :] + more
            else:
                output = total_s[at, :] + more
                total_s[at, :] = output
                result_s[at, :] = output.astype(LOW)

        loop(count // block, feed)
        store(act_s.at[:, columns], act_out.at[:, columns])
        store(slope_s.at[:, columns], slope_out.at[:, columns])
    store(result_s, result_out)
    slots = lax.broadcasted_iota(jnp.int32, (seq, 1), 0)
    for row in range(rows):
        kept = jnp.where(slots < lengths[row], total_s[row * seq : (row + 1) * seq, :], 0.0)
        pooled_out[row : row + 1, :] = jnp.sum(kept, 0, keepdims=True) / lengths[row].astype(FULL)
    for copy in stores:
        copy.wait()


def forward(tokens, lengths, wq, wk, wv, wm, wi, wo, gain1, gain2, table):
    count, width = tokens.shape
    hidden = wi.shape[1]
    rows = lengths.shape[0]
    heads = table.shape[0]
    seq = count // rows
    shape = jax.ShapeDtypeStruct
    any_spec = pl.BlockSpec(memory_space=pl.ANY)
    vmem_spec = pl.BlockSpec(memory_space=pltpu.VMEM)
    smem_spec = pl.BlockSpec(memory_space=pltpu.SMEM)
    low = shape((count, width), LOW)
    wide = shape((count, hidden), LOW)
    weights = [pltpu.VMEM(w.shape, LOW) for w in (wq, wk, wv, wm, wi, wo)]
    narrow_s = pltpu.VMEM((count, width), LOW)
    full_s = pltpu.VMEM((count, width), FULL)
    wide_s = pltpu.VMEM((count, hidden), LOW)
    return pl.pallas_call(
        forward_kernel,
        out_shape=[low, low, low, low, low, low, shape((count, width), FULL), wide, wide, low]
        + [shape((rows * heads, 1, seq), FULL), shape((rows, width), FULL)],
        in_specs=[any_spec, smem_spec] + [any_spec] * 6 + [vmem_spec] * 2 + [smem_spec],
        out_specs=[any_spec] * 10 + [vmem_spec] * 2,
        scratch_shapes=[narrow_s]
        + weights
        + [narrow_s] * 6
        + [full_s, wide_s, wide_s, narrow_s, full_s]
        + [
            pltpu.VMEM((2, seq, seq), FULL),
            pltpu.VMEM((2, seq, seq), LOW),
            pltpu.VMEM((2, 3, 128, 128), FULL),
            pltpu.SemaphoreType.DMA((7,)),
            pltpu.SemaphoreType.DMA((24,)),
        ],
        compiler_params=pltpu.CompilerParams(vmem_limit_bytes=62 * 2**20),
    )(tokens, lengths, wq, wk, wv, wm, wi, wo, gain1, gain2, table)


def norm_back(values, gain, dy):
    scale = lax.rsqrt(jnp.mean(values * values, -1, keepdims=True) + EPSILON)
    along = values * scale
    dscaled = gain * dy
    mean = jnp.mean(along * dscaled, -1, keepdims=True)
    return scale * (dscaled - along * mean), jnp.sum(along * dy, 0, keepdims=True)


def contrast(queries, documents, doc_groups, positives):
    count = doc_groups.shape[1]
    precise = functools.partial(lax.dot_general, precision=HIGHEST, preferred_element_type=FULL)
    rates = [lax.rsqrt(jnp.sum(p * p, -1, keepdims=True) + EPSILON) for p in (queries, documents)]
    unit = [p * rate for p, rate in zip((queries, documents), rates)]
    scores = SCALE * precise(unit[0], unit[1], (((1,), (1,)), ((), ())))
    indices = lax.broadcasted_iota(jnp.int32, (count, count), 0)
    chosen = jnp.where(positives == indices, 1.0, 0.0).T
    query_groups = jnp.sum(chosen * doc_groups.astype(FULL), 1, keepdims=True)
    masked = jnp.where(query_groups == doc_groups.astype(FULL), scores, NEGATIVE)
    highest = jnp.max(masked, 1, keepdims=True)
    weights = jnp.exp(masked - highest)
    mass = jnp.sum(weights, 1, keepdims=True)
    matched = jnp.sum(jnp.where(chosen > 0.5, scores, 0.0), 1, keepdims=True)
    loss = jnp.sum(highest + jnp.log(mass) - matched, 0, keepdims=True) / count
    dscore = weights / mass - chosen
    dunit = (
        SCALE * precise(dscore, unit[1], (((1,), (0,)), ((), ()))),
        SCALE * precise(dscore, unit[0], (((0,), (0,)), ((), ()))),
    )
    dpooled = [rate * (d - u * jnp.sum(u * d, -1, keepdims=True)) for rate, d, u in zip(rates, dunit, unit)]
    return loss, dpooled


def make_units(sizes, hidden, width):
    groups = bit_groups(sizes)
    parts, thirds = hidden // width, width // UNIT_ROWS
    items = [("gather", 12.0), ("loss", 3.0)]
    blocks = []
    for part in range(parts):
        items.append(("outer", 1.9))
        blocks += [(0, part * width + i * UNIT_ROWS, 0, len(items)) for i in range(thirds)]
    for part in range(parts):
        items.append(("inner", 6.2))
        blocks += [(1, i * UNIT_ROWS, part * width, len(items)) for i in range(thirds)]
    items += [("mix", 3.5), ("mixed", 1.8)]
    blocks += [(5, i * UNIT_ROWS, 0, len(items)) for i in range(thirds)]
    items += [("attend", 2.4)] * 24
    for matrix in range(2, 5):
        items.append(("projection", 1.8))
        blocks += [(matrix, i * UNIT_ROWS, 0, len(items)) for i in range(thirds)]
    items.append(("input", 6.0))
    units = []
    for i, (matrix, row, col, item) in enumerate(blocks):
        kind = PATTERN[i % len(PATTERN)]
        units.append(Unit(matrix, row, col, width, kind, groups[kind], item))
    return units, items


def backward_kernel(
    sizes, units, order, counts,
    cot, pooled, lengths, doc_groups, positives, act, slope, wo, wi, n2, h1, ho, q, k, v, n1, tokens, lse,
    wq, wk, wv, wm, gain1, gain2, table,
    *refs,
):
    grads, outs = refs[:6], refs[6:12]
    tokens_grad, small_out, loss_out = refs[12:15]
    (
        narrow, square, staged, full, bias_s, near_s, sums_s, every_s, small_land, kept, land,
        in_sem, chunk_sem, stage_sem, last_sem, hop_send, hop_recv, small_send, small_recv,
        send_sem, recv_sem, load_sem, store_sem,
    ) = refs[15:]
    count, width = narrow.shape[1:]
    rows = lengths.shape[0]
    seq = count // rows
    heads = table.shape[0]
    size = width // heads
    parts = wo.shape[0] // width
    block = 256
    place = Place(sizes)
    names = place.names
    tower, batch = place.at["tower"], place.at["batch"]
    exchange = Exchange(units, place, counts, grads, kept, land, outs, (send_sem, recv_sem, load_sem, store_sem))
    cot_s, n2_s, dout_s = narrow.at[8], narrow.at[9], narrow.at[10]
    act_s = [narrow.at[part] for part in range(parts)]
    slope_s = [narrow.at[parts + part] for part in range(parts)]
    h1_s, sum_s = full.at[0], full.at[1]
    loads = {}

    def load(name, source, target):
        copy = pltpu.make_async_copy(source, target, in_sem.at[len(loads)])
        copy.start()
        loads[name] = copy

    def cut(part):
        return pl.ds(part * width, width)

    load("cot", cot, cot_s)
    for part in range(parts):
        load("act%d" % part, act.at[:, cut(part)], act_s[part])
    for part in range(parts):
        load("wo%d" % part, wo.at[cut(part), :], square.at[part])
    load("n2", n2, n2_s)
    for part in range(parts):
        load("slope%d" % part, slope.at[:, cut(part)], slope_s[part])

    def wi_chunk(part):
        return pltpu.make_async_copy(wi.at[:, cut(part)], square.at[parts + part % 2], chunk_sem.at[part])

    for part in range(2):
        wi_chunk(part).start()
    load("h1", h1, h1_s)

    item = 0
    stage_of = {}

    def act_on(actions):
        for action, u, s in actions:
            if action == "go":
                if s == 0:
                    exchange_ready(u)
                exchange.go(u, s)
            else:
                exchange.serve(u, s)

    def exchange_ready(u):
        unit = units[u]
        key = (unit.matrix, unit.row // width if unit.matrix == 0 else unit.col // width)
        if key in stage_of:
            stage_of.pop(key).wait()

    def between():
        nonlocal item
        act_on(order[item])
        item += 1

    staged_count = 0
    staged_last = {}

    def stage(value, matrix, part, target):
        nonlocal staged_count
        spot = staged_count % 3
        if spot in staged_last and staged_last[spot] in stage_of:
            stage_of.pop(staged_last[spot]).wait()
        staged[spot] = value
        copy = pltpu.make_async_copy(staged.at[spot], target, stage_sem.at[staged_count])
        copy.start()
        stage_of[(matrix, part)] = copy
        staged_last[spot] = (matrix, part)
        staged_count += 1

    hops = gather_groups(sizes)
    every_s[tower, batch] = pooled[...]
    deltas = set()
    for group in list(bit_groups(sizes).values()) + [hops]:
        for bits in group:
            deltas.update(flips_of(bits))
    barrier = pltpu.get_barrier_semaphore()
    for flips in sorted(deltas):
        pl.semaphore_signal(barrier, inc=1, device_id=place.partner(flips), device_id_type=MESH)
    pl.semaphore_wait(barrier, len(deltas))
    for h, group in enumerate(hops):
        masks = [names[bit] for bit in group]
        if masks[0][0] == "tower":
            held = every_s.at[tower]
        else:
            mask = masks[0][1]
            held = every_s.at[tower, pl.ds(lax.div(batch, jnp.int32(mask)) * mask, mask)]
        copies = [
            pltpu.make_async_remote_copy(
                src_ref=held,
                dst_ref=held,
                send_sem=hop_send.at[h, turn],
                recv_sem=hop_recv.at[h, turn],
                device_id=place.partner(flips),
                device_id_type=MESH,
            )
            for turn, flips in enumerate(flips_of(group))
        ]
        for copy in copies:
            copy.start()
        for copy in copies:
            copy.wait()
    between()

    for t in range(2):
        for b in range(sizes["batch"]):
            staged[t, b * rows : (b + 1) * rows, :] = every_s[t, b]
    total = rows * sizes["batch"]
    loss, dpooled = contrast(staged[0, 0:total, :], staged[1, 0:total, :], doc_groups[...], positives[...])
    loss_out[...] = loss
    mine = jnp.where(tower == 0, dpooled[0], dpooled[1])
    ids = lax.broadcasted_iota(jnp.int32, (mine.shape[0], 1), 0)
    spread = [
        jnp.sum(jnp.where(ids == batch * rows + row, mine, 0.0), 0, keepdims=True) / lengths[row].astype(FULL)
        for row in range(rows)
    ]
    loads["cot"].wait()

    def full_dout(row, i):
        at = pl.ds(pl.multiple_of(row * seq + i * block, block), block)
        slot = lax.broadcasted_iota(jnp.int32, (block, 1), 0) + i * block
        return at, cot_s[at, :].astype(FULL) + jnp.where(slot < lengths[row], spread[row], 0.0)

    for row in range(rows):

        def round_dout(i, row=row):
            at, dout = full_dout(row, i)
            dout_s[at, :] = dout.astype(LOW)

        loop(seq // block, round_dout)
    between()

    for part in range(parts):
        loads["act%d" % part].wait()
        stage(dot_tn(act_s[part][...], dout_s[...]), 0, part, grads[0].at[cut(part), :])
        between()
    for name, source, target in (("q", q, 0), ("k", k, 1), ("v", v, 2), ("n1", n1, 3)):
        load(name, source, narrow.at[target])
    loads["n2"].wait()
    for part in range(parts):
        loads["slope%d" % part].wait()
        loads["wo%d" % part].wait()
        wi_chunk(part).wait()

        def inner_back(i, part=part):
            at = rows_of(i, block)
            dact = dot_nt(dout_s[at, :], square[part])
            dinner = (slope_s[part][at, :].astype(FULL) * dact).astype(LOW)
            slope_s[part][at, :] = dinner
            more = dot_nt(dinner, square[parts + part % 2])
            sum_s[at, :] = more if part == 0 else sum_s[at, :] + more

        loop(count // block, inner_back)
        if part + 2 < parts:
            wi_chunk(part + 2).start()
        stage(dot_tn(n2_s[...], slope_s[part][...]), 1, part, grads[1].at[:, cut(part)])
        between()
    load("ho", ho, narrow.at[9])
    for name, source, target in (("wm", wm, 0), ("wq", wq, 1), ("wk", wk, 2), ("wv", wv, 3)):
        load(name, source, square.at[target])
    small_out[...] = jnp.zeros_like(small_out)
    loads["h1"].wait()
    loads["wm"].wait()
    q_s, k_s, v_s, n1_s = (narrow.at[i] for i in range(4))
    dh_s, dq_s, dk_s, dv_s = (narrow.at[i] for i in range(4, 8))

    for row in range(rows):

        def mix_back(i, row=row):
            at, dout = full_dout(row, i)
            dv, dgain = norm_back(h1_s[at, :], gain2[...].reshape(1, width), sum_s[at, :])
            dh1 = dout + dv
            h1_s[at, :] = dh1
            small_out[1:2, :] = small_out[1:2, :] + dgain
            da = dh1.astype(LOW)
            cot_s[at, :] = da
            dh_s[at, :] = dot_nt(da, square[0]).astype(LOW)

        loop(seq // block, mix_back)
    between()
    loads["ho"].wait()
    stage(dot_tn(narrow[9], cot_s[...]), 5, 0, grads[5])
    between()
    for copy in list(stage_of.values()):
        copy.wait()
    stage_of.clear()
    load("x", tokens, narrow.at[9])
    for name in ("q", "k", "v"):
        loads[name].wait()

    blocks = seq // 128
    lanes = lax.broadcasted_iota(jnp.int32, (seq, 2 * size), 1)
    keys = lax.broadcasted_iota(jnp.int32, (128, seq), 0)
    first_item = item
    steps = rows * (heads // 2)

    def between_at(step, side):
        for index in range(steps):
            actions = order[first_item + 2 * index + side] if 2 * index + side < 24 else []
            if actions:
                pl.when(step == index)(functools.partial(act_on, actions))

    def attend_back(step):
        pair = lax.div(step, jnp.int32(rows))
        row = lax.rem(step, jnp.int32(rows))
        at = rows_of(row, seq)
        here = rows_of(pair, 2 * size)
        limit = lengths[row]

        @pl.when(row == 0)
        def _():
            near_s[...] = jnp.zeros_like(near_s)
            fill_bias(bias_s, table, pair * 2, 2)

        qp, kp, vp, dp = q_s[at, here], k_s[at, here], v_s[at, here], dh_s[at, here]
        nothing = jnp.zeros_like(qp)
        kt = kp.T
        dq, dk, dv = [], [], []
        score_s = [staged.at[side, 0:seq, 0:seq] for side in range(2)]
        dprob_s = [staged.at[2 + side, 0:seq, 0:seq] for side in range(2)]
        prob_s = [narrow.at[8, side * seq : (side + 1) * seq, 0:seq] for side in range(2)]
        dscore_s = [narrow.at[10, side * seq : (side + 1) * seq, 0:seq] for side in range(2)]
        for side in range(2):
            chosen = (lanes >= size) == (side == 1)
            score_s[side][...] = dot_nt(kp, jnp.where(chosen, qp, nothing))
            dprob_s[side][...] = dot_nt(vp, jnp.where(chosen, dp, nothing))
        for side in range(2):
            head = pair * 2 + side
            level = lse[row * heads + head]
            delta = jnp.zeros((1, seq), FULL)
            for jb in range(blocks):
                some = slice(jb * 128, (jb + 1) * 128)
                strip = score_s[side][some, :] + bias_strip(bias_s, side, table, head, jb, blocks)
                strip = jnp.where(keys + jb * 128 < limit, strip, NEGATIVE)
                prob = jnp.exp(strip - level)
                prob_s[side][some, :] = prob.astype(LOW)
                score_s[side][some, :] = prob
                delta = delta + jnp.sum(prob * dprob_s[side][some, :], 0, keepdims=True)
            for jb in range(blocks):
                some = slice(jb * 128, (jb + 1) * 128)
                dscore = score_s[side][some, :] * (dprob_s[side][some, :] - delta)
                dscore_s[side][some, :] = dscore.astype(LOW)
                for ib in range(blocks):
                    spot = min(max(jb - ib, -2), 2) + 2
                    near_s[side, spot] = near_s[side, spot] + dscore[:, ib * 128 : (ib + 1) * 128]
            dk.append(dot_nn(dscore_s[side][...], qp))
            dv.append(dot_nn(prob_s[side][...], dp))
            dq.append(dot_nn(kt[side * size : (side + 1) * size, :], dscore_s[side][...]))
            if side == 0:
                between_at(step, 0)
        first = lanes < size
        dk_s[at, here] = jnp.where(first, dk[0], dk[1]).astype(LOW)
        dv_s[at, here] = jnp.where(first, dv[0], dv[1]).astype(LOW)
        dq_s[at, here] = jnp.concatenate(dq, 0).T.astype(LOW)

        @pl.when(row == rows - 1)
        def _():
            ids = [offset_buckets(shift) for shift, _ in NEAR]
            for side in range(2):
                bucket = lax.broadcasted_iota(jnp.int32, (1, 128), 1)
                found = jnp.zeros((1, 128), FULL)
                for spot, (shift, members) in enumerate(NEAR):
                    total = near_s[side, spot + 1]
                    for b in members:
                        share = jnp.sum(jnp.where(ids[spot] == b, total, 0.0), 0, keepdims=True)
                        found = found + jnp.where(bucket == b, jnp.sum(share, 1, keepdims=True), 0.0)
                for spot, b in ((0, 15), (4, 31)):
                    share = jnp.sum(near_s[side, spot], 0, keepdims=True)
                    found = found + jnp.where(bucket == b, jnp.sum(share, 1, keepdims=True), 0.0)
                sums_s[pair * 2 + side] = found

        between_at(step, 1)

    loop(steps, attend_back)
    item = first_item + 24
    for head in range(heads):
        small_out[8 + head : 9 + head, 0:128] = sums_s[head]

    loads["n1"].wait()
    for matrix, d_s in ((2, dq_s), (3, dk_s), (4, dv_s)):
        stage(dot_tn(n1_s[...], d_s[...]), matrix, 0, grads[matrix])
        between()
    for name in ("wq", "wk", "wv", "x"):
        loads[name].wait()

    def input_back(i):
        at = rows_of(i, block)
        dn1 = dot_nt(dq_s[at, :], square[1]) + dot_nt(dk_s[at, :], square[2]) + dot_nt(dv_s[at, :], square[3])
        dv, dgain = norm_back(narrow[9, at, :].astype(FULL), gain1[...].reshape(1, width), dn1)
        small_out[0:1, :] = small_out[0:1, :] + dgain
        cot_s[at, :] = (h1_s[at, :] + dv).astype(LOW)

    loop(count // block, input_back)
    last = pltpu.make_async_copy(cot_s, tokens_grad, last_sem)
    last.start()

    def small_copy(bit):
        return pltpu.make_async_remote_copy(
            src_ref=small_out,
            dst_ref=small_land.at[bit],
            send_sem=small_send.at[bit],
            recv_sem=small_recv.at[bit],
            device_id=place.partner((bit,)),
            device_id_type=MESH,
        )

    small_copy(0).start()
    actions = order[item]
    for bit in range(len(names)):
        act_on(actions[len(actions) * bit // (len(names) + 1) : len(actions) * (bit + 1) // (len(names) + 1)])
        small_copy(bit).wait()
        small_out[...] = small_out[...] + small_land[bit]
        if bit + 1 < len(names):
            small_copy(bit + 1).start()
    act_on(actions[len(actions) * len(names) // (len(names) + 1) :])
    last.wait()
    for copy in stage_of.values():
        copy.wait()


def backward(
    sizes, cot, pooled, lengths, doc_groups, positives, act, slope, wo, wi, n2, h1, ho, q, k, v, n1, tokens, lse,
    wq, wk, wv, wm, gain1, gain2, table,
):
    count, width = cot.shape
    hidden = wo.shape[0]
    rows = lengths.shape[0]
    heads = table.shape[0]
    total = doc_groups.shape[0]
    names = bit_names(sizes)
    units, items = make_units(sizes, hidden, width)
    counts = set_counts(sizes)
    order, _ = plan(units, names, counts, [time for _, time in items])
    steps = max(len(unit.steps) for unit in units)
    sets = sum(counts.values())
    shape = jax.ShapeDtypeStruct
    any_spec = pl.BlockSpec(memory_space=pl.ANY)
    vmem_spec = pl.BlockSpec(memory_space=pltpu.VMEM)
    smem_spec = pl.BlockSpec(memory_space=pltpu.SMEM)
    squares = [shape((hidden, width), FULL), shape((width, hidden), FULL)] + [shape((width, width), FULL)] * 4
    hops = len(gather_groups(sizes))
    dma = pltpu.SemaphoreType.DMA
    return pl.pallas_call(
        functools.partial(backward_kernel, sizes, units, order, counts),
        out_shape=squares + squares + [shape((count, width), LOW), shape((24, width), FULL), shape((1, 1), FULL)],
        in_specs=[any_spec, vmem_spec, smem_spec, vmem_spec, vmem_spec]
        + [any_spec] * 12
        + [vmem_spec]
        + [any_spec] * 4
        + [vmem_spec] * 2
        + [smem_spec],
        out_specs=[any_spec] * 13 + [vmem_spec] * 2,
        scratch_shapes=[
            pltpu.VMEM((11, count, width), LOW),
            pltpu.VMEM((6, width, width), LOW),
            pltpu.VMEM((4, width, width), FULL),
            pltpu.VMEM((2, count, width), FULL),
            pltpu.VMEM((2, 3, 128, 128), FULL),
            pltpu.VMEM((2, 5, 128, 128), FULL),
            pltpu.VMEM((heads, 1, 128), FULL),
            pltpu.VMEM((2, sizes["batch"], rows, width), FULL),
            pltpu.VMEM((len(names), 24, width), FULL),
            pltpu.VMEM((sets, units[0].steps[0][2], width), FULL),
            pltpu.VMEM((sets, max(unit.land for unit in units), width), FULL),
            dma((32,)),
            dma((8,)),
            dma((16,)),
            dma,
            dma((hops, 3)),
            dma((hops, 3)),
            dma((len(names),)),
            dma((len(names),)),
            dma((sets, steps, 3)),
            dma((sets, steps, 3)),
            dma((sets,)),
            dma((sets,)),
        ],
        compiler_params=pltpu.CompilerParams(
            collective_id=0, has_side_effects=True, vmem_limit_bytes=int(63.5 * 2**20)
        ),
    )(
        cot, pooled, lengths, doc_groups.reshape(1, total), positives.reshape(1, total), act, slope, wo, wi, n2, h1,
        ho, q, k, v, n1, tokens, lse, wq, wk, wv, wm, gain1, gain2, table,
    )


def hand_out_kernel(blocks, count, heads, *refs):
    sources, (small, loss_in) = refs[:count], refs[count : count + 2]
    targets = refs[count + 2 : 2 * count + 2]
    gain1, gain2, table, loss = refs[2 * count + 2 : 2 * count + 6]
    full, low, in_sem, out_sem = refs[2 * count + 6 :]
    loads, stores = [], []
    for i, (array, spot, at) in enumerate(blocks):
        held = (low if sources[array].dtype == LOW else full).at[spot]
        loads.append(pltpu.make_async_copy(sources[array].at[at], held, in_sem.at[i]))
        stores.append(pltpu.make_async_copy(held, targets[array].at[at], out_sem.at[i]))
    for load in loads:
        load.start()
    gain1[...] = small[0]
    gain2[...] = small[1]
    loss[...] = loss_in[...]
    table[...] = small[8 : 8 + heads, 0 : table.shape[1]]
    for load, store in zip(loads, stores):
        load.wait()
        store.start()
    for store in stores:
        store.wait()


def hand_out(arrays, small, loss, heads, buckets):
    width = small.shape[1]
    blocks, held = [], {FULL: 0, LOW: 0}
    for i, array in enumerate(arrays):
        for col in range(0, array.shape[1], width):
            for row in range(0, array.shape[0], UNIT_ROWS):
                kind = LOW if array.dtype == LOW else FULL
                blocks.append((i, held[kind], (pl.ds(row, UNIT_ROWS), pl.ds(col, width))))
                held[kind] += 1
    any_spec = pl.BlockSpec(memory_space=pl.ANY)
    vmem_spec = pl.BlockSpec(memory_space=pltpu.VMEM)
    shape = jax.ShapeDtypeStruct
    return pl.pallas_call(
        functools.partial(hand_out_kernel, blocks, len(arrays), heads),
        out_shape=[shape(a.shape, a.dtype) for a in arrays]
        + [shape((width,), FULL), shape((width,), FULL), shape((heads, buckets), FULL), shape((1, 1), FULL)],
        in_specs=[any_spec] * len(arrays) + [vmem_spec] * 2,
        out_specs=[any_spec] * len(arrays) + [vmem_spec] * 4,
        scratch_shapes=[
            pltpu.VMEM((held[FULL], UNIT_ROWS, width), FULL),
            pltpu.VMEM((held[LOW], UNIT_ROWS, width), LOW),
            pltpu.SemaphoreType.DMA((len(blocks),)),
            pltpu.SemaphoreType.DMA((len(blocks),)),
        ],
        compiler_params=pltpu.CompilerParams(vmem_limit_bytes=63 * 2**20),
    )(*arrays, small, loss)


def shards(
    tokens,
    lengths,
    doc_groups,
    positives,
    cotangent,
    w_query,
    w_key,
    w_value,
    w_mixed,
    w_inner,
    w_outer,
    gain_attn,
    gain_ffn,
    rel_table,
):
    rows = tokens.shape[1]
    count, width = rows * tokens.shape[2], tokens.shape[3]
    buckets, heads = rel_table.shape
    sizes = {axis: lax.axis_size(axis) for axis in ("tower", "batch")}
    flat = tokens.reshape(count, width)
    cot = cotangent.reshape(count, width)
    own_lengths = lengths.reshape(rows)
    table = rel_table.T
    q, k, v, ho, n1, n2, h1, act, slope, result, lse, pooled = forward(
        flat, own_lengths, w_query, w_key, w_value, w_mixed, w_inner, w_outer, gain_attn, gain_ffn, table
    )
    found = backward(
        sizes, cot, pooled, own_lengths, doc_groups, positives, act, slope, w_outer, w_inner, n2, h1, ho, q, k, v, n1,
        flat, lse, w_query, w_key, w_value, w_mixed, gain_attn, gain_ffn, table,
    )
    small, loss = found[13:]
    given = hand_out(found[6:13], small, loss, heads, buckets)
    wo_grad, wi_grad, wq_grad, wk_grad, wv_grad, wm_grad, tokens_grad, gain1_grad, gain2_grad, table_grad, loss = given
    return (
        result.reshape(tokens.shape),
        pooled[None],
        loss[0, 0],
        tokens_grad.reshape(tokens.shape),
        wq_grad,
        wk_grad,
        wv_grad,
        wm_grad,
        wi_grad,
        wo_grad,
        gain1_grad,
        gain2_grad,
        table_grad.T,
    )


def solution(mesh):
    return jax.shard_map(
        shards,
        mesh=mesh,
        in_specs=(
            P("tower", "batch", None, None),
            P("tower", "batch"),
            P(),
            P(),
            P("tower", "batch", None, None),
            P(),
            P(),
            P(),
            P(),
            P(),
            P(),
            P(),
            P(),
            P(),
        ),
        out_specs=(
            P("tower", "batch", None, None),
            P("tower", "batch", None),
            P(),
            P("tower", "batch", None, None),
            P(),
            P(),
            P(),
            P(),
            P(),
            P(),
            P(),
            P(),
            P(),
        ),
        check_vma=False,
    )
```

```python
import functools

import jax
import jax.numpy as jnp
from jax import lax
from jax.experimental import pallas as pl
from jax.experimental.pallas import tpu as pltpu
from jax.sharding import PartitionSpec as P

EPSILON = 1e-06
SCALE = 50.0
NEGATIVE = -1000000000.0
THRESHOLDS = (12, 16, 23, 32, 46, 64, 91)
HIGHEST = lax.Precision.HIGHEST


MESH = pl.DeviceIdType.MESH
LINK = 45.7e3
CORE = 500e3
FLIGHT = 4.0
CLASSES = "ABCD"
PATTERN = "ABCABD"
UNIT_COLS = 256


def bit_names(sizes):
    names = []
    for axis in ("tower", "batch"):
        mask = 1
        while mask < sizes[axis]:
            names.append((axis, mask))
            mask *= 2
    return names


def set_counts(sizes):
    return {"A": 7, "B": 7, "C": 4, "D": 4} if sizes["batch"] <= 16 else {"A": 2, "B": 2, "C": 1, "D": 1}


def bit_groups(sizes):
    names = bit_names(sizes)
    rest = [k for k, name in enumerate(names) if name[0] == "batch"]
    x, y, low, high = rest[:4]
    more = [(k,) for k in rest[4:]]
    firsts = {
        "A": [(x,), (y,), (low, high)],
        "B": [(y,), (x,), (low, high)],
        "C": [(low,), (x,), (y,), (high,)],
        "D": [(low,), (y,), (x,), (high,)],
    }
    return {name: groups + more for name, groups in firsts.items()}


def flips_of(group):
    return [tuple(k for i, k in enumerate(group) if choice >> i & 1) for choice in range(1, 2 ** len(group))]


def gather_groups(sizes):
    rest = [k for k, name in enumerate(bit_names(sizes)) if name[0] == "batch"]
    groups = [tuple(rest[i : i + 2]) for i in range(0, len(rest), 2)]
    return groups + [(k,) for k, name in enumerate(bit_names(sizes)) if name[0] == "tower"]


class Place:
    def __init__(self, sizes):
        self.names = bit_names(sizes)
        self.at = {axis: lax.axis_index(axis) for axis in ("tower", "batch")}
        self.bits = [
            lax.rem(lax.div(self.at[axis], jnp.int32(mask)), jnp.int32(2)) for axis, mask in self.names
        ]

    def partner(self, flips):
        other = dict(self.at)
        for k in flips:
            axis, mask = self.names[k]
            other[axis] = other[axis] + mask * (1 - 2 * self.bits[k])
        return (other["tower"], other["batch"])

    def code(self, group, flips=()):
        total = jnp.int32(0)
        for k in group:
            total = total * 2 + (1 - self.bits[k] if k in flips else self.bits[k])
        return total


class Unit:
    def __init__(self, matrix, row, rows, col, cols, kind, groups, item):
        self.matrix, self.row, self.rows, self.col, self.cols, self.kind, self.item = matrix, row, rows, col, cols, kind, item
        self.steps = []
        size, back, land = rows, [], 0
        for group in groups:
            ways = 2 ** len(group)
            if size % (8 * ways) == 0:
                size //= ways
                self.steps.append(("cut", group, size, land))
                back.append(("join", group, size, 0))
                land += size * (ways - 1)
            else:
                for k in group:
                    self.steps.append(("whole", (k,), size, land))
                    land += size
        self.land = land
        self.returns = len(self.steps)
        self.steps += back[::-1]
        self.steps.append(("join", (0,), rows, 0))

    def place_at(self, place):
        start, stack = self.row + place.at["tower"] * self.rows, []
        self.starts = []
        for kind, group, size, _ in self.steps:
            self.starts.append(start)
            if kind == "cut":
                stack.append(start)
                start = start + place.code(group) * size
            elif kind == "join" and stack:
                start = stack.pop()


def link_use(names, group, size):
    link = size / LINK
    masks = [names[k] for k in group]
    if masks[0][0] == "tower":
        return {"core": size / CORE}
    if masks == [("batch", 4)]:
        return {"end": link}
    if masks == [("batch", 8)]:
        return {"end": link, "middle": 2 * link}
    if masks == [("batch", 4), ("batch", 8)]:
        return {"end": 3 * link, "middle": 4 * link}
    return {mask: link * (2 ** len(group) - 1) for mask in masks}


def plan(units, names, counts, items, depth=8.0):
    free, clock, flight, pending = {}, 0.0, [], []
    idle = {kind: [(kind, i) for i in range(counts[kind])] for kind in CLASSES}
    done, order = 0, [[] for _ in items]
    left = list(range(len(units)))

    def use(u, s):
        _, group, size, _ = units[u].steps[s]
        return link_use(names, group, size * units[u].cols * 4)

    def pump():
        nonlocal clock
        for u in left:
            if units[u].item < done and (u, 0) not in pending:
                pending.append((u, 0))
        pending.sort()
        for u, s in list(pending):
            unit = units[u]
            if s == 0 and not idle[unit.kind]:
                continue
            if any(free.get(link, 0.0) - clock > depth for link in use(u, 1 if s == 0 else s)):
                continue
            pending.remove((u, s))
            if s == 0:
                left.remove(u)
                unit.set = idle[unit.kind].pop(0)
            clock += 0.08
            end = clock
            for link, time in use(u, s).items():
                free[link] = max(clock, free.get(link, 0.0)) + time
                end = max(end, free[link])
            flight.append((end + FLIGHT, u, s))
            order[done - 1].append(("go", u, s))

    while left or flight or pending or done < len(items):
        flight.sort()
        if flight and (flight[0][0] <= clock or done == len(items)):
            if flight[0][0] > clock and pending:
                clock = min(flight[0][0], clock + 0.5)
                pump()
                continue
            arrived, u, s = flight.pop(0)
            clock = max(clock, arrived) + 0.15
            kind, group, size, _ = units[u].steps[s]
            if kind != "join":
                clock += size * units[u].cols * 4 * (2 ** len(group) - 1) / 4e6
            order[done - 1].append(("serve", u, s))
            if s + 1 < len(units[u].steps):
                pending.append((u, s + 1))
            else:
                idle[units[u].kind].append(units[u].set)
            pump()
        elif done < len(items):
            clock += items[done]
            done += 1
            pump()
        else:
            clock += 0.5
            pump()
    return order, clock


class Exchange:
    def __init__(self, units, place, counts, grads, kept, land, outs, sems):
        self.units, self.place, self.grads, self.kept, self.land, self.outs = units, place, grads, kept, land, outs
        self.send_sem, self.recv_sem, self.load_sem, self.store_sem, self.last_send, self.last_recv = sems
        self.sets = {name: i for i, name in enumerate((kind, i) for kind in CLASSES for i in range(counts[kind]))}
        for unit in units:
            unit.place_at(place)

    def part(self, refs, unit, start, rows):
        return refs[unit.matrix].at[pl.ds(pl.multiple_of(start, 8), rows), pl.ds(unit.col, unit.cols)]

    def own(self, unit, start, rows):
        ref = self.kept.at[self.sets[unit.set]]
        return ref.at[pl.ds(pl.multiple_of(start - unit.starts[1], 8), rows), :]

    def load(self, unit):
        spot = self.sets[unit.set]
        return pltpu.make_async_copy(
            self.part(self.grads, unit, unit.starts[1], unit.steps[0][2]), self.kept.at[spot], self.load_sem.at[spot]
        )

    def store(self, unit):
        spot, s = self.sets[unit.set], unit.returns
        start, rows = unit.starts[s], unit.steps[s][2]
        return pltpu.make_async_copy(
            self.own(unit, start, rows), self.part(self.outs, unit, start, rows), self.store_sem.at[spot]
        )

    def copies(self, u, s):
        unit = self.units[u]
        last = s == len(unit.steps) - 1
        kind, group, size, land = unit.steps[s]
        spot, found = self.sets[unit.set], []
        for turn, flips in enumerate(flips_of(group)):
            start = unit.starts[s]
            if kind == "cut":
                start = start + self.place.code(group, flips) * size
            if s == 0:
                source = self.part(self.grads, unit, start, size)
            elif s <= unit.returns:
                source = self.own(unit, start, size)
            else:
                source = self.part(self.outs, unit, start, size)
            if kind == "join":
                target = self.part(self.outs, unit, start, size)
            else:
                target = self.land.at[spot, pl.ds(land + turn * size, size), :]
            found.append(
                pltpu.make_async_remote_copy(
                    src_ref=source,
                    dst_ref=target,
                    send_sem=self.last_send.at[u] if last else self.send_sem.at[spot, s, turn],
                    recv_sem=self.last_recv.at[u] if last else self.recv_sem.at[spot, s, turn],
                    device_id=self.place.partner(flips),
                    device_id_type=MESH,
                )
            )
        return found

    def go(self, u, s):
        unit = self.units[u]
        if s == 0:
            self.load(unit).start()
        for copy in self.copies(u, s):
            copy.start()

    def serve(self, u, s):
        unit = self.units[u]
        if s == 0:
            self.load(unit).wait()
        for copy in self.copies(u, s):
            copy.wait()
        kind, group, size, land = unit.steps[s]
        if kind != "join":
            spot = self.sets[unit.set]
            start = unit.starts[s]
            if kind == "cut":
                start = start + self.place.code(group) * size
            kept = self.own(unit, start, size)
            total = kept[...]
            for turn in range(2 ** len(group) - 1):
                total = total + self.land[spot, land + turn * size : land + (turn + 1) * size, :]
            kept[...] = total
        if s + 1 == unit.returns:
            self.store(unit).start()
        if s == unit.returns:
            self.store(unit).wait()


LOW = jnp.bfloat16
FULL = jnp.float32


def dot_nn(left, right):
    return lax.dot_general(left, right, (((1,), (0,)), ((), ())), preferred_element_type=FULL)


def dot_nt(left, right):
    return lax.dot_general(left, right, (((1,), (1,)), ((), ())), preferred_element_type=FULL)


def dot_tn(left, right):
    return lax.dot_general(left, right, (((0,), (0,)), ((), ())), preferred_element_type=FULL)


def loop(count, body):
    def step(i, carry):
        body(i)
        return carry

    lax.fori_loop(0, count, step, 0)


def rows_of(i, size):
    return pl.ds(pl.multiple_of(i * size, size), size)


def offset_buckets(shift):
    keys = lax.broadcasted_iota(jnp.int32, (128, 128), 0)
    queries = lax.broadcasted_iota(jnp.int32, (128, 128), 1)
    offsets = keys - queries + 128 * shift
    distance = jnp.abs(offsets)
    distant = jnp.full((128, 128), 8, jnp.int32)
    for limit in THRESHOLDS:
        distant = distant + jnp.where(distance >= limit, 1, 0)
    buckets = jnp.where(distance < 8, distance, distant)
    return buckets + jnp.where(offsets > 0, 16, 0)


NEAR = ((-1, range(1, 16)), (0, range(32)), (1, range(17, 32)))


def fill_bias(bias, table, head, count):
    ids = [offset_buckets(shift) for shift, _ in NEAR]
    for side in range(count):
        for spot, (shift, members) in enumerate(NEAR):
            block = jnp.zeros((128, 128), FULL)
            for b in members:
                block = jnp.where(ids[spot] == b, table[head + side, b], block)
            bias[side, spot] = block


def bias_strip(bias, side, table, head, jb, blocks):
    parts = []
    for ib in range(blocks):
        shift = jb - ib
        if abs(shift) <= 1:
            parts.append(bias[side, shift + 1])
        else:
            parts.append(jnp.full((128, 128), table[head, 31 if shift > 0 else 15], FULL))
    return jnp.concatenate(parts, axis=1)


def forward_kernel(
    tokens, lengths, wq, wk, wv, wm, wi, wo, gain1, gain2, table,
    q_out, k_out, v_out, ho_out, n1_out, n2_out, h1_out, act_out, slope_out, result_out, lse_out, pooled_out, sums_out,
    x_s, wq_s, wk_s, wv_s, wm_s, wi_s, wo_s, q_s, k_s, v_s, ho_s, n1_s, n2_s, h1_s, act_s, slope_s, result_s, total_s,
    score_s, prob_s, bias_s, in_sem, out_sem,
):
    count, width = tokens.shape
    rows, seq = lengths.shape[0], tokens.shape[0] // lengths.shape[0]
    heads = table.shape[0]
    size = width // heads
    hidden = wi.shape[1]
    parts = hidden // width
    loads = [
        pltpu.make_async_copy(source, target, in_sem.at[i])
        for i, (source, target) in enumerate(
            [(tokens, x_s), (wq, wq_s), (wk, wk_s), (wv, wv_s), (wm, wm_s), (wi, wi_s), (wo, wo_s)]
        )
    ]
    for load in loads:
        load.start()
    stores = []

    def store(source, target):
        copy = pltpu.make_async_copy(source, target, out_sem.at[len(stores)])
        copy.start()
        stores.append(copy)

    block = 256
    loads[0].wait()

    def norm1(i):
        at = rows_of(i, block)
        x = x_s[at, :].astype(FULL)
        scale = lax.rsqrt(jnp.mean(x * x, -1, keepdims=True) + EPSILON)
        n1_s[at, :] = (x * scale * gain1[...].reshape(1, width)).astype(LOW)

    loop(count // block, norm1)
    store(n1_s, n1_out)
    for i, (w_s, p_s, p_out) in enumerate(((wq_s, q_s, q_out), (wk_s, k_s, k_out), (wv_s, v_s, v_out))):
        loads[1 + i].wait()

        def project(m, w_s=w_s, p_s=p_s):
            at = rows_of(m, 512)
            p_s[at, :] = dot_nn(n1_s[at, :], w_s[...]).astype(LOW)

        loop(count // 512, project)
        store(p_s, p_out)
    blocks = seq // 128
    lanes = lax.broadcasted_iota(jnp.int32, (seq, 2 * size), 1)
    keys = lax.broadcasted_iota(jnp.int32, (128, seq), 0)

    def attend(step):
        pair = lax.div(step, jnp.int32(rows))
        row = lax.rem(step, jnp.int32(rows))
        at = rows_of(row, seq)
        here = rows_of(pair, 2 * size)
        limit = lengths[row]

        @pl.when(row == 0)
        def _():
            fill_bias(bias_s, table, pair * 2, 2)

        q, k = q_s[at, here], k_s[at, here]
        vt = v_s[at, here].T
        found = []
        for side in range(2):
            head = pair * 2 + side
            chosen = jnp.where((lanes >= size) == (side == 1), q, jnp.zeros_like(q))
            score_s[side] = dot_nt(k, chosen)
        for side in range(2):
            head = pair * 2 + side
            top = jnp.full((1, seq), NEGATIVE, FULL)
            for jb in range(blocks):
                strip = score_s[side, jb * 128 : (jb + 1) * 128, :] + bias_strip(bias_s, side, table, head, jb, blocks)
                strip = jnp.where(keys + jb * 128 < limit, strip, NEGATIVE)
                score_s[side, jb * 128 : (jb + 1) * 128, :] = strip
                top = jnp.maximum(top, jnp.max(strip, 0, keepdims=True))
            mass = jnp.zeros((1, seq), FULL)
            for jb in range(blocks):
                strip = jnp.exp(score_s[side, jb * 128 : (jb + 1) * 128, :] - top)
                mass = mass + jnp.sum(strip, 0, keepdims=True)
                prob_s[side, jb * 128 : (jb + 1) * 128, :] = strip.astype(LOW)
            lse_out[row * heads + head] = top + jnp.log(mass)
            found.append(dot_nn(vt[side * size : (side + 1) * size, :], prob_s[side]) / mass)
        ho_s[at, here] = jnp.concatenate(found, 0).T.astype(LOW)

    loop(rows * (heads // 2), attend)
    store(ho_s, ho_out)
    loads[4].wait()

    def mix(i):
        at = rows_of(i, block)
        h1 = x_s[at, :].astype(FULL) + dot_nn(ho_s[at, :], wm_s[...])
        h1_s[at, :] = h1
        scale = lax.rsqrt(jnp.mean(h1 * h1, -1, keepdims=True) + EPSILON)
        n2_s[at, :] = (h1 * scale * gain2[...].reshape(1, width)).astype(LOW)

    loop(count // block, mix)
    store(h1_s, h1_out)
    store(n2_s, n2_out)
    loads[5].wait()
    loads[6].wait()
    lane = lax.broadcasted_iota(jnp.int32, (16, count), 1)
    which = lax.broadcasted_iota(jnp.int32, (16, count), 0)
    marks = jnp.zeros((16, count), FULL)
    for row in range(rows):
        inside = (which == row) & (lane >= row * seq) & (lane < row * seq + lengths[row])
        marks = jnp.where(inside, 1.0, marks)
    marks = marks.astype(LOW)

    for part in range(parts):
        columns = pl.ds(part * width, width)

        def feed(i, part=part, columns=columns):
            at = rows_of(i, block)
            inner = dot_nn(n2_s[at, :], wi_s[:, columns])
            share = 0.5 + 0.5 * lax.erf(inner * 0.7071067811865476)
            act = (inner * share).astype(LOW)
            act_s[at, columns] = act
            slope = share + inner * (jnp.exp(inner * inner * -0.5) * 0.3989422804014327)
            slope_s[at, columns] = slope.astype(LOW)
            more = dot_nn(act, wo_s[columns, :])
            if part == 0:
                total_s[at, :] = h1_s[at, :] + more
            elif part < parts - 1:
                total_s[at, :] = total_s[at, :] + more
            else:
                output = total_s[at, :] + more
                total_s[at, :] = output
                result_s[at, :] = output.astype(LOW)

        loop(count // block, feed)
        store(act_s.at[:, columns], act_out.at[:, columns])
        sums = dot_nn(marks, act_s[:, columns])
        for row in range(rows):
            sums_out[part * rows + row : part * rows + row + 1, :] = sums[row : row + 1] / lengths[row].astype(FULL)
        store(slope_s.at[:, columns], slope_out.at[:, columns])
    store(result_s, result_out)
    slots = lax.broadcasted_iota(jnp.int32, (seq, 1), 0)
    for row in range(rows):
        kept = jnp.where(slots < lengths[row], total_s[row * seq : (row + 1) * seq, :], 0.0)
        pooled_out[row : row + 1, :] = jnp.sum(kept, 0, keepdims=True) / lengths[row].astype(FULL)
    for copy in stores:
        copy.wait()


def forward(tokens, lengths, wq, wk, wv, wm, wi, wo, gain1, gain2, table):
    count, width = tokens.shape
    hidden = wi.shape[1]
    rows = lengths.shape[0]
    heads = table.shape[0]
    seq = count // rows
    shape = jax.ShapeDtypeStruct
    any_spec = pl.BlockSpec(memory_space=pl.ANY)
    vmem_spec = pl.BlockSpec(memory_space=pltpu.VMEM)
    smem_spec = pl.BlockSpec(memory_space=pltpu.SMEM)
    low = shape((count, width), LOW)
    wide = shape((count, hidden), LOW)
    weights = [pltpu.VMEM(w.shape, LOW) for w in (wq, wk, wv, wm, wi, wo)]
    narrow_s = pltpu.VMEM((count, width), LOW)
    full_s = pltpu.VMEM((count, width), FULL)
    wide_s = pltpu.VMEM((count, hidden), LOW)
    return pl.pallas_call(
        forward_kernel,
        out_shape=[low, low, low, low, low, low, shape((count, width), FULL), wide, wide, low]
        + [shape((rows * heads, 1, seq), FULL), shape((rows, width), FULL)]
        + [shape((hidden // width * rows, width), FULL)],
        in_specs=[any_spec, smem_spec] + [any_spec] * 6 + [vmem_spec] * 2 + [smem_spec],
        out_specs=[any_spec] * 10 + [vmem_spec] * 3,
        scratch_shapes=[narrow_s]
        + weights
        + [narrow_s] * 6
        + [full_s, wide_s, wide_s, narrow_s, full_s]
        + [
            pltpu.VMEM((2, seq, seq), FULL),
            pltpu.VMEM((2, seq, seq), LOW),
            pltpu.VMEM((2, 3, 128, 128), FULL),
            pltpu.SemaphoreType.DMA((7,)),
            pltpu.SemaphoreType.DMA((24,)),
        ],
        compiler_params=pltpu.CompilerParams(vmem_limit_bytes=62 * 2**20),
    )(tokens, lengths, wq, wk, wv, wm, wi, wo, gain1, gain2, table)


def norm_back(values, gain, dy):
    scale = lax.rsqrt(jnp.mean(values * values, -1, keepdims=True) + EPSILON)
    along = values * scale
    dscaled = gain * dy
    mean = jnp.mean(along * dscaled, -1, keepdims=True)
    return scale * (dscaled - along * mean), jnp.sum(along * dy, 0, keepdims=True)


def contrast(queries, documents, doc_groups, positives):
    count = doc_groups.shape[1]
    precise = functools.partial(lax.dot_general, precision=HIGHEST, preferred_element_type=FULL)
    rates = [lax.rsqrt(jnp.sum(p * p, -1, keepdims=True) + EPSILON) for p in (queries, documents)]
    unit = [p * rate for p, rate in zip((queries, documents), rates)]
    scores = SCALE * precise(unit[0], unit[1], (((1,), (1,)), ((), ())))
    indices = lax.broadcasted_iota(jnp.int32, (count, count), 0)
    chosen = jnp.where(positives == indices, 1.0, 0.0).T
    query_groups = jnp.sum(chosen * doc_groups.astype(FULL), 1, keepdims=True)
    masked = jnp.where(query_groups == doc_groups.astype(FULL), scores, NEGATIVE)
    highest = jnp.max(masked, 1, keepdims=True)
    weights = jnp.exp(masked - highest)
    mass = jnp.sum(weights, 1, keepdims=True)
    matched = jnp.sum(jnp.where(chosen > 0.5, scores, 0.0), 1, keepdims=True)
    loss = jnp.sum(highest + jnp.log(mass) - matched, 0, keepdims=True) / count
    dscore = weights / mass - chosen
    dunit = (
        SCALE * precise(dscore, unit[1], (((1,), (0,)), ((), ()))),
        SCALE * precise(dscore, unit[0], (((0,), (0,)), ((), ()))),
    )
    dpooled = [rate * (d - u * jnp.sum(u * d, -1, keepdims=True)) for rate, d, u in zip(rates, dunit, unit)]
    return loss, dpooled


def is_early(sizes, rows):
    return sizes["tower"] * sizes["batch"] * rows <= 128


def make_units(sizes, rows, hidden, width):
    groups = bit_groups(sizes)
    early = is_early(sizes, rows)
    parts = hidden // width
    items, blocks = [], []

    def add(matrix, row, first, item):
        blocks.extend((matrix, row, col, item) for col in range(first, first + width, UNIT_COLS))

    def outer():
        for part in range(parts):
            items.append(("outer", 2.6))
            add(0, part * width, 0, len(items))

    if early:
        outer()
        items.append(("hop", 2.0))
    else:
        items.append(("hop", 12.0))
    items.append(("loss", 4.0))
    if not early:
        outer()
    for part in range(parts):
        items.append(("inner", 6.4))
        add(1, 0, part * width, len(items))
    items.append(("mix", 4.0))
    items.append(("mixed", 1.8))
    first = len(items)
    items += [("attend", 2.5)] * 24
    add(5, 0, 0, first + 4)
    for turn in range(3):
        item = first + 8 * turn + 10 if turn < 2 else first + 25
        blocks.extend((matrix, 0, turn * UNIT_COLS, item) for matrix in range(2, 5))
    items.append(("flush", 3.0))
    items += [("input", 1.6)] * 4
    units = []
    for i, (matrix, row, col, item) in enumerate(blocks):
        kind = PATTERN[i % len(PATTERN)]
        units.append(Unit(matrix, row, width // 2, col, UNIT_COLS, kind, groups[kind], item))
    return units, items


def backward_kernel(
    sizes, units, order, counts,
    cot, pooled, sums, lengths, doc_groups, positives, act, slope, wo, wi, n2, h1, ho, q, k, v, n1, tokens, lse,
    wq, wk, wv, wm, gain1, gain2, table,
    *refs,
):
    grads, outs = refs[:6], refs[6:12]
    tokens_grad, u_out, small_out, loss_out, dpooled_out = refs[12:17]
    (
        narrow, square, staged, full, bias_s, near_s, sums_s, every_s, every_u, thirds_s, core_land, small_land, kept, land,
        in_sem, chunk_sem, stage_sem, core_send, core_recv, last_sem, hop_send, hop_recv, small_send, small_recv,
        send_sem, recv_sem, load_sem, store_sem, final_send, final_recv,
    ) = refs[17:]
    count, width = narrow.shape[1:]
    rows = lengths.shape[0]
    seq = count // rows
    heads = table.shape[0]
    size = width // heads
    parts = wo.shape[0] // width
    block = 256
    place = Place(sizes)
    names = place.names
    tower, batch = place.at["tower"], place.at["batch"]
    exchange = Exchange(
        units, place, counts, grads, kept, land, outs, (send_sem, recv_sem, load_sem, store_sem, final_send, final_recv)
    )
    cot_s, n2_s, dout_s = narrow.at[8], narrow.at[9], narrow.at[10]
    act_s = [narrow.at[part] for part in range(parts)]
    slope_s = [narrow.at[parts + part] for part in range(parts)]
    h1_s, sum_s = full.at[0], full.at[1]
    loads = {}

    def load(name, source, target):
        copy = pltpu.make_async_copy(source, target, in_sem.at[len(loads)])
        copy.start()
        loads[name] = copy

    def cut(part):
        return pl.ds(part * width, width)

    load("cot", cot, cot_s)
    for part in range(parts):
        load("act%d" % part, act.at[:, cut(part)], act_s[part])
    for part in range(parts):
        load("wo%d" % part, wo.at[cut(part), :], square.at[part])
    load("n2", n2, n2_s)
    for part in range(parts):
        load("slope%d" % part, slope.at[:, cut(part)], slope_s[part])

    def wi_chunk(part):
        return pltpu.make_async_copy(wi.at[:, cut(part)], square.at[parts + part % 2], chunk_sem.at[part])

    for part in range(2):
        wi_chunk(part).start()
    load("h1", h1, h1_s)

    early = is_early(sizes, rows)

    item = 0
    stage_of = {}

    def act_on(actions):
        for action, u, s in actions:
            if action == "go":
                if s == 0:
                    exchange_ready(u)
                exchange.go(u, s)
            else:
                exchange.serve(u, s)

    def exchange_ready(u):
        unit = units[u]
        key = (unit.matrix, unit.row // width if unit.matrix == 0 else unit.col // width)
        if key in stage_of:
            stage_of.pop(key)()

    def between():
        nonlocal item
        act_on(order[item])
        item += 1

    half = width // 2
    own_half = pl.ds(pl.multiple_of(tower * half, 8), half)
    other_half = pl.ds(pl.multiple_of((1 - tower) * half, 8), half)
    core_bit = next(bit for bit, name in enumerate(names) if name[0] == "tower")

    def thirds_of(square_ref):
        return [square_ref.at[:, pl.ds(i * UNIT_COLS, UNIT_COLS)] for i in range(3)]

    def core_copies(turn, pieces):
        return [
            pltpu.make_async_remote_copy(
                src_ref=piece.at[other_half, :],
                dst_ref=core_land.at[turn % 2, i],
                send_sem=core_send.at[turn % 2, i],
                recv_sem=core_recv.at[turn % 2, i],
                device_id=place.partner((core_bit,)),
                device_id_type=MESH,
            )
            for i, piece in enumerate(pieces)
        ]

    def out_copies(turn, pieces, targets):
        return [
            pltpu.make_async_copy(piece.at[own_half, :], target.at[own_half, :], stage_sem.at[turn, i])
            for i, (piece, target) in enumerate(zip(pieces, targets))
        ]

    def core_send_off(turn, pieces):
        for copy in core_copies(turn, pieces):
            copy.start()

    def core_add(turn, pieces, targets):
        for copy in core_copies(turn, pieces):
            copy.wait()
        for i, piece in enumerate(pieces):
            piece[own_half, :] = piece[own_half, :] + core_land[turn % 2, i]
        for copy in out_copies(turn, pieces, targets):
            copy.start()

    def core_done(turn, pieces, targets):
        for copy in out_copies(turn, pieces, targets):
            copy.wait()

    sent = []

    def settle():
        if sent:
            key, turn, pieces, targets = sent.pop()
            core_add(turn, pieces, targets)
            stage_of[key] = functools.partial(core_done, turn, pieces, targets)

    def stage(turn, matrix, part, value, target):
        key = (matrix, part)
        last = [old for old, spot in staged_last.items() if spot == turn % 3]
        for old in last:
            staged_last.pop(old)
            if old in stage_of:
                stage_of.pop(old)()
        staged[turn % 3] = value
        settle()
        pieces = thirds_of(staged.at[turn % 3])
        core_send_off(turn, pieces)
        sent.append((key, turn, pieces, thirds_of(target)))
        staged_last[key] = turn % 3

    staged_last = {}

    hops = gather_groups(sizes)
    every_s[tower, batch] = pooled[...]
    if early:
        every_u[tower, batch] = sums[...]
    deltas = set()
    for group in list(bit_groups(sizes).values()) + [hops]:
        for bits in group:
            deltas.update(flips_of(bits))
    barrier = pltpu.get_barrier_semaphore()
    for flips in sorted(deltas):
        pl.semaphore_signal(barrier, inc=1, device_id=place.partner(flips), device_id_type=MESH)
    pl.semaphore_wait(barrier, len(deltas))

    def hop(h, kind=0):
        group = hops[h]
        masks = [names[bit] for bit in group]
        every = (every_s, every_u)[kind]
        if masks[0][0] == "tower":
            held = every.at[tower]
        else:
            mask = masks[0][1]
            held = every.at[tower, pl.ds(lax.div(batch, jnp.int32(mask)) * mask, mask)]
        return [
            pltpu.make_async_remote_copy(
                src_ref=held,
                dst_ref=held,
                send_sem=hop_send.at[h, 3 * kind + turn],
                recv_sem=hop_recv.at[h, 3 * kind + turn],
                device_id=place.partner(flips),
                device_id_type=MESH,
            )
            for turn, flips in enumerate(flips_of(group))
        ]

    def outer(part, right):
        loads["act%d" % part].wait()
        stage(part, 0, part, dot_tn(act_s[part][...], right[...]), grads[0].at[cut(part), :])

    for copy in hop(0):
        copy.start()
    served = 0
    if early:
        loads["cot"].wait()
        for part in range(parts):
            outer(part, cot_s)
            if part >= 1 and served < len(hops) - 1:
                for copy in hop(served):
                    copy.wait()
                served += 1
                for copy in hop(served):
                    copy.start()
            between()
    while served < len(hops):
        for copy in hop(served):
            copy.wait()
        served += 1
        if served < len(hops):
            for copy in hop(served):
                copy.start()
    settle()
    between()

    total = rows * sizes["batch"]
    for t in range(2):
        for b in range(sizes["batch"]):
            first = t * total + b * rows
            staged[3, first : first + rows, :] = every_s[t, b]
    loss, dpooled = contrast(
        staged[3, 0:total, :], staged[3, total : 2 * total, :], doc_groups[...], positives[...]
    )
    loss_out[...] = loss
    mine = jnp.where(tower == 0, dpooled[0], dpooled[1])
    ids = lax.broadcasted_iota(jnp.int32, (mine.shape[0], 1), 0)
    spread = [
        jnp.sum(jnp.where(ids == batch * rows + row, mine, 0.0), 0, keepdims=True) / lengths[row].astype(FULL)
        for row in range(rows)
    ]
    dpooled_out[0:total, :] = dpooled[0]
    dpooled_out[total : 2 * total, :] = dpooled[1]
    if early:
        for copy in hop(0, 1):
            copy.start()
    else:
        loads["cot"].wait()

    def full_dout(row, i):
        at = pl.ds(pl.multiple_of(row * seq + i * block, block), block)
        slot = lax.broadcasted_iota(jnp.int32, (block, 1), 0) + i * block
        return at, cot_s[at, :].astype(FULL) + jnp.where(slot < lengths[row], spread[row], 0.0)

    for row in range(rows):

        def round_dout(i, row=row):
            at, dout = full_dout(row, i)
            dout_s[at, :] = dout.astype(LOW)

        loop(seq // block, round_dout)
    between()

    if not early:
        for part in range(parts):
            outer(part, dout_s)
            between()
    for name, source, target in (("q", q, 0), ("k", k, 1), ("v", v, 2), ("n1", n1, 3)):
        load(name, source, narrow.at[target])
    loads["n2"].wait()
    for part in range(parts):
        loads["slope%d" % part].wait()
        loads["wo%d" % part].wait()
        wi_chunk(part).wait()

        def inner_back(i, part=part):
            at = rows_of(i, block)
            dact = dot_nt(dout_s[at, :], square[part])
            dinner = (slope_s[part][at, :].astype(FULL) * dact).astype(LOW)
            slope_s[part][at, :] = dinner
            more = dot_nt(dinner, square[parts + part % 2])
            sum_s[at, :] = more if part == 0 else sum_s[at, :] + more

        loop(count // block, inner_back)
        if part + 2 < parts:
            wi_chunk(part + 2).start()
        stage(parts + part, 1, part, dot_tn(n2_s[...], slope_s[part][...]), grads[1].at[:, cut(part)])
        if early and part < len(hops):
            for copy in hop(part, 1):
                copy.wait()
            if part + 1 < len(hops):
                for copy in hop(part + 1, 1):
                    copy.start()
        between()
    if early:
        u_copy = pltpu.make_async_copy(every_u, u_out, last_sem.at[1])
        u_copy.start()
    load("ho", ho, narrow.at[9])
    for name, source, target in (("wm", wm, 0), ("wq", wq, 1), ("wk", wk, 2), ("wv", wv, 3)):
        load(name, source, square.at[target])
    small_out[...] = jnp.zeros_like(small_out)
    loads["h1"].wait()
    loads["wm"].wait()
    q_s, k_s, v_s, n1_s = (narrow.at[i] for i in range(4))
    dh_s, dq_s, dk_s, dv_s = (narrow.at[i] for i in range(4, 8))

    for row in range(rows):

        def mix_back(i, row=row):
            at, dout = full_dout(row, i)
            dv, dgain = norm_back(h1_s[at, :], gain2[...].reshape(1, width), sum_s[at, :])
            dh1 = dout + dv
            h1_s[at, :] = dh1
            small_out[1:2, :] = small_out[1:2, :] + dgain
            da = dh1.astype(LOW)
            cot_s[at, :] = da
            dh_s[at, :] = dot_nt(da, square[0]).astype(LOW)

        loop(seq // block, mix_back)
    settle()
    between()
    loads["ho"].wait()
    third_refs = [thirds_s.at[i] for i in range(3)]
    third_targets = [thirds_of(grads[5])] + [
        [grads[2 + i].at[:, pl.ds(turn * UNIT_COLS, UNIT_COLS)] for i in range(3)] for turn in range(3)
    ]
    first_turn = 2 * parts
    for i in range(3):
        thirds_s[i] = dot_tn(narrow[9], cot_s[:, pl.ds(i * UNIT_COLS, UNIT_COLS)])
    core_send_off(first_turn, third_refs)
    between()
    for done in list(stage_of.values()):
        done()
    stage_of.clear()
    load("x", tokens, narrow.at[9])
    for name in ("q", "k", "v", "n1"):
        loads[name].wait()

    blocks = seq // 128
    lanes = lax.broadcasted_iota(jnp.int32, (seq, 2 * size), 1)
    keys = lax.broadcasted_iota(jnp.int32, (128, seq), 0)
    first_item = item
    steps = rows * (heads // 2)

    def between_at(step, side):
        for index in range(steps):
            actions = order[first_item + 2 * index + side] if 2 * index + side < 24 else []
            if actions:
                pl.when(step == index)(functools.partial(act_on, actions))

    per_turn = 2 * rows

    def third(turn):
        for i, d_s in enumerate((dq_s, dk_s, dv_s)):
            thirds_s[i] = dot_tn(n1_s[...], d_s[:, pl.ds(turn * UNIT_COLS, UNIT_COLS)])
        core_send_off(first_turn + 1 + turn, third_refs)

    def third_add(turn):
        core_add(first_turn + 1 + turn, third_refs, third_targets[1 + turn])

    def third_done(turn):
        core_done(first_turn + 1 + turn, third_refs, third_targets[1 + turn])

    def attend_back(step):
        pair = lax.div(step, jnp.int32(rows))
        row = lax.rem(step, jnp.int32(rows))
        at = rows_of(row, seq)
        here = rows_of(pair, 2 * size)
        limit = lengths[row]
        for turn in range(-1, steps // per_turn - 1):
            ready = per_turn * (turn + 1) if turn >= 0 else 1
            pl.when(step == ready)(functools.partial(third_add, turn))
            pl.when(step == ready + 1)(functools.partial(third_done, turn))

        @pl.when(row == 0)
        def _():
            near_s[...] = jnp.zeros_like(near_s)
            fill_bias(bias_s, table, pair * 2, 2)

        qp, kp, vp, dp = q_s[at, here], k_s[at, here], v_s[at, here], dh_s[at, here]
        nothing = jnp.zeros_like(qp)
        kt = kp.T
        dq, dk, dv = [], [], []
        score_s = [staged.at[side, 0:seq, 0:seq] for side in range(2)]
        dprob_s = [staged.at[2 + side, 0:seq, 0:seq] for side in range(2)]
        prob_s = [narrow.at[8, side * seq : (side + 1) * seq, 0:seq] for side in range(2)]
        dscore_s = [narrow.at[10, side * seq : (side + 1) * seq, 0:seq] for side in range(2)]
        for side in range(2):
            chosen = (lanes >= size) == (side == 1)
            score_s[side][...] = dot_nt(kp, jnp.where(chosen, qp, nothing))
            dprob_s[side][...] = dot_nt(vp, jnp.where(chosen, dp, nothing))
        for side in range(2):
            head = pair * 2 + side
            level = lse[row * heads + head]
            delta = jnp.zeros((1, seq), FULL)
            for jb in range(blocks):
                some = slice(jb * 128, (jb + 1) * 128)
                strip = score_s[side][some, :] + bias_strip(bias_s, side, table, head, jb, blocks)
                strip = jnp.where(keys + jb * 128 < limit, strip, NEGATIVE)
                prob = jnp.exp(strip - level)
                prob_s[side][some, :] = prob.astype(LOW)
                score_s[side][some, :] = prob
                delta = delta + jnp.sum(prob * dprob_s[side][some, :], 0, keepdims=True)
            for jb in range(blocks):
                some = slice(jb * 128, (jb + 1) * 128)
                dscore = score_s[side][some, :] * (dprob_s[side][some, :] - delta)
                dscore_s[side][some, :] = dscore.astype(LOW)
                for ib in range(blocks):
                    spot = min(max(jb - ib, -2), 2) + 2
                    near_s[side, spot] = near_s[side, spot] + dscore[:, ib * 128 : (ib + 1) * 128]
            dk.append(dot_nn(dscore_s[side][...], qp))
            dv.append(dot_nn(prob_s[side][...], dp))
            dq.append(dot_nn(kt[side * size : (side + 1) * size, :], dscore_s[side][...]))
            if side == 0:
                between_at(step, 0)
        first = lanes < size
        dk_s[at, here] = jnp.where(first, dk[0], dk[1]).astype(LOW)
        dv_s[at, here] = jnp.where(first, dv[0], dv[1]).astype(LOW)
        dq_s[at, here] = jnp.concatenate(dq, 0).T.astype(LOW)

        @pl.when(row == rows - 1)
        def _():
            ids = [offset_buckets(shift) for shift, _ in NEAR]
            for side in range(2):
                bucket = lax.broadcasted_iota(jnp.int32, (1, 128), 1)
                found = jnp.zeros((1, 128), FULL)
                for spot, (shift, members) in enumerate(NEAR):
                    total = near_s[side, spot + 1]
                    for b in members:
                        share = jnp.sum(jnp.where(ids[spot] == b, total, 0.0), 0, keepdims=True)
                        found = found + jnp.where(bucket == b, jnp.sum(share, 1, keepdims=True), 0.0)
                for spot, b in ((0, 15), (4, 31)):
                    share = jnp.sum(near_s[side, spot], 0, keepdims=True)
                    found = found + jnp.where(bucket == b, jnp.sum(share, 1, keepdims=True), 0.0)
                sums_s[pair * 2 + side] = found

        for turn in range(steps // per_turn):
            pl.when(step == per_turn * (turn + 1) - 1)(functools.partial(third, turn))
        between_at(step, 1)

    loop(steps, attend_back)
    item = first_item + 24
    for head in range(heads):
        small_out[8 + head : 9 + head, 0:128] = sums_s[head]

    third_add(steps // per_turn - 1)
    for i in range(3):
        stage_of[(2 + i, steps // per_turn - 1)] = lambda: None
    between()
    for name in ("wq", "wk", "wv", "x"):
        loads[name].wait()

    def input_back(i):
        at = rows_of(i, block)
        dn1 = dot_nt(dq_s[at, :], square[1]) + dot_nt(dk_s[at, :], square[2]) + dot_nt(dv_s[at, :], square[3])
        dv, dgain = norm_back(narrow[9, at, :].astype(FULL), gain1[...].reshape(1, width), dn1)
        small_out[0:1, :] = small_out[0:1, :] + dgain
        cot_s[at, :] = (h1_s[at, :] + dv).astype(LOW)

    for i in range(4):
        share = count // block // 4
        loop(share, lambda j, i=i: input_back(j + i * share))
        if i == 0:
            third_done(steps // per_turn - 1)
        if i < 3:
            between()
    last = pltpu.make_async_copy(cot_s, tokens_grad, last_sem.at[0])
    last.start()

    def small_copy(bit):
        return pltpu.make_async_remote_copy(
            src_ref=small_out,
            dst_ref=small_land.at[bit],
            send_sem=small_send.at[bit],
            recv_sem=small_recv.at[bit],
            device_id=place.partner((bit,)),
            device_id_type=MESH,
        )

    small_copy(0).start()
    actions = order[item]
    for bit in range(len(names)):
        act_on(actions[len(actions) * bit // (len(names) + 1) : len(actions) * (bit + 1) // (len(names) + 1)])
        small_copy(bit).wait()
        small_out[...] = small_out[...] + small_land[bit]
        if bit + 1 < len(names):
            small_copy(bit + 1).start()
    act_on(actions[len(actions) * len(names) // (len(names) + 1) :])
    last.wait()
    if early:
        u_copy.wait()
    for done in stage_of.values():
        done()


def backward(
    sizes, cot, pooled, sums, lengths, doc_groups, positives, act, slope, wo, wi, n2, h1, ho, q, k, v, n1, tokens, lse,
    wq, wk, wv, wm, gain1, gain2, table,
):
    count, width = cot.shape
    hidden = wo.shape[0]
    rows = lengths.shape[0]
    heads = table.shape[0]
    total = doc_groups.shape[0]
    names = bit_names(sizes)
    shape = jax.ShapeDtypeStruct
    early = is_early(sizes, rows)
    gathered = shape((2, sizes["batch"]) + sums.shape if early else (8, 128), FULL)
    units, items = make_units(sizes, rows, hidden, width)
    counts = set_counts(sizes)
    order, _ = plan(units, names, counts, [time for _, time in items])
    steps = max(len(unit.steps) for unit in units)
    sets = sum(counts.values())
    any_spec = pl.BlockSpec(memory_space=pl.ANY)
    vmem_spec = pl.BlockSpec(memory_space=pltpu.VMEM)
    smem_spec = pl.BlockSpec(memory_space=pltpu.SMEM)
    squares = [shape((hidden, width), FULL), shape((width, hidden), FULL)] + [shape((width, width), FULL)] * 4
    hops = len(gather_groups(sizes))
    dma = pltpu.SemaphoreType.DMA
    return pl.pallas_call(
        functools.partial(backward_kernel, sizes, units, order, counts),
        out_shape=squares + squares
        + [shape((count, width), LOW), gathered, shape((24, width), FULL), shape((1, 1), FULL)]
        + [shape((2 * total, width), FULL)],
        in_specs=[any_spec, vmem_spec, vmem_spec, smem_spec, vmem_spec, vmem_spec]
        + [any_spec] * 12
        + [vmem_spec]
        + [any_spec] * 4
        + [vmem_spec] * 2
        + [smem_spec],
        out_specs=[any_spec] * 14 + [vmem_spec] * 3,
        scratch_shapes=[
            pltpu.VMEM((11, count, width), LOW),
            pltpu.VMEM((6, width, width), LOW),
            pltpu.VMEM((4, width, width), FULL),
            pltpu.VMEM((2, count, width), FULL),
            pltpu.VMEM((2, 3, 128, 128), FULL),
            pltpu.VMEM((2, 5, 128, 128), FULL),
            pltpu.VMEM((heads, 1, 128), FULL),
            pltpu.VMEM((2, sizes["batch"], rows, width), FULL),
            pltpu.VMEM(gathered.shape, FULL),
            pltpu.VMEM((3, width, UNIT_COLS), FULL),
            pltpu.VMEM((2, 3, width // 2, UNIT_COLS), FULL),
            pltpu.VMEM((len(names), 24, width), FULL),
            pltpu.VMEM((sets, max(unit.steps[0][2] for unit in units), UNIT_COLS), FULL),
            pltpu.VMEM((sets, max(unit.land for unit in units), UNIT_COLS), FULL),
            dma((32,)),
            dma((8,)),
            dma((16, 3)),
            dma((2, 3)),
            dma((2, 3)),
            dma((2,)),
            dma((hops, 6)),
            dma((hops, 6)),
            dma((len(names),)),
            dma((len(names),)),
            dma((sets, steps, 3)),
            dma((sets, steps, 3)),
            dma((sets,)),
            dma((sets,)),
            dma((len(units),)),
            dma((len(units),)),
        ],
        compiler_params=pltpu.CompilerParams(
            collective_id=0, has_side_effects=True, vmem_limit_bytes=int(63.5 * 2**20)
        ),
    )(
        cot, pooled, sums, lengths, doc_groups.reshape(1, total), positives.reshape(1, total), act, slope, wo, wi, n2, h1,
        ho, q, k, v, n1, tokens, lse, wq, wk, wv, wm, gain1, gain2, table,
    )


OUT_ROWS = 256


def hand_out_kernel(blocks, count, heads, early, *refs):
    sources, (u_in, small, loss_in, dpooled) = refs[:count], refs[count : count + 4]
    targets = refs[count + 4 : 2 * count + 4]
    gain1, gain2, table, loss = refs[2 * count + 4 : 2 * count + 8]
    full, low, u_s, sums_s, in_sem, out_sem = refs[2 * count + 8 :]
    width = full.shape[2]
    loads, stores = [], []
    if early:
        u_load = pltpu.make_async_copy(u_in, u_s, in_sem.at[len(blocks)])
        u_load.start()
    for i, (array, spot, row, col) in enumerate(blocks):
        at = (pl.ds(row, OUT_ROWS), pl.ds(col, width))
        held = (low if sources[array].dtype == LOW else full).at[spot]
        loads.append(pltpu.make_async_copy(sources[array].at[at], held, in_sem.at[i]))
        stores.append(pltpu.make_async_copy(held, targets[array].at[at], out_sem.at[i]))
    for load in loads:
        load.start()
    gain1[...] = small[0]
    gain2[...] = small[1]
    table[...] = small[8 : 8 + heads, 0 : table.shape[1]]
    loss[...] = loss_in[...]
    if early:
        u_load.wait()
        towers, places, most, _ = u_s.shape
        parts = targets[0].shape[0] // width
        rows = most // parts
        for part in range(parts):
            for t in range(towers):
                for b in range(places):
                    first = (t * places + b) * rows
                    sums_s[part, first : first + rows, :] = u_s[t, b, part * rows : (part + 1) * rows, :]
    for i, (load, store) in enumerate(zip(loads, stores)):
        load.wait()
        array, spot, row, _ = blocks[i]
        if early and array == 0:
            some = sums_s[row // width, :, row % width : row % width + OUT_ROWS]
            full[spot] = full[spot] + lax.dot_general(
                some, dpooled[...], (((0,), (0,)), ((), ())), precision=HIGHEST, preferred_element_type=FULL
            )
        store.start()
    for store in stores:
        store.wait()


def hand_out(arrays, sums, small, loss, dpooled, heads, buckets):
    width = small.shape[1]
    early = len(sums.shape) == 4
    blocks, held = [], {FULL: 0, LOW: 0}
    for i, array in enumerate(arrays):
        for col in range(0, array.shape[1], width):
            for row in range(0, array.shape[0], OUT_ROWS):
                kind = LOW if array.dtype == LOW else FULL
                blocks.append((i, held[kind], row, col))
                held[kind] += 1
    any_spec = pl.BlockSpec(memory_space=pl.ANY)
    vmem_spec = pl.BlockSpec(memory_space=pltpu.VMEM)
    shape = jax.ShapeDtypeStruct
    return pl.pallas_call(
        functools.partial(hand_out_kernel, blocks, len(arrays), heads, early),
        out_shape=[shape(a.shape, a.dtype) for a in arrays]
        + [shape((width,), FULL), shape((width,), FULL), shape((heads, buckets), FULL), shape((1, 1), FULL)],
        in_specs=[any_spec] * (len(arrays) + 1) + [vmem_spec] * 3,
        out_specs=[any_spec] * len(arrays) + [vmem_spec] * 4,
        scratch_shapes=[
            pltpu.VMEM((held[FULL], OUT_ROWS, width), FULL),
            pltpu.VMEM((held[LOW], OUT_ROWS, width), LOW),
            pltpu.VMEM(sums.shape, FULL),
            pltpu.VMEM((arrays[0].shape[0] // width, dpooled.shape[0], width) if early else (8, 128), FULL),
            pltpu.SemaphoreType.DMA((len(blocks) + 1,)),
            pltpu.SemaphoreType.DMA((len(blocks),)),
        ],
        compiler_params=pltpu.CompilerParams(vmem_limit_bytes=63 * 2**20),
    )(*arrays, sums, small, loss, dpooled)


def shards(
    tokens,
    lengths,
    doc_groups,
    positives,
    cotangent,
    w_query,
    w_key,
    w_value,
    w_mixed,
    w_inner,
    w_outer,
    gain_attn,
    gain_ffn,
    rel_table,
):
    rows = tokens.shape[1]
    count, width = rows * tokens.shape[2], tokens.shape[3]
    buckets, heads = rel_table.shape
    sizes = {axis: lax.axis_size(axis) for axis in ("tower", "batch")}
    flat = tokens.reshape(count, width)
    cot = cotangent.reshape(count, width)
    own_lengths = lengths.reshape(rows)
    table = rel_table.T
    q, k, v, ho, n1, n2, h1, act, slope, result, lse, pooled, sums = forward(
        flat, own_lengths, w_query, w_key, w_value, w_mixed, w_inner, w_outer, gain_attn, gain_ffn, table
    )
    found = backward(
        sizes, cot, pooled, sums, own_lengths, doc_groups, positives, act, slope, w_outer, w_inner, n2, h1, ho, q, k, v, n1,
        flat, lse, w_query, w_key, w_value, w_mixed, gain_attn, gain_ffn, table,
    )
    given = hand_out(found[6:13], *found[13:], heads, buckets)
    wo_grad, wi_grad, wq_grad, wk_grad, wv_grad, wm_grad, tokens_grad, gain1_grad, gain2_grad, table_grad, loss = given
    return (
        result.reshape(tokens.shape),
        pooled[None],
        loss[0, 0],
        tokens_grad.reshape(tokens.shape),
        wq_grad,
        wk_grad,
        wv_grad,
        wm_grad,
        wi_grad,
        wo_grad,
        gain1_grad,
        gain2_grad,
        table_grad.T,
    )


def solution(mesh):
    return jax.shard_map(
        shards,
        mesh=mesh,
        in_specs=(
            P("tower", "batch", None, None),
            P("tower", "batch"),
            P(),
            P(),
            P("tower", "batch", None, None),
            P(),
            P(),
            P(),
            P(),
            P(),
            P(),
            P(),
            P(),
            P(),
        ),
        out_specs=(
            P("tower", "batch", None, None),
            P("tower", "batch", None),
            P(),
            P("tower", "batch", None, None),
            P(),
            P(),
            P(),
            P(),
            P(),
            P(),
            P(),
            P(),
            P(),
        ),
        check_vma=False,
    )
```

```python
import functools

import jax
import jax.numpy as jnp
from jax import lax
from jax.experimental import pallas as pl
from jax.experimental.pallas import tpu as pltpu
from jax.sharding import PartitionSpec as P

EPSILON = 1e-06
SCALE = 50.0
NEGATIVE = -1000000000.0
THRESHOLDS = (12, 16, 23, 32, 46, 64, 91)
HIGHEST = lax.Precision.HIGHEST


MESH = pl.DeviceIdType.MESH
LINK = 46.97e3
CORE = 500e3
FLIGHT = 3.42
DEPTH = 7.40
PACE = 0.885
CLASSES = "ABCD"
PATTERN = "ACBADBCABADBACBADBCBADBAAABBBCCDAAAB"
UNIT_COLS = 256


def bit_names(sizes):
    names = []
    for axis in ("tower", "batch"):
        mask = 1
        while mask < sizes[axis]:
            names.append((axis, mask))
            mask *= 2
    return names


def set_counts(sizes):
    return {"A": 6, "B": 6, "C": 4, "D": 4} if sizes["batch"] <= 16 else {"A": 2, "B": 2, "C": 1, "D": 1}


def bit_groups(sizes):
    names = bit_names(sizes)
    rest = [k for k, name in enumerate(names) if name[0] == "batch"]
    x, y, low, high = rest[:4]
    more = [(k,) for k in rest[4:]]
    firsts = {
        "A": [(x,), (y,), (low, high)],
        "B": [(y,), (x,), (low, high)],
        "C": [(low,), (x,), (y,), (high,)],
        "D": [(low,), (y,), (x,), (high,)],
    }
    return {name: groups + more for name, groups in firsts.items()}


def flips_of(group):
    return [tuple(k for i, k in enumerate(group) if choice >> i & 1) for choice in range(1, 2 ** len(group))]


def gather_groups(sizes):
    rest = [k for k, name in enumerate(bit_names(sizes)) if name[0] == "batch"]
    groups = [tuple(rest[i : i + 2]) for i in range(0, len(rest), 2)]
    return groups + [(k,) for k, name in enumerate(bit_names(sizes)) if name[0] == "tower"]


class Place:
    def __init__(self, sizes):
        self.names = bit_names(sizes)
        self.at = {axis: lax.axis_index(axis) for axis in ("tower", "batch")}
        self.bits = [
            lax.rem(lax.div(self.at[axis], jnp.int32(mask)), jnp.int32(2)) for axis, mask in self.names
        ]

    def partner(self, flips):
        other = dict(self.at)
        for k in flips:
            axis, mask = self.names[k]
            other[axis] = other[axis] + mask * (1 - 2 * self.bits[k])
        return (other["tower"], other["batch"])

    def code(self, group, flips=()):
        total = jnp.int32(0)
        for k in group:
            total = total * 2 + (1 - self.bits[k] if k in flips else self.bits[k])
        return total


class Unit:
    def __init__(self, matrix, row, rows, col, cols, kind, groups, item):
        self.matrix, self.row, self.rows, self.col, self.cols, self.kind, self.item = matrix, row, rows, col, cols, kind, item
        self.steps = []
        size, back, land = rows, [], 0
        for group in groups:
            ways = 2 ** len(group)
            if size % (8 * ways) == 0:
                size //= ways
                self.steps.append(("cut", group, size, land))
                back.append(("join", group, size, 0))
                land += size * (ways - 1)
            else:
                for k in group:
                    self.steps.append(("whole", (k,), size, land))
                    land += size
        self.land = land
        self.returns = len(self.steps)
        self.steps += back[::-1]
        self.steps.append(("join", (0,), rows, 0))

    def place_at(self, place):
        start, stack = self.row + place.at["tower"] * self.rows, []
        self.starts = []
        for kind, group, size, _ in self.steps:
            self.starts.append(start)
            if kind == "cut":
                stack.append(start)
                start = start + place.code(group) * size
            elif kind == "join" and stack:
                start = stack.pop()


def link_use(names, group, size):
    link = size / LINK
    masks = [names[k] for k in group]
    if masks[0][0] == "tower":
        return {"core": size / CORE}
    if masks == [("batch", 4)]:
        return {"end": link}
    if masks == [("batch", 8)]:
        return {"end": link, "middle": 2 * link}
    if masks == [("batch", 4), ("batch", 8)]:
        return {"end": 3 * link, "middle": 4 * link}
    return {mask: link * (2 ** len(group) - 1) for mask in masks}


def plan(units, names, counts, items, depth=DEPTH):
    free, clock, flight, pending = {}, 0.0, [], []
    idle = {kind: [(kind, i) for i in range(counts[kind])] for kind in CLASSES}
    done, order = 0, [[] for _ in items]
    left = list(range(len(units)))

    def use(u, s):
        _, group, size, _ = units[u].steps[s]
        return link_use(names, group, size * units[u].cols * 4)

    def pump():
        nonlocal clock
        for u in left:
            if units[u].item < done and (u, 0) not in pending:
                pending.append((u, 0))
        pending.sort()
        for u, s in list(pending):
            unit = units[u]
            if s == 0 and not idle[unit.kind]:
                continue
            if any(free.get(link, 0.0) - clock > depth for link in use(u, 1 if s == 0 else s)):
                continue
            pending.remove((u, s))
            if s == 0:
                left.remove(u)
                unit.set = idle[unit.kind].pop(0)
            clock += 0.08
            end = clock
            for link, time in use(u, s).items():
                free[link] = max(clock, free.get(link, 0.0)) + time
                end = max(end, free[link])
            flight.append((end + FLIGHT, u, s))
            order[done - 1].append(("go", u, s))

    while left or flight or pending or done < len(items):
        flight.sort()
        if flight and (flight[0][0] <= clock or done == len(items)):
            if flight[0][0] > clock and pending:
                clock = min(flight[0][0], clock + 0.5)
                pump()
                continue
            arrived, u, s = flight.pop(0)
            clock = max(clock, arrived) + 0.15
            kind, group, size, _ = units[u].steps[s]
            if kind != "join":
                clock += size * units[u].cols * 4 * (2 ** len(group) - 1) / 4e6
            order[done - 1].append(("serve", u, s))
            if s + 1 < len(units[u].steps):
                pending.append((u, s + 1))
            else:
                idle[units[u].kind].append(units[u].set)
            pump()
        elif done < len(items):
            clock += items[done]
            done += 1
            pump()
        else:
            clock += 0.5
            pump()
    return order, clock


class Exchange:
    def __init__(self, units, place, counts, grads, kept, land, outs, sems):
        self.units, self.place, self.grads, self.kept, self.land, self.outs = units, place, grads, kept, land, outs
        self.send_sem, self.recv_sem, self.load_sem, self.store_sem, self.last_send, self.last_recv = sems
        self.sets = {name: i for i, name in enumerate((kind, i) for kind in CLASSES for i in range(counts[kind]))}
        for unit in units:
            unit.place_at(place)

    def part(self, refs, unit, start, rows):
        return refs[unit.matrix].at[pl.ds(pl.multiple_of(start, 8), rows), pl.ds(unit.col, unit.cols)]

    def own(self, unit, start, rows):
        ref = self.kept.at[self.sets[unit.set]]
        return ref.at[pl.ds(pl.multiple_of(start - unit.starts[1], 8), rows), :]

    def load(self, unit):
        spot = self.sets[unit.set]
        return pltpu.make_async_copy(
            self.part(self.grads, unit, unit.starts[1], unit.steps[0][2]), self.kept.at[spot], self.load_sem.at[spot]
        )

    def store(self, unit):
        spot, s = self.sets[unit.set], unit.returns
        start, rows = unit.starts[s], unit.steps[s][2]
        return pltpu.make_async_copy(
            self.own(unit, start, rows), self.part(self.outs, unit, start, rows), self.store_sem.at[spot]
        )

    def copies(self, u, s):
        unit = self.units[u]
        last = s == len(unit.steps) - 1
        kind, group, size, land = unit.steps[s]
        spot, found = self.sets[unit.set], []
        for turn, flips in enumerate(flips_of(group)):
            start = unit.starts[s]
            if kind == "cut":
                start = start + self.place.code(group, flips) * size
            if s == 0:
                source = self.part(self.grads, unit, start, size)
            elif s <= unit.returns:
                source = self.own(unit, start, size)
            else:
                source = self.part(self.outs, unit, start, size)
            if kind == "join":
                target = self.part(self.outs, unit, start, size)
            else:
                target = self.land.at[spot, pl.ds(land + turn * size, size), :]
            found.append(
                pltpu.make_async_remote_copy(
                    src_ref=source,
                    dst_ref=target,
                    send_sem=self.last_send.at[u] if last else self.send_sem.at[spot, s, turn],
                    recv_sem=self.last_recv.at[u] if last else self.recv_sem.at[spot, s, turn],
                    device_id=self.place.partner(flips),
                    device_id_type=MESH,
                )
            )
        return found

    def go(self, u, s):
        unit = self.units[u]
        if s == 0:
            self.load(unit).start()
        for copy in self.copies(u, s):
            copy.start()

    def serve(self, u, s):
        unit = self.units[u]
        if s == 0:
            self.load(unit).wait()
        for copy in self.copies(u, s):
            copy.wait()
        kind, group, size, land = unit.steps[s]
        if kind != "join":
            spot = self.sets[unit.set]
            start = unit.starts[s]
            if kind == "cut":
                start = start + self.place.code(group) * size
            kept = self.own(unit, start, size)
            total = kept[...]
            for turn in range(2 ** len(group) - 1):
                total = total + self.land[spot, land + turn * size : land + (turn + 1) * size, :]
            kept[...] = total
        if s + 1 == unit.returns:
            self.store(unit).start()
        if s == unit.returns:
            self.store(unit).wait()


LOW = jnp.bfloat16
FULL = jnp.float32


def dot_nn(left, right):
    return lax.dot_general(left, right, (((1,), (0,)), ((), ())), preferred_element_type=FULL)


def dot_nt(left, right):
    return lax.dot_general(left, right, (((1,), (1,)), ((), ())), preferred_element_type=FULL)


def dot_tn(left, right):
    return lax.dot_general(left, right, (((0,), (0,)), ((), ())), preferred_element_type=FULL)


def loop(count, body):
    def step(i, carry):
        body(i)
        return carry

    lax.fori_loop(0, count, step, 0)


def rows_of(i, size):
    return pl.ds(i * size if isinstance(i, int) else pl.multiple_of(i * size, size), size)


def offset_buckets(shift):
    keys = lax.broadcasted_iota(jnp.int32, (128, 128), 0)
    queries = lax.broadcasted_iota(jnp.int32, (128, 128), 1)
    offsets = keys - queries + 128 * shift
    distance = jnp.abs(offsets)
    distant = jnp.full((128, 128), 8, jnp.int32)
    for limit in THRESHOLDS:
        distant = distant + jnp.where(distance >= limit, 1, 0)
    buckets = jnp.where(distance < 8, distance, distant)
    return buckets + jnp.where(offsets > 0, 16, 0)


NEAR = ((-1, range(1, 16)), (0, range(32)), (1, range(17, 32)))


def fill_bias(bias, table, head, count):
    ids = [offset_buckets(shift) for shift, _ in NEAR]
    for side in range(count):
        for spot, (shift, members) in enumerate(NEAR):
            block = jnp.zeros((128, 128), FULL)
            for b in members:
                block = jnp.where(ids[spot] == b, table[head + side, b], block)
            bias[side, spot] = block


def bias_strip(bias, side, table, head, jb, blocks):
    parts = []
    for ib in range(blocks):
        shift = jb - ib
        if abs(shift) <= 1:
            parts.append(bias[side, shift + 1])
        else:
            parts.append(jnp.full((128, 128), table[head, 31 if shift > 0 else 15], FULL))
    return jnp.concatenate(parts, axis=1)


def forward_kernel(
    tokens, lengths, wq, wk, wv, wm, wi, wo, gain1, gain2, table,
    q_out, k_out, v_out, ho_out, n1_out, n2_out, h1_out, act_out, slope_out, result_out, lse_out, pooled_out, sums_out,
    x_s, wq_s, wk_s, wv_s, wm_s, wi_s, wo_s, q_s, k_s, v_s, ho_s, n1_s, n2_s, h1_s, act_s, slope_s, result_s, total_s,
    score_s, prob_s, bias_s, in_sem, out_sem,
):
    count, width = tokens.shape
    rows, seq = lengths.shape[0], tokens.shape[0] // lengths.shape[0]
    heads = table.shape[0]
    size = width // heads
    hidden = wi.shape[1]
    parts = hidden // width
    loads = [
        pltpu.make_async_copy(source, target, in_sem.at[i])
        for i, (source, target) in enumerate(
            [(tokens, x_s), (wq, wq_s), (wk, wk_s), (wv, wv_s), (wm, wm_s), (wi, wi_s), (wo, wo_s)]
        )
    ]
    for load in loads:
        load.start()
    stores = []

    def store(source, target):
        copy = pltpu.make_async_copy(source, target, out_sem.at[len(stores)])
        copy.start()
        stores.append(copy)

    block = 256
    loads[0].wait()

    def norm1(i):
        at = rows_of(i, block)
        x = x_s[at, :].astype(FULL)
        scale = lax.rsqrt(jnp.mean(x * x, -1, keepdims=True) + EPSILON)
        n1_s[at, :] = (x * scale * gain1[...].reshape(1, width)).astype(LOW)

    for i in range(count // block):
        norm1(i)
    store(n1_s, n1_out)
    for i, (w_s, p_s, p_out) in enumerate(((wq_s, q_s, q_out), (wk_s, k_s, k_out), (wv_s, v_s, v_out))):
        loads[1 + i].wait()

        def project(m, w_s=w_s, p_s=p_s):
            at = rows_of(m, 512)
            p_s[at, :] = dot_nn(n1_s[at, :], w_s[...]).astype(LOW)

        for m in range(count // 512):
            project(m)
        store(p_s, p_out)
    blocks = seq // 128
    lanes = lax.broadcasted_iota(jnp.int32, (seq, 2 * size), 1)
    keys = lax.broadcasted_iota(jnp.int32, (128, seq), 0)

    def attend(pair):
        here = rows_of(pair, 2 * size)
        fill_bias(bias_s, table, pair * 2, 2)
        for row in range(rows):
            at = slice(row * seq, (row + 1) * seq)
            limit = lengths[row]
            q, k = q_s[at, here], k_s[at, here]
            vt = v_s[at, here].T
            found = []
            for side in range(2):
                chosen = jnp.where((lanes >= size) == (side == 1), q, jnp.zeros_like(q))
                score_s[row * 2 + side] = dot_nt(k, chosen)
            for side in range(2):
                head = pair * 2 + side
                spot = row * 2 + side
                top = jnp.full((1, seq), NEGATIVE, FULL)
                for jb in range(blocks):
                    some = slice(jb * 128, (jb + 1) * 128)
                    strip = score_s[spot, some, :] + bias_strip(bias_s, side, table, head, jb, blocks)
                    strip = jnp.where(keys + jb * 128 < limit, strip, NEGATIVE)
                    score_s[spot, some, :] = strip
                    top = jnp.maximum(top, jnp.max(strip, 0, keepdims=True))
                mass = jnp.zeros((1, seq), FULL)
                for jb in range(blocks):
                    some = slice(jb * 128, (jb + 1) * 128)
                    strip = jnp.exp(score_s[spot, some, :] - top)
                    mass = mass + jnp.sum(strip, 0, keepdims=True)
                    prob_s[spot, some, :] = strip.astype(LOW)
                lse_out[row * heads + head] = top + jnp.log(mass)
                found.append(dot_nn(vt[side * size : (side + 1) * size, :], prob_s[spot]) / mass)
            ho_s[at, here] = jnp.concatenate(found, 0).T.astype(LOW)

    loop(heads // 2, attend)
    store(ho_s, ho_out)
    loads[4].wait()

    def mix(i):
        at = rows_of(i, block)
        h1 = x_s[at, :].astype(FULL) + dot_nn(ho_s[at, :], wm_s[...])
        h1_s[at, :] = h1
        scale = lax.rsqrt(jnp.mean(h1 * h1, -1, keepdims=True) + EPSILON)
        n2_s[at, :] = (h1 * scale * gain2[...].reshape(1, width)).astype(LOW)

    for i in range(count // block):
        mix(i)
    store(h1_s, h1_out)
    store(n2_s, n2_out)
    loads[5].wait()
    loads[6].wait()
    lane = lax.broadcasted_iota(jnp.int32, (16, count), 1)
    which = lax.broadcasted_iota(jnp.int32, (16, count), 0)
    marks = jnp.zeros((16, count), FULL)
    for row in range(rows):
        inside = (which == row) & (lane >= row * seq) & (lane < row * seq + lengths[row])
        marks = jnp.where(inside, 1.0, marks)
    marks = marks.astype(LOW)

    for part in range(parts):
        columns = pl.ds(part * width, width)

        def feed(i, part=part, columns=columns):
            at = rows_of(i, block)
            inner = dot_nn(n2_s[at, :], wi_s[:, columns])
            share = 0.5 + 0.5 * lax.erf(inner * 0.7071067811865476)
            act = (inner * share).astype(LOW)
            act_s[at, columns] = act
            slope = share + inner * (jnp.exp(inner * inner * -0.5) * 0.3989422804014327)
            slope_s[at, columns] = slope.astype(LOW)
            more = dot_nn(act, wo_s[columns, :])
            if part == 0:
                total_s[at, :] = h1_s[at, :] + more
            elif part < parts - 1:
                total_s[at, :] = total_s[at, :] + more
            else:
                output = total_s[at, :] + more
                total_s[at, :] = output
                result_s[at, :] = output.astype(LOW)

        for i in range(count // block):
            feed(i)
        store(act_s.at[:, columns], act_out.at[:, columns])
        sums = dot_nn(marks, act_s[:, columns])
        for row in range(rows):
            sums_out[part * rows + row : part * rows + row + 1, :] = sums[row : row + 1] / lengths[row].astype(FULL)
        store(slope_s.at[:, columns], slope_out.at[:, columns])
    store(result_s, result_out)
    slots = lax.broadcasted_iota(jnp.int32, (seq, 1), 0)
    for row in range(rows):
        kept = jnp.where(slots < lengths[row], total_s[row * seq : (row + 1) * seq, :], 0.0)
        pooled_out[row : row + 1, :] = jnp.sum(kept, 0, keepdims=True) / lengths[row].astype(FULL)
    for copy in stores:
        copy.wait()


def forward(tokens, lengths, wq, wk, wv, wm, wi, wo, gain1, gain2, table):
    count, width = tokens.shape
    hidden = wi.shape[1]
    rows = lengths.shape[0]
    heads = table.shape[0]
    seq = count // rows
    shape = jax.ShapeDtypeStruct
    any_spec = pl.BlockSpec(memory_space=pl.ANY)
    vmem_spec = pl.BlockSpec(memory_space=pltpu.VMEM)
    smem_spec = pl.BlockSpec(memory_space=pltpu.SMEM)
    low = shape((count, width), LOW)
    wide = shape((count, hidden), LOW)
    weights = [pltpu.VMEM(w.shape, LOW) for w in (wq, wk, wv, wm, wi, wo)]
    narrow_s = pltpu.VMEM((count, width), LOW)
    full_s = pltpu.VMEM((count, width), FULL)
    wide_s = pltpu.VMEM((count, hidden), LOW)
    return pl.pallas_call(
        forward_kernel,
        out_shape=[low, low, low, low, low, low, shape((count, width), FULL), wide, wide, low]
        + [shape((rows * heads, 1, seq), FULL), shape((rows, width), FULL)]
        + [shape((hidden // width * rows, width), FULL)],
        in_specs=[any_spec, smem_spec] + [any_spec] * 6 + [vmem_spec] * 2 + [smem_spec],
        out_specs=[any_spec] * 10 + [vmem_spec] * 3,
        scratch_shapes=[narrow_s]
        + weights
        + [narrow_s] * 6
        + [full_s, wide_s, wide_s, narrow_s, full_s]
        + [
            pltpu.VMEM((2 * rows, seq, seq), FULL),
            pltpu.VMEM((2 * rows, seq, seq), LOW),
            pltpu.VMEM((2, 3, 128, 128), FULL),
            pltpu.SemaphoreType.DMA((7,)),
            pltpu.SemaphoreType.DMA((24,)),
        ],
        compiler_params=pltpu.CompilerParams(vmem_limit_bytes=62 * 2**20),
    )(tokens, lengths, wq, wk, wv, wm, wi, wo, gain1, gain2, table)


def norm_back(values, gain, dy):
    scale = lax.rsqrt(jnp.mean(values * values, -1, keepdims=True) + EPSILON)
    along = values * scale
    dscaled = gain * dy
    mean = jnp.mean(along * dscaled, -1, keepdims=True)
    return scale * (dscaled - along * mean), jnp.sum(along * dy, 0, keepdims=True)


def contrast(queries, documents, doc_groups, positives):
    count = doc_groups.shape[1]
    precise = functools.partial(lax.dot_general, precision=HIGHEST, preferred_element_type=FULL)
    rates = [lax.rsqrt(jnp.sum(p * p, -1, keepdims=True) + EPSILON) for p in (queries, documents)]
    unit = [p * rate for p, rate in zip((queries, documents), rates)]
    scores = SCALE * precise(unit[0], unit[1], (((1,), (1,)), ((), ())))
    indices = lax.broadcasted_iota(jnp.int32, (count, count), 0)
    chosen = jnp.where(positives == indices, 1.0, 0.0).T
    query_groups = jnp.sum(chosen * doc_groups.astype(FULL), 1, keepdims=True)
    masked = jnp.where(query_groups == doc_groups.astype(FULL), scores, NEGATIVE)
    highest = jnp.max(masked, 1, keepdims=True)
    weights = jnp.exp(masked - highest)
    mass = jnp.sum(weights, 1, keepdims=True)
    matched = jnp.sum(jnp.where(chosen > 0.5, scores, 0.0), 1, keepdims=True)
    loss = jnp.sum(highest + jnp.log(mass) - matched, 0, keepdims=True) / count
    dscore = weights / mass - chosen
    dunit = (
        SCALE * precise(dscore, unit[1], (((1,), (0,)), ((), ()))),
        SCALE * precise(dscore, unit[0], (((0,), (0,)), ((), ()))),
    )
    dpooled = [rate * (d - u * jnp.sum(u * d, -1, keepdims=True)) for rate, d, u in zip(rates, dunit, unit)]
    return loss, dpooled


def is_early(sizes, rows):
    return sizes["tower"] * sizes["batch"] * rows <= 128


def make_units(sizes, rows, hidden, width):
    groups = bit_groups(sizes)
    early = is_early(sizes, rows)
    parts = hidden // width
    items, blocks = [], []

    def add(matrix, row, first, item):
        blocks.extend((matrix, row, col, item) for col in range(first, first + width, UNIT_COLS))

    def outer():
        for part in range(parts):
            items.append(("outer", 4.5 if items else 6.0))
            add(0, part * width, 0, len(items))

    if early:
        outer()
        items.append(("hop", 3.0))
    else:
        items.append(("hop", 12.0))
    items.append(("loss", 4.0))
    if not early:
        outer()
    for part in range(parts):
        items.append(("inner", 6.0))
        add(1, 0, part * width, len(items))
    items.append(("mix", 3.6))
    items.append(("mixed", 2.5))
    first = len(items)
    for turn in range(24):
        items.append(("attend", 5.0 if turn % 8 == 7 else 3.5 if turn in (2, 8, 16) else 2.5))
    add(5, 0, 0, first + 4)
    for turn in range(3):
        item = first + 8 * turn + 10 if turn < 2 else first + 25
        blocks.extend((matrix, 0, turn * UNIT_COLS, item) for matrix in range(2, 5))
    items.append(("flush", 4.0))
    items += [("input", 1.4)] * 4
    units = []
    for i, (matrix, row, col, item) in enumerate(blocks):
        kind = PATTERN[i % len(PATTERN)]
        units.append(Unit(matrix, row, width // 2, col, UNIT_COLS, kind, groups[kind], item))
    return units, items


def backward_kernel(
    sizes, units, order, counts,
    cot, pooled, sums, lengths, doc_groups, positives, act, slope, wo, wi, n2, h1, ho, q, k, v, n1, tokens, lse,
    wq, wk, wv, wm, gain1, gain2, table,
    *refs,
):
    grads, outs = refs[:6], refs[6:12]
    tokens_grad, u_out, small_out, loss_out, dpooled_out = refs[12:17]
    (
        narrow, square, staged, full, bias_s, near_s, sums_s, every_s, every_u, thirds_s, core_land, small_land, kept, land,
        in_sem, chunk_sem, stage_sem, core_send, core_recv, last_sem, hop_send, hop_recv, small_send, small_recv,
        send_sem, recv_sem, load_sem, store_sem, final_send, final_recv,
    ) = refs[17:]
    count, width = narrow.shape[1:]
    rows = lengths.shape[0]
    seq = count // rows
    heads = table.shape[0]
    size = width // heads
    parts = wo.shape[0] // width
    block = 256
    place = Place(sizes)
    names = place.names
    tower, batch = place.at["tower"], place.at["batch"]
    exchange = Exchange(
        units, place, counts, grads, kept, land, outs, (send_sem, recv_sem, load_sem, store_sem, final_send, final_recv)
    )
    cot_s, n2_s, dout_s = narrow.at[8], narrow.at[9], narrow.at[10]
    act_s = [narrow.at[part] for part in range(parts)]
    slope_s = [narrow.at[parts + part] for part in range(parts)]
    h1_s, sum_s = full.at[0], full.at[1]
    loads = {}

    def load(name, source, target):
        copy = pltpu.make_async_copy(source, target, in_sem.at[len(loads)])
        copy.start()
        loads[name] = copy

    def cut(part):
        return pl.ds(part * width, width)

    load("cot", cot, cot_s)
    for part in range(parts):
        load("act%d" % part, act.at[:, cut(part)], act_s[part])
    for part in range(parts):
        load("wo%d" % part, wo.at[cut(part), :], square.at[part])
    load("n2", n2, n2_s)
    for part in range(parts):
        load("slope%d" % part, slope.at[:, cut(part)], slope_s[part])

    def wi_chunk(part):
        return pltpu.make_async_copy(wi.at[:, cut(part)], square.at[parts + part % 2], chunk_sem.at[part])

    for part in range(2):
        wi_chunk(part).start()
    load("h1", h1, h1_s)

    early = is_early(sizes, rows)

    item = 0
    stage_of = {}

    def act_on(actions):
        for action, u, s in actions:
            if action == "go":
                if s == 0:
                    exchange_ready(u)
                exchange.go(u, s)
            else:
                exchange.serve(u, s)

    def exchange_ready(u):
        unit = units[u]
        key = (unit.matrix, unit.row // width if unit.matrix == 0 else unit.col // width)
        if key in stage_of:
            stage_of.pop(key)()

    def between():
        nonlocal item
        act_on(order[item])
        item += 1

    half = width // 2
    own_half = pl.ds(pl.multiple_of(tower * half, 8), half)
    other_half = pl.ds(pl.multiple_of((1 - tower) * half, 8), half)
    core_bit = next(bit for bit, name in enumerate(names) if name[0] == "tower")

    def thirds_of(square_ref):
        return [square_ref.at[:, pl.ds(i * UNIT_COLS, UNIT_COLS)] for i in range(3)]

    def core_copies(turn, pieces):
        return [
            pltpu.make_async_remote_copy(
                src_ref=piece.at[other_half, :],
                dst_ref=core_land.at[turn % 2, i],
                send_sem=core_send.at[turn % 2, i],
                recv_sem=core_recv.at[turn % 2, i],
                device_id=place.partner((core_bit,)),
                device_id_type=MESH,
            )
            for i, piece in enumerate(pieces)
        ]

    def out_copies(turn, pieces, targets):
        return [
            pltpu.make_async_copy(piece.at[own_half, :], target.at[own_half, :], stage_sem.at[turn, i])
            for i, (piece, target) in enumerate(zip(pieces, targets))
        ]

    def core_send_off(turn, pieces):
        for copy in core_copies(turn, pieces):
            copy.start()

    def core_add(turn, pieces, targets):
        for copy in core_copies(turn, pieces):
            copy.wait()
        for i, piece in enumerate(pieces):
            piece[own_half, :] = piece[own_half, :] + core_land[turn % 2, i]
        for copy in out_copies(turn, pieces, targets):
            copy.start()

    def core_done(turn, pieces, targets):
        for copy in out_copies(turn, pieces, targets):
            copy.wait()

    sent = []

    def settle():
        if sent:
            key, turn, pieces, targets = sent.pop()
            core_add(turn, pieces, targets)
            stage_of[key] = functools.partial(core_done, turn, pieces, targets)

    def stage(turn, matrix, part, value, target):
        key = (matrix, part)
        last = [old for old, spot in staged_last.items() if spot == turn % 3]
        for old in last:
            staged_last.pop(old)
            if old in stage_of:
                stage_of.pop(old)()
        staged[turn % 3] = value
        settle()
        pieces = thirds_of(staged.at[turn % 3])
        core_send_off(turn, pieces)
        sent.append((key, turn, pieces, thirds_of(target)))
        staged_last[key] = turn % 3

    staged_last = {}

    hops = gather_groups(sizes)
    every_s[tower, batch] = pooled[...]
    if early:
        every_u[tower, batch] = sums[...]
    deltas = set()
    for group in list(bit_groups(sizes).values()) + [hops]:
        for bits in group:
            deltas.update(flips_of(bits))
    barrier = pltpu.get_barrier_semaphore()
    for flips in sorted(deltas):
        pl.semaphore_signal(barrier, inc=1, device_id=place.partner(flips), device_id_type=MESH)
    pl.semaphore_wait(barrier, len(deltas))

    def hop(h, kind=0):
        group = hops[h]
        masks = [names[bit] for bit in group]
        every = (every_s, every_u)[kind]
        if masks[0][0] == "tower":
            held = every.at[tower]
        else:
            mask = masks[0][1]
            held = every.at[tower, pl.ds(lax.div(batch, jnp.int32(mask)) * mask, mask)]
        return [
            pltpu.make_async_remote_copy(
                src_ref=held,
                dst_ref=held,
                send_sem=hop_send.at[h, 3 * kind + turn],
                recv_sem=hop_recv.at[h, 3 * kind + turn],
                device_id=place.partner(flips),
                device_id_type=MESH,
            )
            for turn, flips in enumerate(flips_of(group))
        ]

    def outer(part, right):
        loads["act%d" % part].wait()
        stage(part, 0, part, dot_tn(act_s[part][...], right[...]), grads[0].at[cut(part), :])

    for copy in hop(0):
        copy.start()
    served = 0
    if early:
        loads["cot"].wait()
        for part in range(parts):
            outer(part, cot_s)
            if part >= 1 and served < len(hops) - 1:
                for copy in hop(served):
                    copy.wait()
                served += 1
                for copy in hop(served):
                    copy.start()
            between()
    while served < len(hops):
        for copy in hop(served):
            copy.wait()
        served += 1
        if served < len(hops):
            for copy in hop(served):
                copy.start()
    settle()
    between()

    total = rows * sizes["batch"]
    for t in range(2):
        for b in range(sizes["batch"]):
            first = t * total + b * rows
            staged[3, first : first + rows, :] = every_s[t, b]
    loss, dpooled = contrast(
        staged[3, 0:total, :], staged[3, total : 2 * total, :], doc_groups[...], positives[...]
    )
    loss_out[...] = loss
    mine = jnp.where(tower == 0, dpooled[0], dpooled[1])
    ids = lax.broadcasted_iota(jnp.int32, (mine.shape[0], 1), 0)
    spread = [
        jnp.sum(jnp.where(ids == batch * rows + row, mine, 0.0), 0, keepdims=True) / lengths[row].astype(FULL)
        for row in range(rows)
    ]
    dpooled_out[0:total, :] = dpooled[0]
    dpooled_out[total : 2 * total, :] = dpooled[1]
    if early:
        for copy in hop(0, 1):
            copy.start()
    else:
        loads["cot"].wait()

    def full_dout(row, i):
        at = pl.ds(row * seq + i * block, block)
        slot = lax.broadcasted_iota(jnp.int32, (block, 1), 0) + i * block
        return at, cot_s[at, :].astype(FULL) + jnp.where(slot < lengths[row], spread[row], 0.0)

    for row in range(rows):

        def round_dout(i, row=row):
            at, dout = full_dout(row, i)
            dout_s[at, :] = dout.astype(LOW)

        for i in range(seq // block):
            round_dout(i)
    between()

    if not early:
        for part in range(parts):
            outer(part, dout_s)
            between()
    for name, source, target in (("q", q, 0), ("k", k, 1), ("v", v, 2), ("n1", n1, 3)):
        load(name, source, narrow.at[target])
    loads["n2"].wait()
    for part in range(parts):
        loads["slope%d" % part].wait()
        loads["wo%d" % part].wait()
        wi_chunk(part).wait()

        def inner_back(i, part=part):
            at = rows_of(i, block)
            dact = dot_nt(dout_s[at, :], square[part])
            dinner = (slope_s[part][at, :].astype(FULL) * dact).astype(LOW)
            slope_s[part][at, :] = dinner
            more = dot_nt(dinner, square[parts + part % 2])
            sum_s[at, :] = more if part == 0 else sum_s[at, :] + more

        for i in range(count // block):
            inner_back(i)
        if part + 2 < parts:
            wi_chunk(part + 2).start()
        stage(parts + part, 1, part, dot_tn(n2_s[...], slope_s[part][...]), grads[1].at[:, cut(part)])
        if early and part < len(hops):
            for copy in hop(part, 1):
                copy.wait()
            if part + 1 < len(hops):
                for copy in hop(part + 1, 1):
                    copy.start()
        between()
    if early:
        u_copy = pltpu.make_async_copy(every_u, u_out, last_sem.at[1])
        u_copy.start()
    load("ho", ho, narrow.at[9])
    for name, source, target in (("wm", wm, 0), ("wq", wq, 1), ("wk", wk, 2), ("wv", wv, 3)):
        load(name, source, square.at[target])
    small_out[...] = jnp.zeros_like(small_out)
    loads["h1"].wait()
    loads["wm"].wait()
    q_s, k_s, v_s, n1_s = (narrow.at[i] for i in range(4))
    dh_s, dq_s, dk_s, dv_s = (narrow.at[i] for i in range(4, 8))

    for row in range(rows):

        def mix_back(i, row=row):
            at, dout = full_dout(row, i)
            dv, dgain = norm_back(h1_s[at, :], gain2[...].reshape(1, width), sum_s[at, :])
            dh1 = dout + dv
            h1_s[at, :] = dh1
            small_out[1:2, :] = small_out[1:2, :] + dgain
            da = dh1.astype(LOW)
            cot_s[at, :] = da
            dh_s[at, :] = dot_nt(da, square[0]).astype(LOW)

        for i in range(seq // block):
            mix_back(i)
    settle()
    between()
    loads["ho"].wait()
    third_refs = [thirds_s.at[i] for i in range(3)]
    third_targets = [thirds_of(grads[5])] + [
        [grads[2 + i].at[:, pl.ds(turn * UNIT_COLS, UNIT_COLS)] for i in range(3)] for turn in range(3)
    ]
    first_turn = 2 * parts
    for i in range(3):
        thirds_s[i] = dot_tn(narrow[9], cot_s[:, pl.ds(i * UNIT_COLS, UNIT_COLS)])
    core_send_off(first_turn, third_refs)
    between()
    for done in list(stage_of.values()):
        done()
    stage_of.clear()
    load("x", tokens, narrow.at[9])
    for name in ("q", "k", "v", "n1"):
        loads[name].wait()

    blocks = seq // 128
    lanes = lax.broadcasted_iota(jnp.int32, (seq, 2 * size), 1)
    keys = lax.broadcasted_iota(jnp.int32, (128, seq), 0)
    first_item = item
    steps = rows * (heads // 2)

    def between_at(step, side):
        for index in range(steps):
            actions = order[first_item + 2 * index + side] if 2 * index + side < 24 else []
            if actions:
                pl.when(step == index)(functools.partial(act_on, actions))

    per_turn = 2 * rows

    def third(turn):
        for i, d_s in enumerate((dq_s, dk_s, dv_s)):
            thirds_s[i] = dot_tn(n1_s[...], d_s[:, pl.ds(turn * UNIT_COLS, UNIT_COLS)])
        core_send_off(first_turn + 1 + turn, third_refs)

    def third_add(turn):
        core_add(first_turn + 1 + turn, third_refs, third_targets[1 + turn])

    def third_done(turn):
        core_done(first_turn + 1 + turn, third_refs, third_targets[1 + turn])

    def attend_back(step):
        pair = lax.div(step, jnp.int32(rows))
        row = lax.rem(step, jnp.int32(rows))
        at = rows_of(row, seq)
        here = rows_of(pair, 2 * size)
        limit = lengths[row]
        for turn in range(-1, steps // per_turn - 1):
            ready = per_turn * (turn + 1) if turn >= 0 else 1
            pl.when(step == ready)(functools.partial(third_add, turn))
            pl.when(step == ready + 1)(functools.partial(third_done, turn))

        @pl.when(row == 0)
        def _():
            near_s[...] = jnp.zeros_like(near_s)
            fill_bias(bias_s, table, pair * 2, 2)

        qp, kp, vp, dp = q_s[at, here], k_s[at, here], v_s[at, here], dh_s[at, here]
        nothing = jnp.zeros_like(qp)
        kt = kp.T
        dq, dk, dv = [], [], []
        score_s = [staged.at[side, 0:seq, 0:seq] for side in range(2)]
        dprob_s = [staged.at[2 + side, 0:seq, 0:seq] for side in range(2)]
        prob_s = [narrow.at[8, side * seq : (side + 1) * seq, 0:seq] for side in range(2)]
        dscore_s = [narrow.at[10, side * seq : (side + 1) * seq, 0:seq] for side in range(2)]
        for side in range(2):
            chosen = (lanes >= size) == (side == 1)
            score_s[side][...] = dot_nt(kp, jnp.where(chosen, qp, nothing))
            dprob_s[side][...] = dot_nt(vp, jnp.where(chosen, dp, nothing))
        for side in range(2):
            head = pair * 2 + side
            level = lse[row * heads + head]
            delta = jnp.zeros((1, seq), FULL)
            for jb in range(blocks):
                some = slice(jb * 128, (jb + 1) * 128)
                strip = score_s[side][some, :] + bias_strip(bias_s, side, table, head, jb, blocks)
                strip = jnp.where(keys + jb * 128 < limit, strip, NEGATIVE)
                prob = jnp.exp(strip - level)
                prob_s[side][some, :] = prob.astype(LOW)
                score_s[side][some, :] = prob
                delta = delta + jnp.sum(prob * dprob_s[side][some, :], 0, keepdims=True)
            for jb in range(blocks):
                some = slice(jb * 128, (jb + 1) * 128)
                dscore = score_s[side][some, :] * (dprob_s[side][some, :] - delta)
                dscore_s[side][some, :] = dscore.astype(LOW)
                for ib in range(blocks):
                    spot = min(max(jb - ib, -2), 2) + 2
                    near_s[side, spot] = near_s[side, spot] + dscore[:, ib * 128 : (ib + 1) * 128]
            dk.append(dot_nn(dscore_s[side][...], qp))
            dv.append(dot_nn(prob_s[side][...], dp))
            dq.append(dot_nn(kt[side * size : (side + 1) * size, :], dscore_s[side][...]))
            if side == 0:
                between_at(step, 0)
        first = lanes < size
        dk_s[at, here] = jnp.where(first, dk[0], dk[1]).astype(LOW)
        dv_s[at, here] = jnp.where(first, dv[0], dv[1]).astype(LOW)
        dq_s[at, here] = jnp.concatenate(dq, 0).T.astype(LOW)

        @pl.when(row == rows - 1)
        def _():
            ids = [offset_buckets(shift) for shift, _ in NEAR]
            for side in range(2):
                bucket = lax.broadcasted_iota(jnp.int32, (1, 128), 1)
                found = jnp.zeros((1, 128), FULL)
                for spot, (shift, members) in enumerate(NEAR):
                    total = near_s[side, spot + 1]
                    for b in members:
                        share = jnp.sum(jnp.where(ids[spot] == b, total, 0.0), 0, keepdims=True)
                        found = found + jnp.where(bucket == b, jnp.sum(share, 1, keepdims=True), 0.0)
                for spot, b in ((0, 15), (4, 31)):
                    share = jnp.sum(near_s[side, spot], 0, keepdims=True)
                    found = found + jnp.where(bucket == b, jnp.sum(share, 1, keepdims=True), 0.0)
                sums_s[pair * 2 + side] = found

        for turn in range(steps // per_turn):
            pl.when(step == per_turn * (turn + 1) - 1)(functools.partial(third, turn))
        between_at(step, 1)

    loop(steps, attend_back)
    item = first_item + 24
    for head in range(heads):
        small_out[8 + head : 9 + head, 0:128] = sums_s[head]

    third_add(steps // per_turn - 1)
    for i in range(3):
        stage_of[(2 + i, steps // per_turn - 1)] = lambda: None
    between()
    for name in ("wq", "wk", "wv", "x"):
        loads[name].wait()

    def input_back(i):
        at = rows_of(i, block)
        dn1 = dot_nt(dq_s[at, :], square[1]) + dot_nt(dk_s[at, :], square[2]) + dot_nt(dv_s[at, :], square[3])
        dv, dgain = norm_back(narrow[9, at, :].astype(FULL), gain1[...].reshape(1, width), dn1)
        small_out[0:1, :] = small_out[0:1, :] + dgain
        cot_s[at, :] = (h1_s[at, :] + dv).astype(LOW)

    for i in range(count // block):
        input_back(i)
        if i == 0:
            third_done(steps // per_turn - 1)
        if i < 3:
            between()
    last = pltpu.make_async_copy(cot_s, tokens_grad, last_sem.at[0])
    last.start()

    def small_copy(bit):
        return pltpu.make_async_remote_copy(
            src_ref=small_out,
            dst_ref=small_land.at[bit],
            send_sem=small_send.at[bit],
            recv_sem=small_recv.at[bit],
            device_id=place.partner((bit,)),
            device_id_type=MESH,
        )

    small_copy(0).start()
    actions = order[item]
    for bit in range(len(names)):
        act_on(actions[len(actions) * bit // (len(names) + 1) : len(actions) * (bit + 1) // (len(names) + 1)])
        small_copy(bit).wait()
        small_out[...] = small_out[...] + small_land[bit]
        if bit + 1 < len(names):
            small_copy(bit + 1).start()
    act_on(actions[len(actions) * len(names) // (len(names) + 1) :])
    last.wait()
    if early:
        u_copy.wait()
    for done in stage_of.values():
        done()


def backward(
    sizes, cot, pooled, sums, lengths, doc_groups, positives, act, slope, wo, wi, n2, h1, ho, q, k, v, n1, tokens, lse,
    wq, wk, wv, wm, gain1, gain2, table,
):
    count, width = cot.shape
    hidden = wo.shape[0]
    rows = lengths.shape[0]
    heads = table.shape[0]
    total = doc_groups.shape[0]
    names = bit_names(sizes)
    shape = jax.ShapeDtypeStruct
    early = is_early(sizes, rows)
    gathered = shape((2, sizes["batch"]) + sums.shape if early else (8, 128), FULL)
    units, items = make_units(sizes, rows, hidden, width)
    counts = set_counts(sizes)
    order, _ = plan(units, names, counts, [PACE * time for _, time in items])
    steps = max(len(unit.steps) for unit in units)
    sets = sum(counts.values())
    any_spec = pl.BlockSpec(memory_space=pl.ANY)
    vmem_spec = pl.BlockSpec(memory_space=pltpu.VMEM)
    smem_spec = pl.BlockSpec(memory_space=pltpu.SMEM)
    squares = [shape((hidden, width), FULL), shape((width, hidden), FULL)] + [shape((width, width), FULL)] * 4
    hops = len(gather_groups(sizes))
    dma = pltpu.SemaphoreType.DMA
    return pl.pallas_call(
        functools.partial(backward_kernel, sizes, units, order, counts),
        out_shape=squares + squares
        + [shape((count, width), LOW), gathered, shape((24, width), FULL), shape((1, 1), FULL)]
        + [shape((2 * total, width), FULL)],
        in_specs=[any_spec, vmem_spec, vmem_spec, smem_spec, vmem_spec, vmem_spec]
        + [any_spec] * 12
        + [vmem_spec]
        + [any_spec] * 4
        + [vmem_spec] * 2
        + [smem_spec],
        out_specs=[any_spec] * 14 + [vmem_spec] * 3,
        scratch_shapes=[
            pltpu.VMEM((11, count, width), LOW),
            pltpu.VMEM((6, width, width), LOW),
            pltpu.VMEM((4, width, width), FULL),
            pltpu.VMEM((2, count, width), FULL),
            pltpu.VMEM((2, 3, 128, 128), FULL),
            pltpu.VMEM((2, 5, 128, 128), FULL),
            pltpu.VMEM((heads, 1, 128), FULL),
            pltpu.VMEM((2, sizes["batch"], rows, width), FULL),
            pltpu.VMEM(gathered.shape, FULL),
            pltpu.VMEM((3, width, UNIT_COLS), FULL),
            pltpu.VMEM((2, 3, width // 2, UNIT_COLS), FULL),
            pltpu.VMEM((len(names), 24, width), FULL),
            pltpu.VMEM((sets, max(unit.steps[0][2] for unit in units), UNIT_COLS), FULL),
            pltpu.VMEM((sets, max(unit.land for unit in units), UNIT_COLS), FULL),
            dma((32,)),
            dma((8,)),
            dma((16, 3)),
            dma((2, 3)),
            dma((2, 3)),
            dma((2,)),
            dma((hops, 6)),
            dma((hops, 6)),
            dma((len(names),)),
            dma((len(names),)),
            dma((sets, steps, 3)),
            dma((sets, steps, 3)),
            dma((sets,)),
            dma((sets,)),
            dma((len(units),)),
            dma((len(units),)),
        ],
        compiler_params=pltpu.CompilerParams(
            collective_id=0, has_side_effects=True, vmem_limit_bytes=int(63.5 * 2**20)
        ),
    )(
        cot, pooled, sums, lengths, doc_groups.reshape(1, total), positives.reshape(1, total), act, slope, wo, wi, n2, h1,
        ho, q, k, v, n1, tokens, lse, wq, wk, wv, wm, gain1, gain2, table,
    )


OUT_ROWS = 256


def hand_out_kernel(blocks, count, heads, early, *refs):
    sources, (u_in, small, loss_in, dpooled) = refs[:count], refs[count : count + 4]
    targets = refs[count + 4 : 2 * count + 4]
    gain1, gain2, table, loss = refs[2 * count + 4 : 2 * count + 8]
    full, low, u_s, sums_s, in_sem, out_sem = refs[2 * count + 8 :]
    width = full.shape[2]
    loads, stores = [], []
    if early:
        u_load = pltpu.make_async_copy(u_in, u_s, in_sem.at[len(blocks)])
        u_load.start()
    for i, (array, spot, row, col) in enumerate(blocks):
        at = (pl.ds(row, OUT_ROWS), pl.ds(col, width))
        held = (low if sources[array].dtype == LOW else full).at[spot]
        loads.append(pltpu.make_async_copy(sources[array].at[at], held, in_sem.at[i]))
        stores.append(pltpu.make_async_copy(held, targets[array].at[at], out_sem.at[i]))
    for load in loads:
        load.start()
    gain1[...] = small[0]
    gain2[...] = small[1]
    table[...] = small[8 : 8 + heads, 0 : table.shape[1]]
    loss[...] = loss_in[...]
    if early:
        u_load.wait()
        towers, places, most, _ = u_s.shape
        parts = targets[0].shape[0] // width
        rows = most // parts
        for part in range(parts):
            for t in range(towers):
                for b in range(places):
                    first = (t * places + b) * rows
                    sums_s[part, first : first + rows, :] = u_s[t, b, part * rows : (part + 1) * rows, :]
    for i, (load, store) in enumerate(zip(loads, stores)):
        load.wait()
        array, spot, row, _ = blocks[i]
        if early and array == 0:
            some = sums_s[row // width, :, row % width : row % width + OUT_ROWS]
            full[spot] = full[spot] + lax.dot_general(
                some, dpooled[...], (((0,), (0,)), ((), ())), precision=HIGHEST, preferred_element_type=FULL
            )
        store.start()
    for store in stores:
        store.wait()


def hand_out(arrays, sums, small, loss, dpooled, heads, buckets):
    width = small.shape[1]
    early = len(sums.shape) == 4
    blocks, held = [], {FULL: 0, LOW: 0}
    for i, array in enumerate(arrays):
        for col in range(0, array.shape[1], width):
            for row in range(0, array.shape[0], OUT_ROWS):
                kind = LOW if array.dtype == LOW else FULL
                blocks.append((i, held[kind], row, col))
                held[kind] += 1
    any_spec = pl.BlockSpec(memory_space=pl.ANY)
    vmem_spec = pl.BlockSpec(memory_space=pltpu.VMEM)
    shape = jax.ShapeDtypeStruct
    return pl.pallas_call(
        functools.partial(hand_out_kernel, blocks, len(arrays), heads, early),
        out_shape=[shape(a.shape, a.dtype) for a in arrays]
        + [shape((width,), FULL), shape((width,), FULL), shape((heads, buckets), FULL), shape((1, 1), FULL)],
        in_specs=[any_spec] * (len(arrays) + 1) + [vmem_spec] * 3,
        out_specs=[any_spec] * len(arrays) + [vmem_spec] * 4,
        scratch_shapes=[
            pltpu.VMEM((held[FULL], OUT_ROWS, width), FULL),
            pltpu.VMEM((held[LOW], OUT_ROWS, width), LOW),
            pltpu.VMEM(sums.shape, FULL),
            pltpu.VMEM((arrays[0].shape[0] // width, dpooled.shape[0], width) if early else (8, 128), FULL),
            pltpu.SemaphoreType.DMA((len(blocks) + 1,)),
            pltpu.SemaphoreType.DMA((len(blocks),)),
        ],
        compiler_params=pltpu.CompilerParams(vmem_limit_bytes=63 * 2**20),
    )(*arrays, sums, small, loss, dpooled)


def shards(
    tokens,
    lengths,
    doc_groups,
    positives,
    cotangent,
    w_query,
    w_key,
    w_value,
    w_mixed,
    w_inner,
    w_outer,
    gain_attn,
    gain_ffn,
    rel_table,
):
    rows = tokens.shape[1]
    count, width = rows * tokens.shape[2], tokens.shape[3]
    buckets, heads = rel_table.shape
    sizes = {axis: lax.axis_size(axis) for axis in ("tower", "batch")}
    flat = tokens.reshape(count, width)
    cot = cotangent.reshape(count, width)
    own_lengths = lengths.reshape(rows)
    table = rel_table.T
    q, k, v, ho, n1, n2, h1, act, slope, result, lse, pooled, sums = forward(
        flat, own_lengths, w_query, w_key, w_value, w_mixed, w_inner, w_outer, gain_attn, gain_ffn, table
    )
    found = backward(
        sizes, cot, pooled, sums, own_lengths, doc_groups, positives, act, slope, w_outer, w_inner, n2, h1, ho, q, k, v, n1,
        flat, lse, w_query, w_key, w_value, w_mixed, gain_attn, gain_ffn, table,
    )
    given = hand_out(found[6:13], *found[13:], heads, buckets)
    wo_grad, wi_grad, wq_grad, wk_grad, wv_grad, wm_grad, tokens_grad, gain1_grad, gain2_grad, table_grad, loss = given
    return (
        result.reshape(tokens.shape),
        pooled[None],
        loss[0, 0],
        tokens_grad.reshape(tokens.shape),
        wq_grad,
        wk_grad,
        wv_grad,
        wm_grad,
        wi_grad,
        wo_grad,
        gain1_grad,
        gain2_grad,
        table_grad.T,
    )


def solution(mesh):
    return jax.shard_map(
        shards,
        mesh=mesh,
        in_specs=(
            P("tower", "batch", None, None),
            P("tower", "batch"),
            P(),
            P(),
            P("tower", "batch", None, None),
            P(),
            P(),
            P(),
            P(),
            P(),
            P(),
            P(),
            P(),
            P(),
        ),
        out_specs=(
            P("tower", "batch", None, None),
            P("tower", "batch", None),
            P(),
            P("tower", "batch", None, None),
            P(),
            P(),
            P(),
            P(),
            P(),
            P(),
            P(),
            P(),
            P(),
        ),
        check_vma=False,
    )
```

```python
import functools

import jax
import jax.numpy as jnp
from jax import lax
from jax.experimental import pallas as pl
from jax.experimental.pallas import tpu as pltpu
from jax.sharding import PartitionSpec as P

EPSILON = 1e-06
SCALE = 50.0
NEGATIVE = -1000000000.0
THRESHOLDS = (12, 16, 23, 32, 46, 64, 91)
HIGHEST = lax.Precision.HIGHEST


MESH = pl.DeviceIdType.MESH
LINK = 46.97e3
CORE = 500e3
FLIGHT = 3.42
DEPTH = 7.40
PACE = 0.885
CLASSES = "ABCD"
PATTERN = "ACBADBCABADBACBADBCBADBAAABBBCCDAAAB"
UNIT_COLS = 256


def bit_names(sizes):
    names = []
    for axis in ("tower", "batch"):
        mask = 1
        while mask < sizes[axis]:
            names.append((axis, mask))
            mask *= 2
    return names


def set_counts(sizes):
    return {"A": 6, "B": 6, "C": 4, "D": 4} if sizes["batch"] <= 16 else {"A": 2, "B": 2, "C": 1, "D": 1}


def bit_groups(sizes):
    names = bit_names(sizes)
    rest = [k for k, name in enumerate(names) if name[0] == "batch"]
    x, y, low, high = rest[:4]
    more = [(k,) for k in rest[4:]]
    firsts = {
        "A": [(x,), (y,), (low, high)],
        "B": [(y,), (x,), (low, high)],
        "C": [(low,), (x,), (y,), (high,)],
        "D": [(low,), (y,), (x,), (high,)],
    }
    return {name: groups + more for name, groups in firsts.items()}


def flips_of(group):
    return [tuple(k for i, k in enumerate(group) if choice >> i & 1) for choice in range(1, 2 ** len(group))]


def gather_groups(sizes):
    rest = [k for k, name in enumerate(bit_names(sizes)) if name[0] == "batch"]
    groups = [tuple(rest[i : i + 2]) for i in range(0, len(rest), 2)]
    return groups + [(k,) for k, name in enumerate(bit_names(sizes)) if name[0] == "tower"]


class Place:
    def __init__(self, sizes):
        self.names = bit_names(sizes)
        self.at = {axis: lax.axis_index(axis) for axis in ("tower", "batch")}
        self.bits = [
            lax.rem(lax.div(self.at[axis], jnp.int32(mask)), jnp.int32(2)) for axis, mask in self.names
        ]

    def partner(self, flips):
        other = dict(self.at)
        for k in flips:
            axis, mask = self.names[k]
            other[axis] = other[axis] + mask * (1 - 2 * self.bits[k])
        return (other["tower"], other["batch"])

    def code(self, group, flips=()):
        total = jnp.int32(0)
        for k in group:
            total = total * 2 + (1 - self.bits[k] if k in flips else self.bits[k])
        return total


class Unit:
    def __init__(self, matrix, row, rows, col, cols, kind, groups, item):
        self.matrix, self.row, self.rows, self.col, self.cols, self.kind, self.item = matrix, row, rows, col, cols, kind, item
        self.steps = []
        size, back, land = rows, [], 0
        for group in groups:
            ways = 2 ** len(group)
            if size % (8 * ways) == 0:
                size //= ways
                self.steps.append(("cut", group, size, land))
                back.append(("join", group, size, 0))
                land += size * (ways - 1)
            else:
                for k in group:
                    self.steps.append(("whole", (k,), size, land))
                    land += size
        self.land = land
        self.returns = len(self.steps)
        self.steps += back[::-1]
        self.steps.append(("join", (0,), rows, 0))

    def place_at(self, place):
        start, stack = self.row + place.at["tower"] * self.rows, []
        self.starts = []
        for kind, group, size, _ in self.steps:
            self.starts.append(start)
            if kind == "cut":
                stack.append(start)
                start = start + place.code(group) * size
            elif kind == "join" and stack:
                start = stack.pop()


def link_use(names, group, size):
    link = size / LINK
    masks = [names[k] for k in group]
    if masks[0][0] == "tower":
        return {"core": size / CORE}
    if masks == [("batch", 4)]:
        return {"end": link}
    if masks == [("batch", 8)]:
        return {"end": link, "middle": 2 * link}
    if masks == [("batch", 4), ("batch", 8)]:
        return {"end": 3 * link, "middle": 4 * link}
    return {mask: link * (2 ** len(group) - 1) for mask in masks}


def plan(units, names, counts, items, depth=DEPTH):
    free, clock, flight, pending = {}, 0.0, [], []
    idle = {kind: [(kind, i) for i in range(counts[kind])] for kind in CLASSES}
    done, order = 0, [[] for _ in items]
    left = list(range(len(units)))

    def use(u, s):
        _, group, size, _ = units[u].steps[s]
        return link_use(names, group, size * units[u].cols * 4)

    def pump():
        nonlocal clock
        for u in left:
            if units[u].item < done and (u, 0) not in pending:
                pending.append((u, 0))
        pending.sort()
        for u, s in list(pending):
            unit = units[u]
            if s == 0 and not idle[unit.kind]:
                continue
            if any(free.get(link, 0.0) - clock > depth for link in use(u, 1 if s == 0 else s)):
                continue
            pending.remove((u, s))
            if s == 0:
                left.remove(u)
                unit.set = idle[unit.kind].pop(0)
            clock += 0.08
            end = clock
            for link, time in use(u, s).items():
                free[link] = max(clock, free.get(link, 0.0)) + time
                end = max(end, free[link])
            flight.append((end + FLIGHT, u, s))
            order[done - 1].append(("go", u, s))

    while left or flight or pending or done < len(items):
        flight.sort()
        if flight and (flight[0][0] <= clock or done == len(items)):
            if flight[0][0] > clock and pending:
                clock = min(flight[0][0], clock + 0.5)
                pump()
                continue
            arrived, u, s = flight.pop(0)
            clock = max(clock, arrived) + 0.15
            kind, group, size, _ = units[u].steps[s]
            if kind != "join":
                clock += size * units[u].cols * 4 * (2 ** len(group) - 1) / 4e6
            order[done - 1].append(("serve", u, s))
            if s + 1 < len(units[u].steps):
                pending.append((u, s + 1))
            else:
                idle[units[u].kind].append(units[u].set)
            pump()
        elif done < len(items):
            clock += items[done]
            done += 1
            pump()
        else:
            clock += 0.5
            pump()
    return order, clock


class Exchange:
    def __init__(self, units, place, counts, grads, kept, land, outs, sems):
        self.units, self.place, self.grads, self.kept, self.land, self.outs = units, place, grads, kept, land, outs
        self.send_sem, self.recv_sem, self.load_sem, self.store_sem, self.last_send, self.last_recv = sems
        self.sets = {name: i for i, name in enumerate((kind, i) for kind in CLASSES for i in range(counts[kind]))}
        for unit in units:
            unit.place_at(place)

    def part(self, refs, unit, start, rows):
        return refs[unit.matrix].at[pl.ds(pl.multiple_of(start, 8), rows), pl.ds(unit.col, unit.cols)]

    def own(self, unit, start, rows):
        ref = self.kept.at[self.sets[unit.set]]
        return ref.at[pl.ds(pl.multiple_of(start - unit.starts[1], 8), rows), :]

    def load(self, unit):
        spot = self.sets[unit.set]
        return pltpu.make_async_copy(
            self.part(self.grads, unit, unit.starts[1], unit.steps[0][2]), self.kept.at[spot], self.load_sem.at[spot]
        )

    def store(self, unit):
        spot, s = self.sets[unit.set], unit.returns
        start, rows = unit.starts[s], unit.steps[s][2]
        return pltpu.make_async_copy(
            self.own(unit, start, rows), self.part(self.outs, unit, start, rows), self.store_sem.at[spot]
        )

    def copies(self, u, s):
        unit = self.units[u]
        last = s == len(unit.steps) - 1
        kind, group, size, land = unit.steps[s]
        spot, found = self.sets[unit.set], []
        for turn, flips in enumerate(flips_of(group)):
            start = unit.starts[s]
            if kind == "cut":
                start = start + self.place.code(group, flips) * size
            if s == 0:
                source = self.part(self.grads, unit, start, size)
            elif s <= unit.returns:
                source = self.own(unit, start, size)
            else:
                source = self.part(self.outs, unit, start, size)
            if kind == "join":
                target = self.part(self.outs, unit, start, size)
            else:
                target = self.land.at[spot, pl.ds(land + turn * size, size), :]
            found.append(
                pltpu.make_async_remote_copy(
                    src_ref=source,
                    dst_ref=target,
                    send_sem=self.last_send.at[u] if last else self.send_sem.at[spot, s, turn],
                    recv_sem=self.last_recv.at[u] if last else self.recv_sem.at[spot, s, turn],
                    device_id=self.place.partner(flips),
                    device_id_type=MESH,
                )
            )
        return found

    def go(self, u, s):
        unit = self.units[u]
        if s == 0:
            self.load(unit).start()
        for copy in self.copies(u, s):
            copy.start()

    def serve(self, u, s):
        unit = self.units[u]
        if s == 0:
            self.load(unit).wait()
        for copy in self.copies(u, s):
            copy.wait()
        kind, group, size, land = unit.steps[s]
        if kind != "join":
            spot = self.sets[unit.set]
            start = unit.starts[s]
            if kind == "cut":
                start = start + self.place.code(group) * size
            kept = self.own(unit, start, size)
            total = kept[...]
            for turn in range(2 ** len(group) - 1):
                total = total + self.land[spot, land + turn * size : land + (turn + 1) * size, :]
            kept[...] = total
        if s + 1 == unit.returns:
            self.store(unit).start()
        if s == unit.returns:
            self.store(unit).wait()


LOW = jnp.bfloat16
FULL = jnp.float32


def dot_nn(left, right):
    return lax.dot_general(left, right, (((1,), (0,)), ((), ())), preferred_element_type=FULL)


def dot_nt(left, right):
    return lax.dot_general(left, right, (((1,), (1,)), ((), ())), preferred_element_type=FULL)


def dot_tn(left, right):
    return lax.dot_general(left, right, (((0,), (0,)), ((), ())), preferred_element_type=FULL)


def loop(count, body):
    def step(i, carry):
        body(i)
        return carry

    lax.fori_loop(0, count, step, 0)


def rows_of(i, size):
    return pl.ds(i * size if isinstance(i, int) else pl.multiple_of(i * size, size), size)


def offset_buckets(shift):
    keys = lax.broadcasted_iota(jnp.int32, (128, 128), 0)
    queries = lax.broadcasted_iota(jnp.int32, (128, 128), 1)
    offsets = keys - queries + 128 * shift
    distance = jnp.abs(offsets)
    distant = jnp.full((128, 128), 8, jnp.int32)
    for limit in THRESHOLDS:
        distant = distant + jnp.where(distance >= limit, 1, 0)
    buckets = jnp.where(distance < 8, distance, distant)
    return buckets + jnp.where(offsets > 0, 16, 0)


NEAR = ((-1, range(1, 16)), (0, range(32)), (1, range(17, 32)))


def fill_bias(bias, table, head, count):
    ids = [offset_buckets(shift) for shift, _ in NEAR]
    for spot, (shift, members) in enumerate(NEAR):
        found = [jnp.zeros((128, 128), FULL)] * count
        for b in members:
            here = ids[spot] == b
            found = [jnp.where(here, table[head + side, b], block) for side, block in enumerate(found)]
        for side, block in enumerate(found):
            bias[side, spot] = block


def bias_strip(bias, side, table, head, jb, blocks):
    parts = []
    for ib in range(blocks):
        shift = jb - ib
        if abs(shift) <= 1:
            parts.append(bias[side, shift + 1])
        else:
            parts.append(jnp.full((128, 128), table[head, 31 if shift > 0 else 15], FULL))
    return jnp.concatenate(parts, axis=1)


def forward_kernel(
    tokens, lengths, wq, wk, wv, wm, wi, wo, gain1, gain2, table,
    q_out, k_out, v_out, ho_out, n1_out, n2_out, h1_out, act_out, slope_out, result_out, lse_out, pooled_out, sums_out,
    x_s, wq_s, wk_s, wv_s, wm_s, wi_s, wo_s, q_s, k_s, v_s, ho_s, n1_s, n2_s, h1_s, act_s, slope_s, result_s, total_s,
    score_s, prob_s, bias_s, in_sem, out_sem,
):
    count, width = tokens.shape
    rows, seq = lengths.shape[0], tokens.shape[0] // lengths.shape[0]
    heads = table.shape[0]
    size = width // heads
    hidden = wi.shape[1]
    parts = hidden // width
    loads = [
        pltpu.make_async_copy(source, target, in_sem.at[i])
        for i, (source, target) in enumerate(
            [(tokens, x_s), (wq, wq_s), (wk, wk_s), (wv, wv_s), (wm, wm_s), (wi, wi_s), (wo, wo_s)]
        )
    ]
    for load in loads:
        load.start()
    stores = []

    def store(source, target):
        copy = pltpu.make_async_copy(source, target, out_sem.at[len(stores)])
        copy.start()
        stores.append(copy)

    block = 256
    loads[0].wait()

    def norm1(i):
        at = rows_of(i, block)
        x = x_s[at, :].astype(FULL)
        scale = lax.rsqrt(jnp.mean(x * x, -1, keepdims=True) + EPSILON)
        n1_s[at, :] = (x * scale * gain1[...].reshape(1, width)).astype(LOW)

    for i in range(count // block):
        norm1(i)
    store(n1_s, n1_out)
    for i, (w_s, p_s, p_out) in enumerate(((wq_s, q_s, q_out), (wk_s, k_s, k_out), (wv_s, v_s, v_out))):
        loads[1 + i].wait()

        def project(m, w_s=w_s, p_s=p_s):
            at = rows_of(m, 512)
            p_s[at, :] = dot_nn(n1_s[at, :], w_s[...]).astype(LOW)

        for m in range(count // 512):
            project(m)
        store(p_s, p_out)
    blocks = seq // 128
    lanes = lax.broadcasted_iota(jnp.int32, (seq, 2 * size), 1)
    keys = lax.broadcasted_iota(jnp.int32, (128, seq), 0)

    def attend(pair):
        here = rows_of(pair, 2 * size)
        fill_bias(bias_s, table, pair * 2, 2)
        for row in range(rows):
            at = slice(row * seq, (row + 1) * seq)
            q, k = q_s[at, here], k_s[at, here]
            for side in range(2):
                chosen = jnp.where((lanes >= size) == (side == 1), q, jnp.zeros_like(q))
                score_s[row * 2 + side] = dot_nt(k, chosen)
        for row in range(rows):
            at = slice(row * seq, (row + 1) * seq)
            limit = lengths[row]
            vt = v_s[at, here].T
            found = []
            for side in range(2):
                head = pair * 2 + side
                spot = row * 2 + side
                top = jnp.full((1, seq), NEGATIVE, FULL)
                for jb in range(blocks):
                    some = slice(jb * 128, (jb + 1) * 128)
                    strip = score_s[spot, some, :] + bias_strip(bias_s, side, table, head, jb, blocks)
                    strip = jnp.where(keys + jb * 128 < limit, strip, NEGATIVE)
                    score_s[spot, some, :] = strip
                    top = jnp.maximum(top, jnp.max(strip, 0, keepdims=True))
                mass = jnp.zeros((1, seq), FULL)
                for jb in range(blocks):
                    some = slice(jb * 128, (jb + 1) * 128)
                    strip = jnp.exp(score_s[spot, some, :] - top)
                    mass = mass + jnp.sum(strip, 0, keepdims=True)
                    prob_s[spot, some, :] = strip.astype(LOW)
                lse_out[row * heads + head] = top + jnp.log(mass)
                found.append(dot_nn(vt[side * size : (side + 1) * size, :], prob_s[spot]) / mass)
            ho_s[at, here] = jnp.concatenate(found, 0).T.astype(LOW)

    loop(heads // 2, attend)
    store(ho_s, ho_out)
    loads[4].wait()

    def mix(i):
        at = rows_of(i, block)
        h1 = x_s[at, :].astype(FULL) + dot_nn(ho_s[at, :], wm_s[...])
        h1_s[at, :] = h1
        scale = lax.rsqrt(jnp.mean(h1 * h1, -1, keepdims=True) + EPSILON)
        n2_s[at, :] = (h1 * scale * gain2[...].reshape(1, width)).astype(LOW)

    for i in range(count // block):
        mix(i)
    store(h1_s, h1_out)
    store(n2_s, n2_out)
    loads[5].wait()
    loads[6].wait()
    lane = lax.broadcasted_iota(jnp.int32, (16, count), 1)
    which = lax.broadcasted_iota(jnp.int32, (16, count), 0)
    marks = jnp.zeros((16, count), FULL)
    for row in range(rows):
        inside = (which == row) & (lane >= row * seq) & (lane < row * seq + lengths[row])
        marks = jnp.where(inside, 1.0, marks)
    marks = marks.astype(LOW)

    for part in range(parts):
        columns = pl.ds(part * width, width)

        def feed(i, part=part, columns=columns):
            at = rows_of(i, block)
            inner = dot_nn(n2_s[at, :], wi_s[:, columns])
            share = 0.5 + 0.5 * lax.erf(inner * 0.7071067811865476)
            act = (inner * share).astype(LOW)
            act_s[at, columns] = act
            slope = share + inner * (jnp.exp(inner * inner * -0.5) * 0.3989422804014327)
            slope_s[at, columns] = slope.astype(LOW)
            more = dot_nn(act, wo_s[columns, :])
            if part == 0:
                total_s[at, :] = h1_s[at, :] + more
            elif part < parts - 1:
                total_s[at, :] = total_s[at, :] + more
            else:
                output = total_s[at, :] + more
                total_s[at, :] = output
                result_s[at, :] = output.astype(LOW)

        for i in range(count // block):
            feed(i)
        store(act_s.at[:, columns], act_out.at[:, columns])
        sums = dot_nn(marks, act_s[:, columns])
        for row in range(rows):
            sums_out[part * rows + row : part * rows + row + 1, :] = sums[row : row + 1] / lengths[row].astype(FULL)
        store(slope_s.at[:, columns], slope_out.at[:, columns])
    store(result_s, result_out)
    slots = lax.broadcasted_iota(jnp.int32, (seq, 1), 0)
    for row in range(rows):
        kept = jnp.where(slots < lengths[row], total_s[row * seq : (row + 1) * seq, :], 0.0)
        pooled_out[row : row + 1, :] = jnp.sum(kept, 0, keepdims=True) / lengths[row].astype(FULL)
    for copy in stores:
        copy.wait()


def forward(tokens, lengths, wq, wk, wv, wm, wi, wo, gain1, gain2, table):
    count, width = tokens.shape
    hidden = wi.shape[1]
    rows = lengths.shape[0]
    heads = table.shape[0]
    seq = count // rows
    shape = jax.ShapeDtypeStruct
    any_spec = pl.BlockSpec(memory_space=pl.ANY)
    vmem_spec = pl.BlockSpec(memory_space=pltpu.VMEM)
    smem_spec = pl.BlockSpec(memory_space=pltpu.SMEM)
    low = shape((count, width), LOW)
    wide = shape((count, hidden), LOW)
    weights = [pltpu.VMEM(w.shape, LOW) for w in (wq, wk, wv, wm, wi, wo)]
    narrow_s = pltpu.VMEM((count, width), LOW)
    full_s = pltpu.VMEM((count, width), FULL)
    wide_s = pltpu.VMEM((count, hidden), LOW)
    return pl.pallas_call(
        forward_kernel,
        out_shape=[low, low, low, low, low, low, shape((count, width), FULL), wide, wide, low]
        + [shape((rows * heads, 1, seq), FULL), shape((rows, width), FULL)]
        + [shape((hidden // width * rows, width), FULL)],
        in_specs=[any_spec, smem_spec] + [any_spec] * 6 + [vmem_spec] * 2 + [smem_spec],
        out_specs=[any_spec] * 10 + [vmem_spec] * 3,
        scratch_shapes=[narrow_s]
        + weights
        + [narrow_s] * 6
        + [full_s, wide_s, wide_s, narrow_s, full_s]
        + [
            pltpu.VMEM((2 * rows, seq, seq), FULL),
            pltpu.VMEM((2 * rows, seq, seq), LOW),
            pltpu.VMEM((2, 3, 128, 128), FULL),
            pltpu.SemaphoreType.DMA((7,)),
            pltpu.SemaphoreType.DMA((24,)),
        ],
        compiler_params=pltpu.CompilerParams(vmem_limit_bytes=62 * 2**20),
    )(tokens, lengths, wq, wk, wv, wm, wi, wo, gain1, gain2, table)


def norm_back(values, gain, dy):
    scale = lax.rsqrt(jnp.mean(values * values, -1, keepdims=True) + EPSILON)
    along = values * scale
    dscaled = gain * dy
    mean = jnp.mean(along * dscaled, -1, keepdims=True)
    return scale * (dscaled - along * mean), jnp.sum(along * dy, 0, keepdims=True)


def contrast(queries, documents, doc_groups, positives):
    count = doc_groups.shape[1]
    precise = functools.partial(lax.dot_general, precision=HIGHEST, preferred_element_type=FULL)
    rates = [lax.rsqrt(jnp.sum(p * p, -1, keepdims=True) + EPSILON) for p in (queries, documents)]
    unit = [p * rate for p, rate in zip((queries, documents), rates)]
    scores = SCALE * precise(unit[0], unit[1], (((1,), (1,)), ((), ())))
    indices = lax.broadcasted_iota(jnp.int32, (count, count), 0)
    chosen = jnp.where(positives == indices, 1.0, 0.0).T
    query_groups = jnp.sum(chosen * doc_groups.astype(FULL), 1, keepdims=True)
    masked = jnp.where(query_groups == doc_groups.astype(FULL), scores, NEGATIVE)
    highest = jnp.max(masked, 1, keepdims=True)
    weights = jnp.exp(masked - highest)
    mass = jnp.sum(weights, 1, keepdims=True)
    matched = jnp.sum(jnp.where(chosen > 0.5, scores, 0.0), 1, keepdims=True)
    loss = jnp.sum(highest + jnp.log(mass) - matched, 0, keepdims=True) / count
    dscore = weights / mass - chosen
    dunit = (
        SCALE * precise(dscore, unit[1], (((1,), (0,)), ((), ()))),
        SCALE * precise(dscore, unit[0], (((0,), (0,)), ((), ()))),
    )
    dpooled = [rate * (d - u * jnp.sum(u * d, -1, keepdims=True)) for rate, d, u in zip(rates, dunit, unit)]
    return loss, dpooled


def is_early(sizes, rows):
    return sizes["tower"] * sizes["batch"] * rows <= 128


def make_units(sizes, rows, hidden, width):
    groups = bit_groups(sizes)
    early = is_early(sizes, rows)
    parts = hidden // width
    items, blocks = [], []

    def add(matrix, row, first, item):
        blocks.extend((matrix, row, col, item) for col in range(first, first + width, UNIT_COLS))

    def outer():
        for part in range(parts):
            items.append(("outer", 4.5 if items else 6.0))
            add(0, part * width, 0, len(items))

    if early:
        outer()
        items.append(("hop", 3.0))
    else:
        items.append(("hop", 12.0))
    items.append(("loss", 4.0))
    if not early:
        outer()
    for part in range(parts):
        items.append(("inner", 6.0))
        add(1, 0, part * width, len(items))
    items.append(("mix", 3.6))
    items.append(("mixed", 2.5))
    first = len(items)
    for turn in range(24):
        items.append(("attend", 5.0 if turn % 8 == 7 else 3.5 if turn in (2, 8, 16) else 2.5))
    add(5, 0, 0, first + 4)
    for turn in range(3):
        item = first + 8 * turn + 10 if turn < 2 else first + 25
        blocks.extend((matrix, 0, turn * UNIT_COLS, item) for matrix in range(2, 5))
    items.append(("flush", 4.0))
    items += [("input", 1.4)] * 4
    units = []
    for i, (matrix, row, col, item) in enumerate(blocks):
        kind = PATTERN[i % len(PATTERN)]
        units.append(Unit(matrix, row, width // 2, col, UNIT_COLS, kind, groups[kind], item))
    return units, items


def backward_kernel(
    sizes, units, order, counts,
    cot, pooled, sums, lengths, doc_groups, positives, act, slope, wo, wi, n2, h1, ho, q, k, v, n1, tokens, lse,
    wq, wk, wv, wm, gain1, gain2, table,
    *refs,
):
    grads, outs = refs[:6], refs[6:12]
    tokens_grad, u_out, small_out, loss_out, dpooled_out = refs[12:17]
    (
        narrow, square, staged, full, bias_s, near_s, sums_s, every_s, every_u, thirds_s, core_land, small_land, kept, land,
        in_sem, chunk_sem, stage_sem, core_send, core_recv, last_sem, hop_send, hop_recv, small_send, small_recv,
        send_sem, recv_sem, load_sem, store_sem, final_send, final_recv,
    ) = refs[17:]
    count, width = narrow.shape[1:]
    rows = lengths.shape[0]
    seq = count // rows
    heads = table.shape[0]
    size = width // heads
    parts = wo.shape[0] // width
    block = 256
    place = Place(sizes)
    names = place.names
    tower, batch = place.at["tower"], place.at["batch"]
    exchange = Exchange(
        units, place, counts, grads, kept, land, outs, (send_sem, recv_sem, load_sem, store_sem, final_send, final_recv)
    )
    cot_s, n2_s, dout_s = narrow.at[8], narrow.at[9], narrow.at[10]
    act_s = [narrow.at[part] for part in range(parts)]
    slope_s = [narrow.at[parts + part] for part in range(parts)]
    h1_s, sum_s = full.at[0], full.at[1]
    loads = {}

    def load(name, source, target):
        copy = pltpu.make_async_copy(source, target, in_sem.at[len(loads)])
        copy.start()
        loads[name] = copy

    def cut(part):
        return pl.ds(part * width, width)

    load("cot", cot, cot_s)
    for part in range(parts):
        load("act%d" % part, act.at[:, cut(part)], act_s[part])
    for part in range(parts):
        load("wo%d" % part, wo.at[cut(part), :], square.at[part])
    load("n2", n2, n2_s)
    for part in range(parts):
        load("slope%d" % part, slope.at[:, cut(part)], slope_s[part])

    def wi_chunk(part):
        return pltpu.make_async_copy(wi.at[:, cut(part)], square.at[parts + part % 2], chunk_sem.at[part])

    for part in range(2):
        wi_chunk(part).start()
    load("h1", h1, h1_s)

    early = is_early(sizes, rows)

    item = 0
    stage_of = {}

    def act_on(actions):
        for action, u, s in actions:
            if action == "go":
                if s == 0:
                    exchange_ready(u)
                exchange.go(u, s)
            else:
                exchange.serve(u, s)

    def exchange_ready(u):
        unit = units[u]
        key = (unit.matrix, unit.row // width if unit.matrix == 0 else unit.col // width)
        if key in stage_of:
            stage_of.pop(key)()

    def between():
        nonlocal item
        act_on(order[item])
        item += 1

    half = width // 2
    own_half = pl.ds(pl.multiple_of(tower * half, 8), half)
    other_half = pl.ds(pl.multiple_of((1 - tower) * half, 8), half)
    core_bit = next(bit for bit, name in enumerate(names) if name[0] == "tower")

    def thirds_of(square_ref):
        return [square_ref.at[:, pl.ds(i * UNIT_COLS, UNIT_COLS)] for i in range(3)]

    def core_copies(turn, pieces):
        return [
            pltpu.make_async_remote_copy(
                src_ref=piece.at[other_half, :],
                dst_ref=core_land.at[turn % 2, i],
                send_sem=core_send.at[turn % 2, i],
                recv_sem=core_recv.at[turn % 2, i],
                device_id=place.partner((core_bit,)),
                device_id_type=MESH,
            )
            for i, piece in enumerate(pieces)
        ]

    def out_copies(turn, pieces, targets):
        return [
            pltpu.make_async_copy(piece.at[own_half, :], target.at[own_half, :], stage_sem.at[turn, i])
            for i, (piece, target) in enumerate(zip(pieces, targets))
        ]

    def core_send_off(turn, pieces):
        for copy in core_copies(turn, pieces):
            copy.start()

    def core_add(turn, pieces, targets):
        for copy in core_copies(turn, pieces):
            copy.wait()
        for i, piece in enumerate(pieces):
            piece[own_half, :] = piece[own_half, :] + core_land[turn % 2, i]
        for copy in out_copies(turn, pieces, targets):
            copy.start()

    def core_done(turn, pieces, targets):
        for copy in out_copies(turn, pieces, targets):
            copy.wait()

    sent = []

    def settle():
        if sent:
            key, turn, pieces, targets = sent.pop()
            core_add(turn, pieces, targets)
            stage_of[key] = functools.partial(core_done, turn, pieces, targets)

    def stage(turn, matrix, part, value, target):
        key = (matrix, part)
        last = [old for old, spot in staged_last.items() if spot == turn % 3]
        for old in last:
            staged_last.pop(old)
            if old in stage_of:
                stage_of.pop(old)()
        staged[turn % 3] = value
        settle()
        pieces = thirds_of(staged.at[turn % 3])
        core_send_off(turn, pieces)
        sent.append((key, turn, pieces, thirds_of(target)))
        staged_last[key] = turn % 3

    staged_last = {}

    hops = gather_groups(sizes)
    every_s[tower, batch] = pooled[...]
    if early:
        every_u[tower, batch] = sums[...]
    deltas = set()
    for group in list(bit_groups(sizes).values()) + [hops]:
        for bits in group:
            deltas.update(flips_of(bits))
    barrier = pltpu.get_barrier_semaphore()
    for flips in sorted(deltas):
        pl.semaphore_signal(barrier, inc=1, device_id=place.partner(flips), device_id_type=MESH)
    pl.semaphore_wait(barrier, len(deltas))

    def hop(h, kind=0):
        group = hops[h]
        masks = [names[bit] for bit in group]
        every = (every_s, every_u)[kind]
        if masks[0][0] == "tower":
            held = every.at[tower]
        else:
            mask = masks[0][1]
            held = every.at[tower, pl.ds(lax.div(batch, jnp.int32(mask)) * mask, mask)]
        return [
            pltpu.make_async_remote_copy(
                src_ref=held,
                dst_ref=held,
                send_sem=hop_send.at[h, 3 * kind + turn],
                recv_sem=hop_recv.at[h, 3 * kind + turn],
                device_id=place.partner(flips),
                device_id_type=MESH,
            )
            for turn, flips in enumerate(flips_of(group))
        ]

    def outer(part, right):
        loads["act%d" % part].wait()
        stage(part, 0, part, dot_tn(act_s[part][...], right[...]), grads[0].at[cut(part), :])

    for copy in hop(0):
        copy.start()
    served = 0
    if early:
        loads["cot"].wait()
        for part in range(parts):
            outer(part, cot_s)
            if part >= 1 and served < len(hops) - 1:
                for copy in hop(served):
                    copy.wait()
                served += 1
                for copy in hop(served):
                    copy.start()
            between()
    while served < len(hops):
        for copy in hop(served):
            copy.wait()
        served += 1
        if served < len(hops):
            for copy in hop(served):
                copy.start()
    settle()
    between()

    total = rows * sizes["batch"]
    for t in range(2):
        for b in range(sizes["batch"]):
            first = t * total + b * rows
            staged[3, first : first + rows, :] = every_s[t, b]
    loss, dpooled = contrast(
        staged[3, 0:total, :], staged[3, total : 2 * total, :], doc_groups[...], positives[...]
    )
    loss_out[...] = loss
    mine = jnp.where(tower == 0, dpooled[0], dpooled[1])
    ids = lax.broadcasted_iota(jnp.int32, (mine.shape[0], 1), 0)
    spread = [
        jnp.sum(jnp.where(ids == batch * rows + row, mine, 0.0), 0, keepdims=True) / lengths[row].astype(FULL)
        for row in range(rows)
    ]
    dpooled_out[0:total, :] = dpooled[0]
    dpooled_out[total : 2 * total, :] = dpooled[1]
    if early:
        for copy in hop(0, 1):
            copy.start()
    else:
        loads["cot"].wait()

    def full_dout(row, i):
        at = pl.ds(row * seq + i * block, block)
        slot = lax.broadcasted_iota(jnp.int32, (block, 1), 0) + i * block
        return at, cot_s[at, :].astype(FULL) + jnp.where(slot < lengths[row], spread[row], 0.0)

    for row in range(rows):

        def round_dout(i, row=row):
            at, dout = full_dout(row, i)
            dout_s[at, :] = dout.astype(LOW)

        for i in range(seq // block):
            round_dout(i)
    between()

    if not early:
        for part in range(parts):
            outer(part, dout_s)
            between()
    for name, source, target in (("q", q, 0), ("k", k, 1), ("v", v, 2), ("n1", n1, 3)):
        load(name, source, narrow.at[target])
    loads["n2"].wait()
    for part in range(parts):
        loads["slope%d" % part].wait()
        loads["wo%d" % part].wait()
        wi_chunk(part).wait()

        def inner_back(i, part=part):
            at = rows_of(i, block)
            dact = dot_nt(dout_s[at, :], square[part])
            dinner = (slope_s[part][at, :].astype(FULL) * dact).astype(LOW)
            slope_s[part][at, :] = dinner
            more = dot_nt(dinner, square[parts + part % 2])
            sum_s[at, :] = more if part == 0 else sum_s[at, :] + more

        for i in range(count // block):
            inner_back(i)
        if part + 2 < parts:
            wi_chunk(part + 2).start()
        stage(parts + part, 1, part, dot_tn(n2_s[...], slope_s[part][...]), grads[1].at[:, cut(part)])
        if early and part < len(hops):
            for copy in hop(part, 1):
                copy.wait()
            if part + 1 < len(hops):
                for copy in hop(part + 1, 1):
                    copy.start()
        between()
    if early:
        u_copy = pltpu.make_async_copy(every_u, u_out, last_sem.at[1])
        u_copy.start()
    load("ho", ho, narrow.at[9])
    for name, source, target in (("wm", wm, 0), ("wq", wq, 1), ("wk", wk, 2), ("wv", wv, 3)):
        load(name, source, square.at[target])
    small_out[...] = jnp.zeros_like(small_out)
    loads["h1"].wait()
    loads["wm"].wait()
    q_s, k_s, v_s, n1_s = (narrow.at[i] for i in range(4))
    dh_s, dq_s, dk_s, dv_s = (narrow.at[i] for i in range(4, 8))

    for row in range(rows):

        def mix_back(i, row=row):
            at, dout = full_dout(row, i)
            dv, dgain = norm_back(h1_s[at, :], gain2[...].reshape(1, width), sum_s[at, :])
            dh1 = dout + dv
            h1_s[at, :] = dh1
            small_out[1:2, :] = small_out[1:2, :] + dgain
            da = dh1.astype(LOW)
            cot_s[at, :] = da
            dh_s[at, :] = dot_nt(da, square[0]).astype(LOW)

        for i in range(seq // block):
            mix_back(i)
    settle()
    between()
    loads["ho"].wait()
    third_refs = [thirds_s.at[i] for i in range(3)]
    third_targets = [thirds_of(grads[5])] + [
        [grads[2 + i].at[:, pl.ds(turn * UNIT_COLS, UNIT_COLS)] for i in range(3)] for turn in range(3)
    ]
    first_turn = 2 * parts
    for i in range(3):
        thirds_s[i] = dot_tn(narrow[9], cot_s[:, pl.ds(i * UNIT_COLS, UNIT_COLS)])
    core_send_off(first_turn, third_refs)
    between()
    for done in list(stage_of.values()):
        done()
    stage_of.clear()
    load("x", tokens, narrow.at[9])
    for name in ("q", "k", "v", "n1"):
        loads[name].wait()

    blocks = seq // 128
    lanes = lax.broadcasted_iota(jnp.int32, (seq, 2 * size), 1)
    keys = lax.broadcasted_iota(jnp.int32, (128, seq), 0)
    first_item = item
    steps = rows * (heads // 2)

    def between_at(step, side):
        for index in range(steps):
            actions = order[first_item + 2 * index + side] if 2 * index + side < 24 else []
            if actions:
                pl.when(step == index)(functools.partial(act_on, actions))

    per_turn = 2 * rows

    def third(turn):
        for i, d_s in enumerate((dq_s, dk_s, dv_s)):
            thirds_s[i] = dot_tn(n1_s[...], d_s[:, pl.ds(turn * UNIT_COLS, UNIT_COLS)])
        core_send_off(first_turn + 1 + turn, third_refs)

    def third_add(turn):
        core_add(first_turn + 1 + turn, third_refs, third_targets[1 + turn])

    def third_done(turn):
        core_done(first_turn + 1 + turn, third_refs, third_targets[1 + turn])

    def attend_back(step):
        pair = lax.div(step, jnp.int32(rows))
        row = lax.rem(step, jnp.int32(rows))
        at = rows_of(row, seq)
        here = rows_of(pair, 2 * size)
        limit = lengths[row]
        for turn in range(-1, steps // per_turn - 1):
            ready = per_turn * (turn + 1) if turn >= 0 else 1
            pl.when(step == ready)(functools.partial(third_add, turn))
            pl.when(step == ready + 1)(functools.partial(third_done, turn))

        @pl.when(row == 0)
        def _():
            near_s[...] = jnp.zeros_like(near_s)
            fill_bias(bias_s, table, pair * 2, 2)

        qp, kp, vp, dp = q_s[at, here], k_s[at, here], v_s[at, here], dh_s[at, here]
        nothing = jnp.zeros_like(qp)
        kt = kp.T
        dq, dk, dv = [], [], []
        score_s = [staged.at[side, 0:seq, 0:seq] for side in range(2)]
        dprob_s = [staged.at[2 + side, 0:seq, 0:seq] for side in range(2)]
        prob_s = [narrow.at[8, side * seq : (side + 1) * seq, 0:seq] for side in range(2)]
        dscore_s = [narrow.at[10, side * seq : (side + 1) * seq, 0:seq] for side in range(2)]
        for side in range(2):
            chosen = (lanes >= size) == (side == 1)
            score_s[side][...] = dot_nt(kp, jnp.where(chosen, qp, nothing))
            dprob_s[side][...] = dot_nt(vp, jnp.where(chosen, dp, nothing))
        for side in range(2):
            head = pair * 2 + side
            level = lse[row * heads + head]
            delta = jnp.zeros((1, seq), FULL)
            for jb in range(blocks):
                some = slice(jb * 128, (jb + 1) * 128)
                strip = score_s[side][some, :] + bias_strip(bias_s, side, table, head, jb, blocks)
                strip = jnp.where(keys + jb * 128 < limit, strip, NEGATIVE)
                prob = jnp.exp(strip - level)
                prob_s[side][some, :] = prob.astype(LOW)
                score_s[side][some, :] = prob
                delta = delta + jnp.sum(prob * dprob_s[side][some, :], 0, keepdims=True)
            for jb in range(blocks):
                some = slice(jb * 128, (jb + 1) * 128)
                dscore = score_s[side][some, :] * (dprob_s[side][some, :] - delta)
                dscore_s[side][some, :] = dscore.astype(LOW)
                for ib in range(blocks):
                    spot = min(max(jb - ib, -2), 2) + 2
                    near_s[side, spot] = near_s[side, spot] + dscore[:, ib * 128 : (ib + 1) * 128]
            dk.append(dot_nn(dscore_s[side][...], qp))
            dv.append(dot_nn(prob_s[side][...], dp))
            dq.append(dot_nn(kt[side * size : (side + 1) * size, :], dscore_s[side][...]))
            if side == 0:
                between_at(step, 0)
        first = lanes < size
        dk_s[at, here] = jnp.where(first, dk[0], dk[1]).astype(LOW)
        dv_s[at, here] = jnp.where(first, dv[0], dv[1]).astype(LOW)
        dq_s[at, here] = jnp.concatenate(dq, 0).T.astype(LOW)

        @pl.when(row == rows - 1)
        def _():
            ids = [offset_buckets(shift) for shift, _ in NEAR]
            for side in range(2):
                bucket = lax.broadcasted_iota(jnp.int32, (1, 128), 1)
                found = jnp.zeros((1, 128), FULL)
                for spot, (shift, members) in enumerate(NEAR):
                    total = near_s[side, spot + 1]
                    for b in members:
                        share = jnp.sum(jnp.where(ids[spot] == b, total, 0.0), 0, keepdims=True)
                        found = found + jnp.where(bucket == b, jnp.sum(share, 1, keepdims=True), 0.0)
                for spot, b in ((0, 15), (4, 31)):
                    share = jnp.sum(near_s[side, spot], 0, keepdims=True)
                    found = found + jnp.where(bucket == b, jnp.sum(share, 1, keepdims=True), 0.0)
                sums_s[pair * 2 + side] = found

        for turn in range(steps // per_turn):
            pl.when(step == per_turn * (turn + 1) - 1)(functools.partial(third, turn))
        between_at(step, 1)

    loop(steps, attend_back)
    item = first_item + 24
    for head in range(heads):
        small_out[8 + head : 9 + head, 0:128] = sums_s[head]

    third_add(steps // per_turn - 1)
    for i in range(3):
        stage_of[(2 + i, steps // per_turn - 1)] = lambda: None
    between()
    for name in ("wq", "wk", "wv", "x"):
        loads[name].wait()

    def input_back(i):
        at = rows_of(i, block)
        dn1 = dot_nt(dq_s[at, :], square[1]) + dot_nt(dk_s[at, :], square[2]) + dot_nt(dv_s[at, :], square[3])
        dv, dgain = norm_back(narrow[9, at, :].astype(FULL), gain1[...].reshape(1, width), dn1)
        small_out[0:1, :] = small_out[0:1, :] + dgain
        cot_s[at, :] = (h1_s[at, :] + dv).astype(LOW)

    for i in range(count // block):
        input_back(i)
        if i == 0:
            third_done(steps // per_turn - 1)
        if i < 3:
            between()
    last = pltpu.make_async_copy(cot_s, tokens_grad, last_sem.at[0])
    last.start()

    def small_copy(bit):
        return pltpu.make_async_remote_copy(
            src_ref=small_out,
            dst_ref=small_land.at[bit],
            send_sem=small_send.at[bit],
            recv_sem=small_recv.at[bit],
            device_id=place.partner((bit,)),
            device_id_type=MESH,
        )

    small_copy(0).start()
    actions = order[item]
    for bit in range(len(names)):
        act_on(actions[len(actions) * bit // (len(names) + 1) : len(actions) * (bit + 1) // (len(names) + 1)])
        small_copy(bit).wait()
        small_out[...] = small_out[...] + small_land[bit]
        if bit + 1 < len(names):
            small_copy(bit + 1).start()
    act_on(actions[len(actions) * len(names) // (len(names) + 1) :])
    last.wait()
    if early:
        u_copy.wait()
    for done in stage_of.values():
        done()


def backward(
    sizes, cot, pooled, sums, lengths, doc_groups, positives, act, slope, wo, wi, n2, h1, ho, q, k, v, n1, tokens, lse,
    wq, wk, wv, wm, gain1, gain2, table,
):
    count, width = cot.shape
    hidden = wo.shape[0]
    rows = lengths.shape[0]
    heads = table.shape[0]
    total = doc_groups.shape[0]
    names = bit_names(sizes)
    shape = jax.ShapeDtypeStruct
    early = is_early(sizes, rows)
    gathered = shape((2, sizes["batch"]) + sums.shape if early else (8, 128), FULL)
    units, items = make_units(sizes, rows, hidden, width)
    counts = set_counts(sizes)
    order, _ = plan(units, names, counts, [PACE * time for _, time in items])
    steps = max(len(unit.steps) for unit in units)
    sets = sum(counts.values())
    any_spec = pl.BlockSpec(memory_space=pl.ANY)
    vmem_spec = pl.BlockSpec(memory_space=pltpu.VMEM)
    smem_spec = pl.BlockSpec(memory_space=pltpu.SMEM)
    squares = [shape((hidden, width), FULL), shape((width, hidden), FULL)] + [shape((width, width), FULL)] * 4
    hops = len(gather_groups(sizes))
    dma = pltpu.SemaphoreType.DMA
    return pl.pallas_call(
        functools.partial(backward_kernel, sizes, units, order, counts),
        out_shape=squares + squares
        + [shape((count, width), LOW), gathered, shape((24, width), FULL), shape((1, 1), FULL)]
        + [shape((2 * total, width), FULL)],
        in_specs=[any_spec, vmem_spec, vmem_spec, smem_spec, vmem_spec, vmem_spec]
        + [any_spec] * 12
        + [vmem_spec]
        + [any_spec] * 4
        + [vmem_spec] * 2
        + [smem_spec],
        out_specs=[any_spec] * 14 + [vmem_spec] * 3,
        scratch_shapes=[
            pltpu.VMEM((11, count, width), LOW),
            pltpu.VMEM((6, width, width), LOW),
            pltpu.VMEM((4, width, width), FULL),
            pltpu.VMEM((2, count, width), FULL),
            pltpu.VMEM((2, 3, 128, 128), FULL),
            pltpu.VMEM((2, 5, 128, 128), FULL),
            pltpu.VMEM((heads, 1, 128), FULL),
            pltpu.VMEM((2, sizes["batch"], rows, width), FULL),
            pltpu.VMEM(gathered.shape, FULL),
            pltpu.VMEM((3, width, UNIT_COLS), FULL),
            pltpu.VMEM((2, 3, width // 2, UNIT_COLS), FULL),
            pltpu.VMEM((len(names), 24, width), FULL),
            pltpu.VMEM((sets, max(unit.steps[0][2] for unit in units), UNIT_COLS), FULL),
            pltpu.VMEM((sets, max(unit.land for unit in units), UNIT_COLS), FULL),
            dma((32,)),
            dma((8,)),
            dma((16, 3)),
            dma((2, 3)),
            dma((2, 3)),
            dma((2,)),
            dma((hops, 6)),
            dma((hops, 6)),
            dma((len(names),)),
            dma((len(names),)),
            dma((sets, steps, 3)),
            dma((sets, steps, 3)),
            dma((sets,)),
            dma((sets,)),
            dma((len(units),)),
            dma((len(units),)),
        ],
        compiler_params=pltpu.CompilerParams(
            collective_id=0, has_side_effects=True, vmem_limit_bytes=int(63.5 * 2**20)
        ),
    )(
        cot, pooled, sums, lengths, doc_groups.reshape(1, total), positives.reshape(1, total), act, slope, wo, wi, n2, h1,
        ho, q, k, v, n1, tokens, lse, wq, wk, wv, wm, gain1, gain2, table,
    )


OUT_ROWS = 256


def hand_out_kernel(blocks, count, heads, early, *refs):
    sources, (u_in, small, loss_in, dpooled) = refs[:count], refs[count : count + 4]
    targets = refs[count + 4 : 2 * count + 4]
    gain1, gain2, table, loss = refs[2 * count + 4 : 2 * count + 8]
    full, low, u_s, sums_s, in_sem, out_sem = refs[2 * count + 8 :]
    width = full.shape[2]
    loads, stores = [], []
    if early:
        u_load = pltpu.make_async_copy(u_in, u_s, in_sem.at[len(blocks)])
        u_load.start()
    for i, (array, spot, row, col) in enumerate(blocks):
        at = (pl.ds(row, OUT_ROWS), pl.ds(col, width))
        held = (low if sources[array].dtype == LOW else full).at[spot]
        loads.append(pltpu.make_async_copy(sources[array].at[at], held, in_sem.at[i]))
        stores.append(pltpu.make_async_copy(held, targets[array].at[at], out_sem.at[i]))
    for load in loads:
        load.start()
    gain1[...] = small[0]
    gain2[...] = small[1]
    table[...] = small[8 : 8 + heads, 0 : table.shape[1]]
    loss[...] = loss_in[...]
    if early:
        u_load.wait()
        towers, places, most, _ = u_s.shape
        parts = targets[0].shape[0] // width
        rows = most // parts
        for part in range(parts):
            for t in range(towers):
                for b in range(places):
                    first = (t * places + b) * rows
                    sums_s[part, first : first + rows, :] = u_s[t, b, part * rows : (part + 1) * rows, :]
    for i, (load, store) in enumerate(zip(loads, stores)):
        load.wait()
        array, spot, row, _ = blocks[i]
        if early and array == 0:
            some = sums_s[row // width, :, row % width : row % width + OUT_ROWS]
            full[spot] = full[spot] + lax.dot_general(
                some, dpooled[...], (((0,), (0,)), ((), ())), precision=HIGHEST, preferred_element_type=FULL
            )
        store.start()
    for store in stores:
        store.wait()


def hand_out(arrays, sums, small, loss, dpooled, heads, buckets):
    width = small.shape[1]
    early = len(sums.shape) == 4
    blocks, held = [], {FULL: 0, LOW: 0}
    for i, array in enumerate(arrays):
        for col in range(0, array.shape[1], width):
            for row in range(0, array.shape[0], OUT_ROWS):
                kind = LOW if array.dtype == LOW else FULL
                blocks.append((i, held[kind], row, col))
                held[kind] += 1
    any_spec = pl.BlockSpec(memory_space=pl.ANY)
    vmem_spec = pl.BlockSpec(memory_space=pltpu.VMEM)
    shape = jax.ShapeDtypeStruct
    return pl.pallas_call(
        functools.partial(hand_out_kernel, blocks, len(arrays), heads, early),
        out_shape=[shape(a.shape, a.dtype) for a in arrays]
        + [shape((width,), FULL), shape((width,), FULL), shape((heads, buckets), FULL), shape((1, 1), FULL)],
        in_specs=[any_spec] * (len(arrays) + 1) + [vmem_spec] * 3,
        out_specs=[any_spec] * len(arrays) + [vmem_spec] * 4,
        scratch_shapes=[
            pltpu.VMEM((held[FULL], OUT_ROWS, width), FULL),
            pltpu.VMEM((held[LOW], OUT_ROWS, width), LOW),
            pltpu.VMEM(sums.shape, FULL),
            pltpu.VMEM((arrays[0].shape[0] // width, dpooled.shape[0], width) if early else (8, 128), FULL),
            pltpu.SemaphoreType.DMA((len(blocks) + 1,)),
            pltpu.SemaphoreType.DMA((len(blocks),)),
        ],
        compiler_params=pltpu.CompilerParams(vmem_limit_bytes=63 * 2**20),
    )(*arrays, sums, small, loss, dpooled)


def shards(
    tokens,
    lengths,
    doc_groups,
    positives,
    cotangent,
    w_query,
    w_key,
    w_value,
    w_mixed,
    w_inner,
    w_outer,
    gain_attn,
    gain_ffn,
    rel_table,
):
    rows = tokens.shape[1]
    count, width = rows * tokens.shape[2], tokens.shape[3]
    buckets, heads = rel_table.shape
    sizes = {axis: lax.axis_size(axis) for axis in ("tower", "batch")}
    flat = tokens.reshape(count, width)
    cot = cotangent.reshape(count, width)
    own_lengths = lengths.reshape(rows)
    table = rel_table.T
    q, k, v, ho, n1, n2, h1, act, slope, result, lse, pooled, sums = forward(
        flat, own_lengths, w_query, w_key, w_value, w_mixed, w_inner, w_outer, gain_attn, gain_ffn, table
    )
    found = backward(
        sizes, cot, pooled, sums, own_lengths, doc_groups, positives, act, slope, w_outer, w_inner, n2, h1, ho, q, k, v, n1,
        flat, lse, w_query, w_key, w_value, w_mixed, gain_attn, gain_ffn, table,
    )
    given = hand_out(found[6:13], *found[13:], heads, buckets)
    wo_grad, wi_grad, wq_grad, wk_grad, wv_grad, wm_grad, tokens_grad, gain1_grad, gain2_grad, table_grad, loss = given
    return (
        result.reshape(tokens.shape),
        pooled[None],
        loss[0, 0],
        tokens_grad.reshape(tokens.shape),
        wq_grad,
        wk_grad,
        wv_grad,
        wm_grad,
        wi_grad,
        wo_grad,
        gain1_grad,
        gain2_grad,
        table_grad.T,
    )


def solution(mesh):
    return jax.shard_map(
        shards,
        mesh=mesh,
        in_specs=(
            P("tower", "batch", None, None),
            P("tower", "batch"),
            P(),
            P(),
            P("tower", "batch", None, None),
            P(),
            P(),
            P(),
            P(),
            P(),
            P(),
            P(),
            P(),
            P(),
        ),
        out_specs=(
            P("tower", "batch", None, None),
            P("tower", "batch", None),
            P(),
            P("tower", "batch", None, None),
            P(),
            P(),
            P(),
            P(),
            P(),
            P(),
            P(),
            P(),
            P(),
        ),
        check_vma=False,
    )
```
